32 devices in a mesh: prompts: 2 (over x), beam: 16 (over z, y, core).
Axes of the slice: x: 2, y: 2, z: 4, core: 2. Of those that a mesh axis runs over, the one named last changes fastest.
Arguments:
- queries: bfloat16 [128, 256, 4096], P(('prompts', 'beam')), parts along dimension 0, may hold values from -4.375 to 4.375
- new_keys: bfloat16 [128, 256, 1024], P(('prompts', 'beam')), parts along dimension 0, may hold values from -4.375 to 4.375
- new_values: bfloat16 [128, 256, 1024], P(('prompts', 'beam')), parts along dimension 0, may hold values from -6 to 6
- step_kv: bfloat16 [128, 2, 64, 1024], P(('prompts', 'beam')), parts along dimension 0, may hold values from -6 to 6
- prm_last: bfloat16 [128, 4096], P(('prompts', 'beam')), parts along dimension 0, may hold values from -6 to 6
- value_head: float32 [4096], replicated, may hold values from -0.09375 to 0.09375
- parents: int32 [128], P('prompts'), parts along dimension 0, may hold values from 0 to 63, as said below
Outputs:
- attended: bfloat16 [128, 256, 4096], P(('prompts', 'beam')), parts along dimension 0
- child_share: float32 [128], P(('prompts', 'beam')), parts along dimension 0
The draws below stay inside these ranges and needn't reach their ends.
There are 2 independent parts, one for each index of `prompts`. The reference program is written for one: setup_inputs(seed, part) draws one part's arguments, and reference() takes and returns one part's arrays. A program takes and returns all parts, laid end to end along the dimension named above; an argument that names none is the same for every part. Nothing has to cross between parts.
Inputs may be any that keep to these rules, and one draw needn't show every extreme that they name: `parents`: on every device exactly 2 of its 4 beams are the parent of one or more children and the other beams of none.
All inputs are finite; a program needn't handle non-finite values.
Results may differ from the reference program's by a relative error of at most 0.008.
Values may be sent and summed in bfloat16 or wider, within the bound.
No kernel may reach another device: no remote copies, remote signals or barrier semaphores. Data moves between devices by JAX's collectives and lax.ppermute only.
A program may use at most 192 MiB of HBM per device.

```python
import jax
import jax.numpy as jnp
from jax import lax

D = 4096
HEADS = 32
KV_HEADS = 8
HEAD_SIZE = 128
NEW = 256
STEP = 64
BEAM_DEV = 4
KEEP = 2
BEAMS = 64
CHILDREN = 64


def drawn_pair(key):
    base = jax.random.fold_in(key, 7919)
    key_q, key_k = jax.random.split(base, 2)
    q_shape = (CHILDREN, NEW, HEADS * HEAD_SIZE)
    k_shape = (CHILDREN, NEW, KV_HEADS * HEAD_SIZE)
    queries = jnp.clip(jax.random.normal(key_q, q_shape, jnp.float32), -4.375, 4.375)
    keys = jnp.clip(jax.random.normal(key_k, k_shape, jnp.float32), -4.375, 4.375)
    return (queries, keys)


def draw_queries(key, part):
    return drawn_pair(key)[0].astype(jnp.bfloat16)


def draw_new_keys(key, part):
    return drawn_pair(key)[1].astype(jnp.bfloat16)


def draw_parents(key, part):
    base = jax.random.fold_in(key, 5303)
    key_a, key_b, key_c, key_d, key_e = jax.random.split(base, 5)
    groups = BEAMS // BEAM_DEV
    ranks = jax.random.randint(key_a, (groups, BEAM_DEV), 0, 1048576) * BEAM_DEV + jnp.arange(BEAM_DEV)[None, :]
    order = jnp.argsort(ranks, axis=1, stable=True)
    kept_beams = (jnp.arange(groups)[:, None] * BEAM_DEV + order[:, :KEEP]).reshape(-1)
    kept_count = groups * KEEP
    shuffled = jax.random.permutation(key_b, kept_beams)
    extra = CHILDREN - kept_count
    upper = jax.random.randint(key_c, (extra,), 1, kept_count + 1)
    picks = jax.random.randint(key_d, (extra,), 0, upper)
    assign = jnp.concatenate([shuffled, shuffled[picks]])
    return jax.random.permutation(key_e, assign).astype(jnp.int32)


def shard_levels(rng, dims, cuts, smallest, high):
    level, own = 1.0, jax.random.fold_in(rng, 6)
    for position, parts in cuts:
        draws = jnp.exp(jax.random.uniform(jax.random.fold_in(own, position), (parts,), jnp.float32, smallest / len(cuts), high / len(cuts)))
        level = level * jnp.repeat(draws, dims[position] // parts).reshape([-1 if axis == position else 1 for axis in range(len(dims))])
    return level


def centred(key, dims, deviation, most, cuts=(), held_as=jnp.bfloat16):
    level = shard_levels(key, dims, cuts, -0.22, 0.18) if cuts else 1.0
    entries = jax.random.normal(key, dims, jnp.float32) * deviation * level
    return jnp.minimum(jnp.maximum(entries, -most), most).astype(held_as)


def setup_inputs(seed: int = 0, part: int = 0) -> dict:
    key_list = jax.random.split(jax.random.key(seed), 8)
    part_keys = jax.random.split(jax.random.fold_in(key_list[7], part), 8)
    queries = draw_queries(jax.random.fold_in(jax.random.fold_in(key_list[7], part), 71), part)
    new_keys = draw_new_keys(jax.random.fold_in(jax.random.fold_in(key_list[7], part), 71), part)
    new_values = centred(part_keys[2], (CHILDREN, NEW, KV_HEADS * HEAD_SIZE), 1.0, 6.0, ((0, 16),))
    step_kv = centred(part_keys[3], (BEAMS, 2, STEP, KV_HEADS * HEAD_SIZE), 1.0, 6.0, ((0, 16),))
    prm_last = centred(part_keys[4], (BEAMS, D), 1.0, 6.0, ((0, 16),))
    value_head = centred(key_list[5], (D,), D ** -0.5, 0.09375, (), jnp.float32)
    parents = draw_parents(jax.random.fold_in(jax.random.fold_in(key_list[7], part), 71), part)
    return dict(queries=queries, new_keys=new_keys, new_values=new_values, step_kv=step_kv, prm_last=prm_last, value_head=value_head, parents=parents)


def attend_child(operands):
    query, keys, values = operands
    total_len = keys.shape[0]
    new_len = query.shape[0]
    step_len = total_len - new_len
    kv_width = keys.shape[1]
    kv_heads = kv_width // HEAD_SIZE
    group = query.shape[1] // kv_width
    query_head_rows = query.astype(jnp.float32).reshape(new_len, kv_heads, group, HEAD_SIZE)
    key_head_rows = keys.astype(jnp.float32).reshape(total_len, kv_heads, HEAD_SIZE)
    value_head_rows = values.astype(jnp.float32).reshape(total_len, kv_heads, HEAD_SIZE)
    attention_scores = jnp.einsum('yfli,xfi->flyx', query_head_rows, key_head_rows) * HEAD_SIZE ** (-0.5)
    column = jnp.arange(total_len)[None, :]
    row_pos = jnp.arange(new_len)[:, None]
    visible = (column < step_len) | (column - step_len <= row_pos)
    attention_scores = jnp.where(visible, attention_scores, -jnp.inf)
    attention_weights = jax.nn.softmax(attention_scores, axis=-1).astype(jnp.bfloat16).astype(jnp.float32)
    attended_values = jnp.einsum('fjip,pfa->ifja', attention_weights, value_head_rows)
    return attended_values.reshape(new_len, -1).astype(jnp.bfloat16)

def reference(queries, new_keys, new_values, step_kv, prm_last, value_head, parents):
    hidden = prm_last.astype(jnp.float32)
    square = lax.optimization_barrier(jnp.mean(hidden * hidden, axis=-1, keepdims=True))
    normed = hidden * lax.rsqrt(square + 1e-05)
    score = jnp.dot(normed, value_head, precision=lax.Precision.HIGHEST)
    reward = jax.nn.sigmoid(score).astype(jnp.bfloat16)
    child_reward = jnp.take(reward, parents, axis=0).astype(jnp.float32)
    total = jnp.sum(child_reward)
    child_share = CHILDREN * child_reward / total
    copied = jnp.take(step_kv, parents, axis=0)
    keys_all = jnp.concatenate([copied[:, 0], new_keys], axis=1)
    values_all = jnp.concatenate([copied[:, 1], new_values], axis=1)
    attended = lax.map(attend_child, (queries, keys_all, values_all))
    return (attended, child_share)
```

```python
import functools
import math

import jax
import jax.numpy as jnp
from jax import lax
from jax.experimental import pallas as pl
from jax.experimental.pallas import tpu as pltpu
from jax.sharding import PartitionSpec as P

HEAD = 128
KEEP = 2
MARK = 16
LOG2E = math.log2(math.e)
MIB = 1 << 20
NT = (((1,), (1,)), ((), ()))
NN = (((1,), (0,)), ((), ()))


def mm(a, b, dims=NN):
    return lax.dot_general(a, b, dims, preferred_element_type=jnp.float32)


def kept_pair(parents, base, local):
    own = (parents >= base) & (parents < base + local)
    first = jnp.min(jnp.where(own, parents - base, local))
    last = jnp.max(jnp.where(own, parents - base, -1))
    return first, last


def pack_keys(parents_ref, kv_ref, last_ref, value_ref, out_ref):
    local, _, step, width = kv_ref.shape
    heads = width // HEAD
    base = lax.axis_index("beam") * local
    kept = kept_pair(parents_ref[...], base, local)
    hidden = last_ref[...].astype(jnp.float32)
    square = jnp.mean(hidden * hidden, axis=-1, keepdims=True)
    normed = hidden * lax.rsqrt(square + 1e-05)
    score = jnp.sum(normed * value_ref[...], axis=-1, keepdims=True)
    reward = jax.nn.sigmoid(score)
    row = lax.broadcasted_iota(jnp.int32, reward.shape, 0)
    marks = [jnp.sum(jnp.where(row == k, reward, 0.0)) for k in kept]
    tile = lax.broadcasted_iota(jnp.int32, (MARK, HEAD), 0)
    tile = jnp.where(tile < MARK // 2, marks[0], marks[1]).astype(jnp.bfloat16)
    for d in range(out_ref.shape[0]):
        out_ref[d, KEEP * step :, :] = tile
    for r, k in enumerate(kept):
        for f in range(heads):
            piece = kv_ref[k, 0, :, f * HEAD : (f + 1) * HEAD]
            for d in range(f, out_ref.shape[0], heads):
                out_ref[d, r * step : (r + 1) * step, :] = piece


def pack_values(parents_ref, kv_ref, out_ref):
    local, _, step, width = kv_ref.shape
    heads = width // HEAD
    base = lax.axis_index("beam") * local
    kept = kept_pair(parents_ref[...], base, local)
    for r, k in enumerate(kept):
        for f in range(heads):
            piece = kv_ref[k, 0, :, f * HEAD : (f + 1) * HEAD]
            for d in range(f, out_ref.shape[0], heads):
                out_ref[d, r * step : (r + 1) * step, :] = piece


def pick_pieces(step, item_ref, table_ref, out_ref):
    heads = out_ref.shape[0]
    local = out_ref.shape[1] // step
    for d in range(heads):
        for i in range(local):
            item = item_ref[d * local + i]
            start = pl.multiple_of((item % KEEP) * step, step)
            piece = table_ref[item // KEEP, pl.ds(start, step), :]
            out_ref[d, i * step : (i + 1) * step, :] = piece


def attend_new(q_ref, k_ref, v_ref, out_ref, lse_ref):
    new = q_ref.shape[1]
    half = new // 2
    heads = k_ref.shape[2] // HEAD
    group = q_ref.shape[2] // k_ref.shape[2]
    scale = HEAD**-0.5 * LOG2E
    ones = jnp.ones((new, HEAD), jnp.bfloat16)
    low = lax.broadcasted_iota(jnp.int32, (half, HEAD), 1) < HEAD // 2
    row = lax.broadcasted_iota(jnp.int32, (half, half), 0)
    column = lax.broadcasted_iota(jnp.int32, (half, half), 1)
    bias = jnp.where(column <= row, 0.0, -jnp.inf)
    bias = jnp.concatenate([bias] * group, axis=0)
    for f in range(heads):
        keys = k_ref[0, :, f * HEAD : (f + 1) * HEAD]
        values = jnp.concatenate([v_ref[0, :, f * HEAD : (f + 1) * HEAD], ones], axis=1)
        for r in range(2):
            seen = (r + 1) * half
            rows = slice(r * half, (r + 1) * half)
            columns = [slice((f * group + h) * HEAD, (f * group + h + 1) * HEAD) for h in range(group)]
            query = jnp.concatenate([q_ref[0, rows, c] for c in columns], axis=0)
            logits = mm(query, keys[:seen], NT) * scale
            masked = logits[:, seen - half :] + bias
            if r == 0:
                logits = masked
                top = jnp.max(logits, axis=1, keepdims=True)
            else:
                free = logits[:, :half]
                top = jnp.max(jnp.maximum(free, masked), axis=1, keepdims=True)
                logits = jnp.concatenate([free, masked], axis=1)
            weights = jnp.exp2(logits - top).astype(jnp.bfloat16)
            both = mm(weights, values[:seen])
            total = both[:, HEAD:]
            part = both[:, :HEAD] / total
            lse = top + jnp.log2(total)
            for h in range(group):
                out_ref[0, rows, columns[h]] = part[h * half : (h + 1) * half].astype(jnp.bfloat16)
            for h in range(0, group, 2):
                pair = jnp.where(low, lse[h * half : (h + 1) * half], lse[(h + 1) * half : (h + 2) * half])
                start = (f * group + h) // 2 * HEAD
                lse_ref[0, rows, start : start + HEAD] = pair


def block_pair(a):
    zero = jnp.zeros_like(a)
    return jnp.concatenate([jnp.concatenate([a, zero], axis=1), jnp.concatenate([zero, a], axis=1)], axis=0)


def weigh_step(q_ref, k_ref, lse_ref, new_ref, weights_ref, out_ref):
    heads = k_ref.shape[0]
    step = k_ref.shape[1]
    pairs = lse_ref.shape[2] // HEAD
    new = q_ref.shape[1]
    scale = HEAD**-0.5 * LOG2E
    low = lax.broadcasted_iota(jnp.int32, (new, HEAD), 1) < step
    ones = block_pair(jnp.ones((step, HEAD), jnp.bfloat16))
    for f in range(heads):
        keys = block_pair(k_ref[f])
        for p in range(f * pairs // heads, (f + 1) * pairs // heads):
            wide = slice(p * 2 * HEAD, (p + 1) * 2 * HEAD)
            narrow = slice(p * HEAD, (p + 1) * HEAD)
            logits = mm(q_ref[0, :, wide], keys, NT) * scale - lse_ref[0, :, narrow]
            tops = [
                jnp.maximum(jnp.max(jnp.where(m, logits, 0.0), axis=1, keepdims=True), 0.0) for m in (low, ~low)
            ]
            weights = jnp.exp2(logits - jnp.where(low, tops[0], tops[1]))
            rest = [jnp.broadcast_to(jnp.exp2(-t), (new, HEAD)) for t in tops]
            total = mm(weights.astype(jnp.bfloat16), ones)
            shares = [1.0 / (rest[h] + total[:, h * HEAD : (h + 1) * HEAD]) for h in range(2)]
            weights_ref[0, :, narrow] = (weights * jnp.where(low, shares[0], shares[1])).astype(jnp.bfloat16)
            for h in range(2):
                c = slice((2 * p + h) * HEAD, (2 * p + h + 1) * HEAD)
                part = new_ref[0, :, c].astype(jnp.float32) * (shares[h] * rest[h])
                out_ref[0, :, c] = part.astype(jnp.bfloat16)


def add_step(v_ref, weights_ref, part_ref, out_ref):
    heads = v_ref.shape[0]
    pairs = weights_ref.shape[2] // HEAD
    for f in range(heads):
        values = block_pair(v_ref[f])
        for p in range(f * pairs // heads, (f + 1) * pairs // heads):
            wide = slice(p * 2 * HEAD, (p + 1) * 2 * HEAD)
            narrow = slice(p * HEAD, (p + 1) * HEAD)
            added = mm(weights_ref[0, :, narrow], values)
            out_ref[0, :, wide] = (part_ref[0, :, wide].astype(jnp.float32) + added).astype(jnp.bfloat16)


def params(mib):
    return pltpu.CompilerParams(vmem_limit_bytes=mib * MIB)


def body(queries, new_keys, new_values, step_kv, prm_last, value_head, parents):
    beam_count = lax.axis_size("beam")
    group_index = lax.axis_index("beam")
    local, new, width = queries.shape
    children = parents.shape[0]
    step = step_kv.shape[2]
    kv_width = step_kv.shape[3]
    heads = kv_width // HEAD
    groups = [list(range(g, g + heads)) for g in range(0, beam_count, heads)]
    vmem = pl.BlockSpec(memory_space=pltpu.VMEM)
    smem = pl.BlockSpec(memory_space=pltpu.SMEM)
    bf16 = jnp.bfloat16

    parent_row = parents.reshape(1, children)
    packed_keys = pl.pallas_call(
        pack_keys,
        grid=(1,),
        out_shape=jax.ShapeDtypeStruct((beam_count, KEEP * step + MARK, HEAD), bf16),
        in_specs=[
            pl.BlockSpec((1, children), lambda i: (0, 0)),
            pl.BlockSpec((local, 1, step, kv_width), lambda i: (0, 0, 0, 0)),
            pl.BlockSpec(prm_last.shape, lambda i: (0, 0)),
            pl.BlockSpec((1, value_head.shape[0]), lambda i: (0, 0)),
        ],
        out_specs=pl.BlockSpec((beam_count, KEEP * step + MARK, HEAD), lambda i: (0, 0, 0)),
        name="pack_keys",
    )(parent_row, step_kv, prm_last, value_head.reshape(1, -1))
    packed_values = pl.pallas_call(
        pack_values,
        grid=(1,),
        out_shape=jax.ShapeDtypeStruct((beam_count, KEEP * step, HEAD), bf16),
        in_specs=[
            pl.BlockSpec((1, children), lambda i: (0, 0)),
            pl.BlockSpec((local, 1, step, kv_width), lambda i: (0, 1, 0, 0)),
        ],
        out_specs=pl.BlockSpec((beam_count, KEEP * step, HEAD), lambda i: (0, 0, 0)),
        name="pack_values",
    )(parent_row, step_kv)

    owner = parents // local
    earlier = (owner[:, None] == owner[None, :]) & (parents[None, :] < parents[:, None])
    item = owner * KEEP + jnp.any(earlier, axis=1).astype(jnp.int32)
    near = lax.dynamic_slice_in_dim(item, group_index // heads * (heads * local), heads * local)

    def deliver(packed, name):
        table = lax.all_to_all(packed, "beam", 0, 0)
        picked = pl.pallas_call(
            functools.partial(pick_pieces, step),
            out_shape=jax.ShapeDtypeStruct((heads, local * step, HEAD), bf16),
            in_specs=[smem, vmem],
            out_specs=vmem,
            name=name,
        )(near, table)
        return table, lax.all_to_all(picked, "beam", 0, 0, axis_index_groups=groups)

    table, step_keys = deliver(packed_keys, "pick_keys")
    _, step_values = deliver(packed_values, "pick_values")

    marks = jnp.stack([table[:, KEEP * step, 0], table[:, KEEP * step + MARK // 2, 0]], axis=1).reshape(-1)
    match = item[:, None] == jnp.arange(beam_count * KEEP, dtype=jnp.int32)[None, :]
    picked = jnp.sum(jnp.where(match, marks.astype(jnp.float32)[None, :], 0.0), axis=1)
    mine = lax.dynamic_slice_in_dim(picked, group_index * local, local)
    child_share = children * mine / jnp.sum(picked)

    parts = 2
    cost = lambda f, t, b: pl.CostEstimate(flops=f, transcendentals=t, bytes_accessed=b)
    pair_width = width // 2
    part, lse = pl.pallas_call(
        attend_new,
        grid=(local, parts),
        out_shape=[
            jax.ShapeDtypeStruct((local, new, width), bf16),
            jax.ShapeDtypeStruct((local, new, pair_width), jnp.float32),
        ],
        in_specs=[
            pl.BlockSpec((1, new, width // parts), lambda i, j: (i, 0, j)),
            pl.BlockSpec((1, new, kv_width // parts), lambda i, j: (i, 0, j)),
            pl.BlockSpec((1, new, kv_width // parts), lambda i, j: (i, 0, j)),
        ],
        out_specs=[
            pl.BlockSpec((1, new, width // parts), lambda i, j: (i, 0, j)),
            pl.BlockSpec((1, new, pair_width // parts), lambda i, j: (i, 0, j)),
        ],
        compiler_params=params(24),
        cost_estimate=cost(4 * local * new * new * width, local * new * new * width // HEAD, 6 * local * new * width),
        name="attend_new",
    )(queries, new_keys, new_values)

    weights, part = pl.pallas_call(
        weigh_step,
        grid=(local, parts),
        out_shape=[
            jax.ShapeDtypeStruct((local, new, pair_width), bf16),
            jax.ShapeDtypeStruct((local, new, width), bf16),
        ],
        in_specs=[
            pl.BlockSpec((1, new, width // parts), lambda i, j: (i, 0, j)),
            pl.BlockSpec((heads // parts, step, HEAD), lambda i, j: (j, i, 0)),
            pl.BlockSpec((1, new, pair_width // parts), lambda i, j: (i, 0, j)),
            pl.BlockSpec((1, new, width // parts), lambda i, j: (i, 0, j)),
        ],
        out_specs=[
            pl.BlockSpec((1, new, pair_width // parts), lambda i, j: (i, 0, j)),
            pl.BlockSpec((1, new, width // parts), lambda i, j: (i, 0, j)),
        ],
        compiler_params=params(24),
        cost_estimate=cost(4 * local * new * step * width, local * new * step * width // HEAD, 6 * local * new * width),
        name="weigh_step",
    )(queries, step_keys, lse, part)

    attended = pl.pallas_call(
        add_step,
        grid=(local, parts),
        out_shape=jax.ShapeDtypeStruct((local, new, width), bf16),
        in_specs=[
            pl.BlockSpec((heads // parts, step, HEAD), lambda i, j: (j, i, 0)),
            pl.BlockSpec((1, new, pair_width // parts), lambda i, j: (i, 0, j)),
            pl.BlockSpec((1, new, width // parts), lambda i, j: (i, 0, j)),
        ],
        out_specs=pl.BlockSpec((1, new, width // parts), lambda i, j: (i, 0, j)),
        compiler_params=params(24),
        cost_estimate=cost(2 * local * new * step * width, 0, 5 * local * new * width),
        name="add_step",
    )(step_values, weights, part)
    return (attended, child_share)


def solution(mesh):
    in_specs = (
        P(("prompts", "beam"), None, None),
        P(("prompts", "beam"), None, None),
        P(("prompts", "beam"), None, None),
        P(("prompts", "beam"), None, None, None),
        P(("prompts", "beam"), None),
        P(),
        P("prompts"),
    )
    out_specs = (P(("prompts", "beam"), None, None), P(("prompts", "beam")))
    return jax.shard_map(body, mesh=mesh, in_specs=in_specs, out_specs=out_specs, check_vma=False)
```

```python
import functools
import math

import jax
import jax.numpy as jnp
from jax import lax
from jax.experimental import pallas as pl
from jax.experimental.pallas import tpu as pltpu
from jax.sharding import PartitionSpec as P

HEAD = 128
KEEP = 2
MARK = 16
WAIT = (0, 1, 2, 2)
LOG2E = math.log2(math.e)
MIB = 1 << 20
NT = (((1,), (1,)), ((), ()))
NN = (((1,), (0,)), ((), ()))


def mm(a, b, dims=NN):
    return lax.dot_general(a, b, dims, preferred_element_type=jnp.float32)


def kept_pair(parents, base, local):
    own = (parents >= base) & (parents < base + local)
    first = jnp.min(jnp.where(own, parents - base, local))
    last = jnp.max(jnp.where(own, parents - base, -1))
    return first, last


def pack(parents_ref, kv_ref, last_ref, value_ref, out_ref, held_ref, sems):
    local, _, step, width = kv_ref.shape
    heads = width // HEAD
    base = lax.axis_index("beam") * local
    kept = kept_pair(parents_ref[...], base, local)
    copies = [pltpu.make_async_copy(kv_ref.at[k], held_ref.at[r], sems.at[r]) for r, k in enumerate(kept)]
    for copy in copies:
        copy.start()
    hidden = last_ref[...].astype(jnp.float32)
    square = jnp.mean(hidden * hidden, axis=-1, keepdims=True)
    normed = hidden * lax.rsqrt(square + 1e-05)
    score = jnp.sum(normed * value_ref[...], axis=-1, keepdims=True)
    reward = jax.nn.sigmoid(score)
    row = lax.broadcasted_iota(jnp.int32, reward.shape, 0)
    marks = [jnp.sum(jnp.where(row == k, reward, 0.0)) for k in kept]
    tile = lax.broadcasted_iota(jnp.int32, (MARK, HEAD), 0)
    tile = jnp.where(tile < MARK // 2, marks[0], marks[1]).astype(jnp.bfloat16)
    for d in range(out_ref.shape[0]):
        out_ref[d, KEEP * 2 * step :, :] = tile
    for r, copy in enumerate(copies):
        copy.wait()
        for s in range(2):
            for f in range(heads):
                piece = held_ref[r, s, :, f * HEAD : (f + 1) * HEAD]
                start = (r * 2 + s) * step
                for d in range(f, out_ref.shape[0], heads):
                    out_ref[d, start : start + step, :] = piece


def pick(item_ref, table_ref, _, *out_refs):
    rows = (table_ref.shape[1] - MARK) // KEEP
    chips = len(out_refs)
    local = out_refs[0].shape[0] // (2 * rows)
    chip = lax.axis_index("beam") % (2 * chips) // 2
    core = lax.axis_index("beam") % 2
    for m in range(chips):
        for other in range(2):
            owner = (chip ^ m) * 2 + (core ^ other)
            for i in range(local):
                item = item_ref[owner * local + i]
                start = pl.multiple_of((item % KEEP) * rows, rows)
                to = (other * local + i) * rows
                out_refs[m][to : to + rows, :] = table_ref[item // KEEP, pl.ds(start, rows), :]


def share_rewards(item_ref, table_ref, _, out_ref):
    children, local = item_ref.shape[0], out_ref.shape[1]
    rows = table_ref.shape[1] - MARK
    mine = lax.axis_index("beam") * local
    upper = lax.broadcasted_iota(jnp.int32, (MARK, HEAD), 0) < MARK // 2
    lane = lax.broadcasted_iota(jnp.int32, (1, HEAD), 1)

    def reward(child):
        item = item_ref[child]
        tile = table_ref[item // KEEP, rows:, :].astype(jnp.float32)
        tile = jnp.where(upper == (item % KEEP == 0), tile, 0.0)
        return tile[:1, :] + tile[MARK // 2 : MARK // 2 + 1, :]

    total = jnp.zeros((1, HEAD), jnp.float32)
    for child in range(children):
        total = total + reward(child)
    picked = jnp.zeros((1, HEAD), jnp.float32)
    for i in range(local):
        picked = jnp.where(lane == i, reward(mine + i), picked)
    out_ref[...] = (children * picked / total)[:, :local]


def attend_new(q_ref, k_ref, v_ref, out_ref, stat_ref):
    new = q_ref.shape[1]
    half = new // 2
    heads = k_ref.shape[2] // HEAD
    group = q_ref.shape[2] // k_ref.shape[2]
    count = heads * group
    scale = HEAD**-0.5 * LOG2E
    ones = jnp.ones((new, HEAD), jnp.bfloat16)
    lane = lax.broadcasted_iota(jnp.int32, (half, HEAD), 1)
    row = lax.broadcasted_iota(jnp.int32, (half, half), 0)
    column = lax.broadcasted_iota(jnp.int32, (half, half), 1)
    bias = jnp.concatenate([jnp.where(column <= row, 0.0, -jnp.inf)] * group, axis=0)
    tops = [jnp.zeros((half, HEAD), jnp.float32) for _ in range(2)]
    sums = [jnp.ones((half, HEAD), jnp.float32) for _ in range(2)]
    for f in range(heads):
        keys = k_ref[0, :, f * HEAD : (f + 1) * HEAD]
        values = jnp.concatenate([v_ref[0, :, f * HEAD : (f + 1) * HEAD], ones], axis=1)
        columns = [slice((f * group + h) * HEAD, (f * group + h + 1) * HEAD) for h in range(group)]
        for r in range(2):
            seen = (r + 1) * half
            rows = slice(r * half, (r + 1) * half)
            query = jnp.concatenate([q_ref[0, rows, c] for c in columns], axis=0)
            logits = mm(query, keys[:seen], NT) * scale
            masked = logits[:, seen - half :] + bias
            if r == 0:
                logits = masked
                top = jnp.max(masked, axis=1, keepdims=True)
            else:
                free = logits[:, :half]
                logits = jnp.concatenate([free, masked], axis=1)
                top = jnp.max(jnp.maximum(free, masked), axis=1, keepdims=True)
            weights = jnp.exp2(logits - top).astype(jnp.bfloat16)
            both = mm(weights, values[:seen])
            total = both[:, HEAD:]
            part = both[:, :HEAD] * pltpu.reciprocal(total, approx=True)
            for h in range(group):
                s = slice(h * half, (h + 1) * half)
                out_ref[0, rows, columns[h]] = part[s].astype(jnp.bfloat16)
                here = lane == f * group + h
                tops[r] = jnp.where(here, top[s], tops[r])
                sums[r] = jnp.where(here, total[s], sums[r])
    for r in range(2):
        lse = (tops[r] + jnp.log2(sums[r])) * (-1.0 / scale)
        high = lse.astype(jnp.bfloat16).astype(jnp.float32)
        rest = pltpu.roll(lse - high, count, 1)
        both = jnp.where(lane < count, high, jnp.where(lane < 2 * count, rest, 0.0))
        stat_ref[0, r * half : (r + 1) * half, :] = both.astype(jnp.bfloat16)


def block_pair(a):
    zero = jnp.zeros_like(a)
    return jnp.concatenate([jnp.concatenate([a, zero], axis=1), jnp.concatenate([zero, a], axis=1)], axis=0)


def forward(sent_ref, _, out_ref):
    out_ref[...] = sent_ref[sent_ref.shape[0] - out_ref.shape[0] :, :]


def attend_block(q_ref, part_ref, stat_ref, own_ref, other_ref, out_ref, place, i, f, shifted):
    new, width = q_ref.shape[1:]
    rows = own_ref.shape[0] // (2 * q_ref.shape[0])
    step = rows // 2
    pairs = width // (2 * HEAD)
    core = lax.axis_index("beam") % 2
    scale = HEAD**-0.5 * LOG2E
    ones = block_pair(jnp.ones((step, HEAD), jnp.bfloat16))
    lane = lax.broadcasted_iota(jnp.int32, (new, HEAD), 1)
    pair_of_lane = lane % (HEAD // 4) // 2 - place * pairs
    odd_lane = lax.broadcasted_iota(jnp.int32, (rows, HEAD), 1) % 2
    spread = (odd_lane == lax.broadcasted_iota(jnp.int32, (rows, HEAD), 0) // step).astype(jnp.bfloat16)
    low = lax.broadcasted_iota(jnp.int32, (new * pairs // 2, HEAD), 1) < step

    here = pl.ds(pl.multiple_of(i * rows, rows), rows)
    piece = jnp.where(f == core, own_ref[here, :], other_ref[here, :])
    stat = stat_ref[i]
    keys = jnp.concatenate([block_pair(piece[:step]), spread], axis=1)
    values = jnp.concatenate([block_pair(piece[step:]), ones], axis=1)
    group = [f * (pairs // 2) + p for p in range(pairs // 2)]
    columns = [pl.ds(pl.multiple_of(p * 2 * HEAD, 2 * HEAD), 2 * HEAD) for p in group]
    shifts = [jnp.where(pair_of_lane == p, stat, jnp.zeros_like(stat)) for p in group]
    left = [jnp.concatenate([q_ref[i, :, c], t], axis=1) for c, t in zip(columns, shifts)]
    logits = mm(jnp.concatenate(left, axis=0), keys, NT) * scale
    part = jnp.concatenate([part_ref[i, :, c] for c in columns], axis=0).astype(jnp.float32)
    rest = 1.0
    most = None
    if shifted:
        tops = [jnp.maximum(jnp.max(jnp.where(k, logits, 0.0), axis=1, keepdims=True), 0.0) for k in (low, ~low)]
        logits = logits - jnp.where(low, tops[0], tops[1])
        rest = jnp.concatenate([jnp.broadcast_to(jnp.exp2(-t), low.shape) for t in tops], axis=1)
        part = part * rest
    else:
        most = jnp.max(logits.reshape(-1, 8, HEAD), axis=0)
    both = mm(jnp.exp2(logits).astype(jnp.bfloat16), values)
    share = pltpu.reciprocal(rest + both[:, 2 * HEAD :], approx=True)
    result = ((part + both[:, : 2 * HEAD]) * share).astype(jnp.bfloat16)
    for n, c in enumerate(columns):
        out_ref[i, :, c] = result[n * new : (n + 1) * new]
    return most


def attend_blocks(q_ref, part_ref, stat_ref, own_ref, other_ref, held_ref, out_ref, sems, place, ready):
    local, _, width = q_ref.shape
    lanes = pl.ds(pl.multiple_of(place * width, width), width)
    refs = (q_ref, part_ref, stat_ref, own_ref, other_ref, held_ref, place)

    def send(i):
        return pltpu.make_async_copy(held_ref.at[i], out_ref.at[i, :, lanes], sems.at[i])

    def work(i, most):
        ready(i)
        most = jnp.maximum(most, jnp.maximum(attend_block(*refs, i, 0, False), attend_block(*refs, i, 1, False)))
        send(i).start()
        return most

    most = lax.fori_loop(0, local, work, jnp.full((8, HEAD), -jnp.inf, jnp.float32))
    for i in range(local):
        send(i).wait()

    @pl.when(jnp.max(most) > 100.0)
    def _():
        lax.fori_loop(0, 2 * local, lambda t, c: (attend_block(*refs, t // 2, t % 2, True), c)[1], 0)
        for i in range(local):
            send(i).start()
        for i in range(local):
            send(i).wait()


def attend_first(q_ref, part_ref, stat_ref, own_ref, other_ref, *refs):
    out_ref, later_q, later_part, later_stat, token_ref, held_q, held_part, held, sems, stat_sem, out_sems = refs
    stat_copy = pltpu.make_async_copy(stat_ref, later_stat, stat_sem)
    stat_copy.start()
    token_ref[...] = jnp.zeros_like(token_ref)
    local, _, width = held.shape
    chips = later_q.shape[0] + 1
    chip = lax.axis_index("beam") % (2 * chips) // 2

    def copy(k, m, i, to):
        lanes = pl.ds(pl.multiple_of((chip ^ m) * width, width), width)
        return pltpu.make_async_copy((q_ref, part_ref)[k].at[i, :, lanes], to.at[i], sems.at[k, m, i])

    targets = [(held_q, held_part)] + [(later_q.at[m], later_part.at[m]) for m in range(chips - 1)]
    for m in range(chips):
        for i in range(local):
            for k in range(2):
                copy(k, m, i, targets[m][k]).start()

    def ready(i):
        for k in range(2):
            copy(k, 0, i, targets[0][k]).wait()

    stat_copy.wait()
    attend_blocks(held_q, held_part, later_stat, own_ref, other_ref, held, out_ref, out_sems, chip, ready)
    for m in range(1, chips):
        for i in range(local):
            for k in range(2):
                copy(k, m, i, targets[m][k]).wait()


def attend_later(m, q_ref, part_ref, stat_ref, own_ref, other_ref, _, out_ref, token_ref, held, sems):
    chips = q_ref.shape[0] + 1
    place = lax.axis_index("beam") % (2 * chips) // 2 ^ m
    token_ref[...] = jnp.zeros_like(token_ref)
    views = (q_ref.at[m - 1], part_ref.at[m - 1])
    attend_blocks(*views, stat_ref, own_ref, other_ref, held, out_ref, sems, place, lambda i: None)


def params(mib):
    return pltpu.CompilerParams(vmem_limit_bytes=mib * MIB)


def swap(a, distance):
    count = lax.axis_size("beam")
    return lax.ppermute(a, "beam", [(i, i ^ distance) for i in range(count)])


def body(queries, new_keys, new_values, step_kv, prm_last, value_head, parents):
    beam_count = lax.axis_size("beam")
    group_index = lax.axis_index("beam")
    local, new, width = queries.shape
    children = parents.shape[0]
    step = step_kv.shape[2]
    kv_width = step_kv.shape[3]
    heads = kv_width // HEAD
    chips = heads // 2
    vmem = pl.BlockSpec(memory_space=pltpu.VMEM)
    smem = pl.BlockSpec(memory_space=pltpu.SMEM)
    bf16 = jnp.bfloat16

    rows = 2 * step
    in_hbm = lambda a: pltpu.with_memory_space_constraint(a, pltpu.HBM)
    in_vmem = lambda a: pltpu.with_memory_space_constraint(a, pltpu.VMEM)
    packed = pl.pallas_call(
        pack,
        out_shape=jax.ShapeDtypeStruct((beam_count, KEEP * rows + MARK, HEAD), bf16),
        in_specs=[vmem, pl.BlockSpec(memory_space=pl.ANY), vmem, vmem],
        out_specs=vmem,
        scratch_shapes=[pltpu.VMEM((KEEP, 2, step, kv_width), bf16), pltpu.SemaphoreType.DMA((KEEP,))],
        name="pack",
    )(parents.reshape(1, children), step_kv, prm_last, value_head.reshape(1, -1))
    table = lax.all_to_all(packed, "beam", 0, 0)

    cost = lambda f, t, b: pl.CostEstimate(flops=f, transcendentals=t, bytes_accessed=b)
    whole = lambda w: pl.BlockSpec((1, new, w), lambda i: (i, 0, 0))
    part, stat = pl.pallas_call(
        attend_new,
        grid=(local,),
        out_shape=[
            jax.ShapeDtypeStruct((local, new, width), bf16),
            jax.ShapeDtypeStruct((local, new, HEAD), bf16),
        ],
        in_specs=[whole(width), whole(kv_width), whole(kv_width)],
        out_specs=[whole(width), whole(HEAD)],
        compiler_params=params(56),
        cost_estimate=cost(4 * local * new * new * width, local * new * new * width // HEAD, 6 * local * new * width),
        name="attend_new",
    )(queries, new_keys, new_values)

    owner = parents // local
    earlier = (owner[:, None] == owner[None, :]) & (parents[None, :] < parents[:, None])
    item = owner * KEEP + jnp.any(earlier, axis=1).astype(jnp.int32)
    near = lax.dynamic_slice_in_dim(item, group_index // heads * (heads * local), heads * local)
    pieces = pl.pallas_call(
        pick,
        out_shape=[jax.ShapeDtypeStruct((2 * local * rows, HEAD), bf16)] * chips,
        in_specs=[smem, vmem, pl.BlockSpec(memory_space=pl.ANY)],
        out_specs=[vmem] * chips,
        compiler_params=params(4),
        name="pick",
    )(near, table, in_hbm(stat))

    anywhere = pl.BlockSpec(memory_space=pl.ANY)
    hbm = pl.BlockSpec(memory_space=pltpu.HBM)
    wide = width // chips
    own = [pieces[0]] + [swap(pieces[m], 2 * m) for m in range(1, chips)]
    done = [near]
    step_cost = cost(local * new * step * width, local * new * step * width // HEAD, 3 * local * new * width)
    result = jax.ShapeDtypeStruct((local, new, width), bf16)
    later = pltpu.VMEM((chips - 1, local, new, wide), bf16)
    held = pltpu.VMEM((local, new, wide), bf16)
    for m in range(chips):
        passed = pl.pallas_call(
            forward,
            out_shape=jax.ShapeDtypeStruct((local * rows, HEAD), bf16),
            in_specs=[vmem, anywhere],
            out_specs=vmem,
            compiler_params=params(2),
            name="forward",
        )(own[m], done[WAIT[m]])
        other = swap(passed, 1)
        if m == 0:
            attended, later_q, later_part, later_stat, token = pl.pallas_call(
                attend_first,
                out_shape=[result, later, later, pltpu.VMEM(stat.shape, bf16), jax.ShapeDtypeStruct((8, HEAD), jnp.float32)],
                in_specs=[hbm, hbm, hbm, vmem, vmem],
                out_specs=[hbm] + [vmem] * 4,
                scratch_shapes=[held] * 3
                + [pltpu.SemaphoreType.DMA((2, chips, local)), pltpu.SemaphoreType.DMA, pltpu.SemaphoreType.DMA((local,))],
                compiler_params=params(16),
                cost_estimate=step_cost,
                name="attend_first",
            )(in_hbm(queries), in_hbm(part), in_hbm(stat), own[m], other)
            done.append(token)
        else:
            attended, token = pl.pallas_call(
                functools.partial(attend_later, m),
                out_shape=[result, jax.ShapeDtypeStruct((8, HEAD), jnp.float32)],
                in_specs=[vmem] * 5 + [hbm],
                out_specs=[hbm, vmem],
                scratch_shapes=[held, pltpu.SemaphoreType.DMA((local,))],
                input_output_aliases={5: 0},
                compiler_params=params(12),
                cost_estimate=step_cost,
                name="attend_later",
            )(in_vmem(later_q), in_vmem(later_part), in_vmem(later_stat), own[m], other, attended)
            done.append(token)

    child_share = pl.pallas_call(
        share_rewards,
        out_shape=jax.ShapeDtypeStruct((1, local), jnp.float32),
        in_specs=[smem, vmem, vmem],
        out_specs=vmem,
        compiler_params=params(2),
        name="share_rewards",
    )(item, table, done[1]).reshape(local)
    return (attended, child_share)


def solution(mesh):
    in_specs = (
        P(("prompts", "beam"), None, None),
        P(("prompts", "beam"), None, None),
        P(("prompts", "beam"), None, None),
        P(("prompts", "beam"), None, None, None),
        P(("prompts", "beam"), None),
        P(),
        P("prompts"),
    )
    out_specs = (P(("prompts", "beam"), None, None), P(("prompts", "beam")))
    return jax.shard_map(body, mesh=mesh, in_specs=in_specs, out_specs=out_specs, check_vma=False)
```

```python
import functools
import math

import jax
import jax.numpy as jnp
from jax import lax
from jax.experimental import pallas as pl
from jax.experimental.pallas import tpu as pltpu
from jax.sharding import PartitionSpec as P

HEAD = 128
KEEP = 2
MARK = 16
LIMIT = 100.0
LOG2E = math.log2(math.e)
MIB = 1 << 20
NT = (((1,), (1,)), ((), ()))
NN = (((1,), (0,)), ((), ()))


def mm(a, b, dims=NN):
    return lax.dot_general(a, b, dims, preferred_element_type=jnp.float32)


def kept_pair(parents, base, local):
    own = (parents >= base) & (parents < base + local)
    first = jnp.min(jnp.where(own, parents - base, local))
    last = jnp.max(jnp.where(own, parents - base, -1))
    return first, last


def pack(parents_ref, kv_ref, last_ref, value_ref, out_ref, held_ref, sems):
    local, _, step, width = kv_ref.shape
    heads = width // HEAD
    base = lax.axis_index("beam") * local
    kept = kept_pair(parents_ref[...], base, local)
    copies = [pltpu.make_async_copy(kv_ref.at[k], held_ref.at[r], sems.at[r]) for r, k in enumerate(kept)]
    for copy in copies:
        copy.start()
    hidden = last_ref[...].astype(jnp.float32)
    square = jnp.mean(hidden * hidden, axis=-1, keepdims=True)
    normed = hidden * lax.rsqrt(square + 1e-05)
    score = jnp.sum(normed * value_ref[...], axis=-1, keepdims=True)
    reward = jax.nn.sigmoid(score)
    row = lax.broadcasted_iota(jnp.int32, reward.shape, 0)
    marks = [jnp.sum(jnp.where(row == k, reward, 0.0)) for k in kept]
    tile = lax.broadcasted_iota(jnp.int32, (MARK, HEAD), 0)
    tile = jnp.where(tile < MARK // 2, marks[0], marks[1]).astype(jnp.bfloat16)
    for d in range(out_ref.shape[0]):
        out_ref[d, KEEP * 2 * step :, :] = tile
    for r, copy in enumerate(copies):
        copy.wait()
        for s in range(2):
            for f in range(heads):
                piece = held_ref[r, s, :, f * HEAD : (f + 1) * HEAD]
                start = (r * 2 + s) * step
                for d in range(f, out_ref.shape[0], heads):
                    out_ref[d, start : start + step, :] = piece


def pick(chips, ms, item_ref, table_ref, _, *out_refs):
    rows = (table_ref.shape[1] - MARK) // KEEP
    local = out_refs[0].shape[0] // (2 * rows)
    chip = lax.axis_index("beam") % (2 * chips) // 2
    core = lax.axis_index("beam") % 2
    for n, m in enumerate(ms):
        for other in range(2):
            owner = (chip ^ m) * 2 + (core ^ other)
            for i in range(local):
                item = item_ref[owner * local + i]
                start = pl.multiple_of((item % KEEP) * rows, rows)
                to = (other * local + i) * rows
                out_refs[n][to : to + rows, :] = table_ref[item // KEEP, pl.ds(start, rows), :]


def share_rewards(item_ref, table_ref, out_ref):
    children, local = item_ref.shape[0], out_ref.shape[1]
    rows = table_ref.shape[1] - MARK
    mine = lax.axis_index("beam") * local
    upper = lax.broadcasted_iota(jnp.int32, (MARK, HEAD), 0) < MARK // 2
    lane = lax.broadcasted_iota(jnp.int32, (1, HEAD), 1)

    def reward(child):
        item = item_ref[child]
        tile = table_ref[item // KEEP, rows:, :].astype(jnp.float32)
        tile = jnp.where(upper == (item % KEEP == 0), tile, 0.0)
        return tile[:1, :] + tile[MARK // 2 : MARK // 2 + 1, :]

    total = jnp.zeros((1, HEAD), jnp.float32)
    for child in range(children):
        total = total + reward(child)
    picked = jnp.zeros((1, HEAD), jnp.float32)
    for i in range(local):
        picked = jnp.where(lane == i, reward(mine + i), picked)
    out_ref[...] = (children * picked / total)[:, :local]


def attend_new(q_ref, k_ref, v_ref, out_ref, stat_ref, sums_ref, tops_ref):
    new = q_ref.shape[1]
    half = new // 2
    heads = k_ref.shape[2] // HEAD
    group = q_ref.shape[2] // k_ref.shape[2]
    count = heads * group
    scale = HEAD**-0.5 * LOG2E
    ones = jnp.ones((new, HEAD), jnp.bfloat16)
    lane = lax.broadcasted_iota(jnp.int32, (half, HEAD), 1)
    row = lax.broadcasted_iota(jnp.int32, (half, half), 0)
    column = lax.broadcasted_iota(jnp.int32, (half, half), 1)
    hidden = jnp.concatenate([jnp.where(column <= row, 0.0, -jnp.inf)] * group, axis=0)
    sums_ref[...] = jnp.ones_like(sums_ref)
    tops_ref[...] = jnp.zeros_like(tops_ref)

    def block(f, shifted):
        lanes = lambda n: pl.ds(pl.multiple_of(n * HEAD, HEAD), HEAD)
        keys = k_ref[0, :, lanes(f)]
        values = jnp.concatenate([v_ref[0, :, lanes(f)], ones], axis=1)
        columns = [lanes(f * group + h) for h in range(group)]
        most = None
        for r in range(2):
            seen = (r + 1) * half
            rows = slice(r * half, (r + 1) * half)
            query = jnp.concatenate([q_ref[0, rows, c] for c in columns], axis=0)
            logits = mm(query, keys[:seen], NT) * scale
            blocks = [logits[:, n * half : (n + 1) * half] for n in range(r + 1)]
            if not shifted:
                for a in blocks:
                    size = jnp.max(jnp.abs(a).reshape(-1, 8, half), axis=0)
                    most = size if most is None else jnp.maximum(most, size)
            blocks[r] = blocks[r] + hidden
            if shifted:
                top = functools.reduce(jnp.maximum, [jnp.max(a, axis=1, keepdims=True) for a in blocks])
                top = top.astype(jnp.bfloat16).astype(jnp.float32)
                blocks = [a - top for a in blocks]
            weights = jnp.concatenate([jnp.exp2(a).astype(jnp.bfloat16) for a in blocks], axis=1)
            both = mm(weights, values[:seen])
            for h in range(group):
                s = slice(h * half, (h + 1) * half)
                out_ref[0, rows, columns[h]] = both[s, :HEAD].astype(jnp.bfloat16)
                here = lane == f * group + h
                sums_ref[rows, :] = jnp.where(here, both[s, HEAD:], sums_ref[rows, :])
                if shifted:
                    tops_ref[rows, :] = jnp.where(here, top[s], tops_ref[rows, :])
        return most

    most = functools.reduce(jnp.maximum, [block(f, False) for f in range(heads)])

    @pl.when(jnp.max(most) > LIMIT)
    def _():
        lax.fori_loop(0, heads, lambda f, c: (block(f, True), c)[1], 0)

    sums = sums_ref[...]
    high = sums.astype(jnp.bfloat16).astype(jnp.float32)
    rest = pltpu.roll(sums - high, count, 1)
    tops = pltpu.roll(tops_ref[...], 2 * count, 1)
    lane = lax.broadcasted_iota(jnp.int32, (new, HEAD), 1)
    stat = jnp.where(lane < count, high, jnp.where(lane < 2 * count, rest, jnp.where(lane < 3 * count, tops, 0.0)))
    stat_ref[0] = stat.astype(jnp.bfloat16)


def block_pair(a):
    zero = jnp.zeros_like(a)
    return jnp.concatenate([jnp.concatenate([a, zero], axis=1), jnp.concatenate([zero, a], axis=1)], axis=0)


def forward(sent_ref, _, out_ref):
    out_ref[...] = sent_ref[sent_ref.shape[0] - out_ref.shape[0] :, :]


class Block:
    def __init__(self, q_ref, part_ref, stat_ref, own_ref, other_ref, out_ref, count, place, i, f):
        new, width = q_ref.shape[1:]
        rows = own_ref.shape[0] // (2 * q_ref.shape[0])
        self.step = rows // 2
        pairs = width // (2 * HEAD)
        core = lax.axis_index("beam") % 2
        here = pl.ds(pl.multiple_of(i * rows, rows), rows)
        self.piece = jnp.where(f == core, own_ref[here, :], other_ref[here, :])
        group = [f * (pairs // 2) + p for p in range(pairs // 2)]
        self.columns = [pl.ds(pl.multiple_of(p * 2 * HEAD, 2 * HEAD), 2 * HEAD) for p in group]
        self.heads = [(place * pairs + p) * 2 for p in group]
        self.q_ref, self.part_ref, self.stat_ref, self.out_ref = q_ref, part_ref, stat_ref, out_ref
        self.i, self.count, self.new = i, count, new

    def logits(self):
        keys = block_pair(self.piece[: self.step])
        queries = jnp.concatenate([self.q_ref[self.i, :, c] for c in self.columns], axis=0)
        return mm(queries, keys, NT) * (HEAD**-0.5 * LOG2E)

    def tail(self):
        lane = lax.broadcasted_iota(jnp.int32, (self.new, HEAD), 1)
        pair_of_lane = jnp.where(lane < 2 * self.count, lane % self.count // 2 * 2, -1)
        stat = self.stat_ref[self.i]
        sums = jnp.concatenate([jnp.where(pair_of_lane == h, stat, jnp.zeros_like(stat)) for h in self.heads], axis=0)
        part = jnp.concatenate([self.part_ref[self.i, :, c] for c in self.columns], axis=0).astype(jnp.float32)
        values = block_pair(self.piece[self.step :])
        ones = block_pair(jnp.ones((self.step, HEAD), jnp.bfloat16))
        odd = lax.broadcasted_iota(jnp.int32, (HEAD, 2 * HEAD), 0) % 2
        spread = (odd == lax.broadcasted_iota(jnp.int32, (HEAD, 2 * HEAD), 1) // HEAD).astype(jnp.bfloat16)
        return values, ones, spread, sums, part

    def store(self, added, total):
        result = (added * pltpu.reciprocal(total, approx=True)).astype(jnp.bfloat16)
        for n, c in enumerate(self.columns):
            self.out_ref[self.i, :, c] = result[n * self.new : (n + 1) * self.new]

    def weigh(self):
        logits = self.logits()
        return jnp.exp2(logits).astype(jnp.bfloat16), jnp.max(logits.reshape(-1, 8, HEAD), axis=0)

    def finish(self, weights):
        part = jnp.concatenate([self.part_ref[self.i, :, c] for c in self.columns], axis=0).astype(jnp.float32)
        added = mm(weights, block_pair(self.piece[self.step :]))
        lane = lax.broadcasted_iota(jnp.int32, (self.new, HEAD), 1)
        low = lax.broadcasted_iota(jnp.int32, weights.shape, 1) < self.step
        stat = self.stat_ref[self.i].astype(jnp.float32)
        here = jnp.where(lane < 2 * self.count, lane % self.count, -1)
        wide = weights.astype(jnp.float32)
        totals = []
        for n, k in enumerate((low, ~low)):
            sums = jnp.concatenate([jnp.where(here == h + n, stat, 0.0) for h in self.heads], axis=0)
            total = jnp.sum(jnp.where(k, wide, 0.0) + sums, axis=1, keepdims=True)
            totals.append(jnp.broadcast_to(pltpu.reciprocal(total, approx=True), low.shape))
        result = ((part + added) * jnp.concatenate(totals, axis=1)).astype(jnp.bfloat16)
        for n, c in enumerate(self.columns):
            self.out_ref[self.i, :, c] = result[n * self.new : (n + 1) * self.new]

    def shifted(self):
        logits = self.logits()
        low = lax.broadcasted_iota(jnp.int32, logits.shape, 1) < self.step
        lane = lax.broadcasted_iota(jnp.int32, (self.new, HEAD), 1) - 2 * self.count
        stat = self.stat_ref[self.i].astype(jnp.float32)
        shift = lambda h: jnp.sum(jnp.where(lane == h, stat, 0.0), axis=1, keepdims=True)
        shifts = [jnp.concatenate([shift(h + n) for h in self.heads], axis=0) for n in range(2)]
        logits = logits - jnp.where(low, shifts[0], shifts[1])
        tops = [jnp.maximum(jnp.max(jnp.where(k, logits, 0.0), axis=1, keepdims=True), 0.0) for k in (low, ~low)]
        weights = jnp.exp2(logits - jnp.where(low, tops[0], tops[1])).astype(jnp.bfloat16)
        rest = jnp.concatenate([jnp.broadcast_to(jnp.exp2(-t), low.shape) for t in tops], axis=1)
        values, ones, spread, sums, part = self.tail()
        self.store(part * rest + mm(weights, values), mm(weights, ones) + mm(sums, spread) * rest)


def attend_blocks(works, stat_ref, held_ref, out_ref, sems, ready):
    local, _, width = works[0][0].shape
    count = out_ref.shape[2] // HEAD

    def block(n, i, f):
        q_ref, part_ref, own_ref, other_ref, place = works[n]
        return Block(q_ref, part_ref, stat_ref, own_ref, other_ref, held_ref.at[n], count, place, i, f)

    def send(n, i):
        lanes = pl.ds(pl.multiple_of(works[n][4] * width, width), width)
        return pltpu.make_async_copy(held_ref.at[n, i], out_ref.at[i, :, lanes], sems.at[n, i])

    lane = lax.broadcasted_iota(jnp.int32, stat_ref.shape[1:], 1)

    def work(n, i, carry):
        most, weights = carry
        later, top = block(n, i, 1).weigh()
        block(n, i, 0).finish(weights)
        most = jnp.maximum(most, top)
        following = jnp.minimum(i + 1, local - 1)
        ready(following, i + 1 < local)
        weights, top = block(n, following, 0).weigh()
        block(n, i, 1).finish(later)
        send(n, i).start()
        return jnp.maximum(most, top), weights

    def moved(i, most):
        tops = jnp.where(lane >= 2 * count, stat_ref[i].astype(jnp.float32), 0.0)
        tops = jnp.where(tops == 0.0, -jnp.inf, jnp.inf)
        return jnp.maximum(most, jnp.max(tops.reshape(-1, 8, HEAD), axis=0))

    most = jnp.full((8, HEAD), -jnp.inf, jnp.float32)
    ready(0, True)
    for n in range(len(works)):
        weights, top = block(n, 0, 0).weigh()
        most, _ = lax.fori_loop(0, local, functools.partial(work, n), (jnp.maximum(most, top), weights))
    most = lax.fori_loop(0, local, moved, most)
    every = [(n, i) for n in range(len(works)) for i in range(local)]
    for n, i in every:
        send(n, i).wait()

    @pl.when(jnp.max(most) > LIMIT)
    def _():
        for n in range(len(works)):
            lax.fori_loop(0, 2 * local, lambda t, c: (block(n, t // 2, t % 2).shifted(), c)[1], 0)
        for n, i in every:
            send(n, i).start()
        for n, i in every:
            send(n, i).wait()


def stage(q_ref, part_ref, m, i, to_q, to_part, sems, chips):
    width = to_q.shape[2]
    place = lax.axis_index("beam") % (2 * chips) // 2 ^ m
    lanes = pl.ds(pl.multiple_of(place * width, width), width)
    pairs = ((q_ref, to_q), (part_ref, to_part))
    return [pltpu.make_async_copy(a.at[i, :, lanes], to.at[i], sems.at[k, i]) for k, (a, to) in enumerate(pairs)]


def attend_first(chips, item_ref, table_ref, q_ref, part_ref, stat_ref, own_ref, other_ref, *refs):
    out_ref, share_ref, next_q, next_part, stat_out, token_ref = refs[:6]
    held_q, held_part, held, sems, next_sems, stat_sem, out_sems = refs[6:]
    local = held_q.shape[0]
    chip = lax.axis_index("beam") % (2 * chips) // 2
    mine = lambda i: stage(q_ref, part_ref, 0, i, held_q, held_part, sems, chips)
    following = lambda i: stage(q_ref, part_ref, 1, i, next_q, next_part, next_sems, chips)
    stat_copy = pltpu.make_async_copy(stat_ref, stat_out, stat_sem)
    stat_copy.start()
    for i in range(local):
        for copy in mine(i):
            copy.start()
    token_ref[...] = jnp.zeros_like(token_ref)
    share_rewards(item_ref, table_ref, share_ref)

    def ready(i, due):
        @pl.when(due)
        def _():
            for copy in mine(i):
                copy.wait()
            for copy in following(i):
                copy.start()

    stat_copy.wait()
    attend_blocks([(held_q, held_part, own_ref, other_ref, chip)], stat_out, held, out_ref, out_sems, ready)
    for i in range(local):
        for copy in following(i):
            copy.wait()


def attend_second(chips, q_ref, part_ref, next_q, next_part, stat_ref, own_ref, other_ref, _, *refs):
    out_ref, token_ref, *later = refs[: 2 + 2 * (chips - 2)]
    held, sems, next_sems = refs[2 + 2 * (chips - 2) :]
    local = held.shape[1]
    chip = lax.axis_index("beam") % (2 * chips) // 2

    def staged():
        for n, m in enumerate(range(2, chips)):
            for i in range(local):
                yield from stage(q_ref, part_ref, m, i, later[2 * n], later[2 * n + 1], next_sems.at[n], chips)

    for copy in staged():
        copy.start()
    token_ref[...] = jnp.zeros_like(token_ref)
    works = [(next_q, next_part, own_ref, other_ref, chip ^ 1)]
    attend_blocks(works, stat_ref, held, out_ref, sems, lambda i, due: None)
    for copy in staged():
        copy.wait()


def attend_last(chips, stat_ref, *refs):
    operands, (_, out_ref, held, sems) = refs[: 4 * (chips - 2)], refs[4 * (chips - 2) :]
    chip = lax.axis_index("beam") % (2 * chips) // 2
    works = [(*operands[4 * n : 4 * n + 4], chip ^ m) for n, m in enumerate(range(2, chips))]
    attend_blocks(works, stat_ref, held, out_ref, sems, lambda i, due: None)


def params(mib):
    return pltpu.CompilerParams(vmem_limit_bytes=mib * MIB)


def swap(a, distance):
    count = lax.axis_size("beam")
    return lax.ppermute(a, "beam", [(i, i ^ distance) for i in range(count)])


def body(queries, new_keys, new_values, step_kv, prm_last, value_head, parents):
    beam_count = lax.axis_size("beam")
    group_index = lax.axis_index("beam")
    local, new, width = queries.shape
    children = parents.shape[0]
    step = step_kv.shape[2]
    kv_width = step_kv.shape[3]
    heads = kv_width // HEAD
    chips = heads // 2
    vmem = pl.BlockSpec(memory_space=pltpu.VMEM)
    smem = pl.BlockSpec(memory_space=pltpu.SMEM)
    bf16 = jnp.bfloat16

    rows = 2 * step
    in_hbm = lambda a: pltpu.with_memory_space_constraint(a, pltpu.HBM)
    in_vmem = lambda a: pltpu.with_memory_space_constraint(a, pltpu.VMEM)
    packed = pl.pallas_call(
        pack,
        out_shape=jax.ShapeDtypeStruct((beam_count, KEEP * rows + MARK, HEAD), bf16),
        in_specs=[vmem, pl.BlockSpec(memory_space=pl.ANY), vmem, vmem],
        out_specs=vmem,
        scratch_shapes=[pltpu.VMEM((KEEP, 2, step, kv_width), bf16), pltpu.SemaphoreType.DMA((KEEP,))],
        name="pack",
    )(parents.reshape(1, children), step_kv, prm_last, value_head.reshape(1, -1))
    table = lax.all_to_all(packed, "beam", 0, 0)

    cost = lambda f, t, b: pl.CostEstimate(flops=f, transcendentals=t, bytes_accessed=b)
    small = cost(1024, 0, 1024)
    whole = lambda w: pl.BlockSpec((1, new, w), lambda i: (i, 0, 0))
    part, stat = pl.pallas_call(
        attend_new,
        grid=(local,),
        out_shape=[
            jax.ShapeDtypeStruct((local, new, width), bf16),
            jax.ShapeDtypeStruct((local, new, HEAD), bf16),
        ],
        in_specs=[whole(width), whole(kv_width), whole(kv_width)],
        out_specs=[whole(width), whole(HEAD)],
        scratch_shapes=[pltpu.VMEM((new, HEAD), jnp.float32)] * 2,
        compiler_params=params(56),
        cost_estimate=cost(4 * local * new * new * width, local * new * new * width // HEAD, 6 * local * new * width),
        name="attend_new",
    )(queries, new_keys, new_values)

    owner = parents // local
    earlier = (owner[:, None] == owner[None, :]) & (parents[None, :] < parents[:, None])
    item = owner * KEEP + jnp.any(earlier, axis=1).astype(jnp.int32)
    near = lax.dynamic_slice_in_dim(item, group_index // heads * (heads * local), heads * local)
    anywhere = pl.BlockSpec(memory_space=pl.ANY)
    hbm = pl.BlockSpec(memory_space=pltpu.HBM)

    def picked(ms, after):
        return pl.pallas_call(
            functools.partial(pick, chips, ms),
            out_shape=[jax.ShapeDtypeStruct((2 * local * rows, HEAD), bf16)] * len(ms),
            in_specs=[smem, vmem, anywhere],
            out_specs=[vmem] * len(ms),
            compiler_params=params(4),
            cost_estimate=small,
            name="pick",
        )(near, table, after)

    def pass_on(piece, after):
        passed = pl.pallas_call(
            forward,
            out_shape=jax.ShapeDtypeStruct((local * rows, HEAD), bf16),
            in_specs=[vmem, anywhere],
            out_specs=vmem,
            compiler_params=params(2),
            cost_estimate=small,
            name="forward",
        )(piece, after)
        return swap(passed, 1)

    far = tuple(range(2, chips))
    pieces = picked(far, in_hbm(stat))
    pieces = picked((0, 1), pieces[0]) + pieces
    own = [pieces[0]] + [swap(pieces[m], 2 * m) for m in range(1, chips)]
    wide = width // chips
    result = jax.ShapeDtypeStruct((local, new, width), bf16)
    token = jax.ShapeDtypeStruct((8, HEAD), jnp.float32)
    later = pltpu.VMEM((local, new, wide), bf16)
    held = lambda n: pltpu.VMEM((n, local, new, wide), bf16)
    many = pltpu.SemaphoreType.DMA
    attended, child_share, next_q, next_part, stat_held, done = pl.pallas_call(
        functools.partial(attend_first, chips),
        out_shape=[
            result,
            jax.ShapeDtypeStruct((1, local), jnp.float32),
            later,
            later,
            pltpu.VMEM(stat.shape, bf16),
            token,
        ],
        in_specs=[smem, vmem, hbm, hbm, hbm, vmem, vmem],
        out_specs=[hbm] + [vmem] * 5,
        scratch_shapes=[later] * 2 + [held(1), many((2, local)), many((2, local)), many, many((1, local))],
        compiler_params=params(16),
        cost_estimate=small,
        name="attend_first",
    )(item, table, in_hbm(queries), in_hbm(part), in_hbm(stat), own[0], pass_on(own[0], near))
    attended, done, *staged = pl.pallas_call(
        functools.partial(attend_second, chips),
        out_shape=[result, token] + [later] * (2 * len(far)),
        in_specs=[hbm, hbm] + [vmem] * 5 + [hbm],
        out_specs=[hbm, vmem] + [vmem] * (2 * len(far)),
        scratch_shapes=[held(1), many((1, local)), many((len(far), 2, local))],
        input_output_aliases={7: 0},
        compiler_params=params(12),
        cost_estimate=small,
        name="attend_second",
    )(
        in_hbm(queries),
        in_hbm(part),
        in_vmem(next_q),
        in_vmem(next_part),
        in_vmem(stat_held),
        own[1],
        pass_on(own[1], done),
        attended,
    )
    operands = []
    for n, m in enumerate(far):
        operands += [in_vmem(staged[2 * n]), in_vmem(staged[2 * n + 1]), own[m], pass_on(own[m], done)]
    attended = pl.pallas_call(
        functools.partial(attend_last, chips),
        out_shape=result,
        in_specs=[vmem] * (1 + len(operands)) + [hbm],
        out_specs=hbm,
        scratch_shapes=[held(len(far)), many((len(far), local))],
        input_output_aliases={1 + len(operands): 0},
        compiler_params=params(12),
        cost_estimate=small,
        name="attend_last",
    )(in_vmem(stat_held), *operands, attended)
    child_share = child_share.reshape(local)
    return (attended, child_share)


def solution(mesh):
    in_specs = (
        P(("prompts", "beam"), None, None),
        P(("prompts", "beam"), None, None),
        P(("prompts", "beam"), None, None),
        P(("prompts", "beam"), None, None, None),
        P(("prompts", "beam"), None),
        P(),
        P("prompts"),
    )
    out_specs = (P(("prompts", "beam"), None, None), P(("prompts", "beam")))
    return jax.shard_map(body, mesh=mesh, in_specs=in_specs, out_specs=out_specs, check_vma=False)
```

```python
import functools
import math

import jax
import jax.numpy as jnp
from jax import lax
from jax.experimental import pallas as pl
from jax.experimental.pallas import tpu as pltpu
from jax.sharding import PartitionSpec as P

HEAD = 128
KEEP = 2
MARK = 16
LIMIT = 100.0
LOG2E = math.log2(math.e)
MIB = 1 << 20
NT = (((1,), (1,)), ((), ()))
NN = (((1,), (0,)), ((), ()))


def mm(a, b, dims=NN):
    return lax.dot_general(a, b, dims, preferred_element_type=jnp.float32)


def kept_pair(parents, base, local):
    own = (parents >= base) & (parents < base + local)
    first = jnp.min(jnp.where(own, parents - base, local))
    last = jnp.max(jnp.where(own, parents - base, -1))
    return first, last


def pack(parents_hbm, kv_hbm, last_hbm, value_hbm, out_ref, parents_ref, held_ref, last_ref, value_ref, piece_ref, *sems):
    local, _, step, width = kv_hbm.shape
    heads = width // HEAD
    kv_sems, sems, out_sems = sems
    small = [(parents_hbm, parents_ref), (last_hbm, last_ref), (value_hbm, value_ref)]
    small = [pltpu.make_async_copy(a, to, sems.at[n]) for n, (a, to) in enumerate(small)]
    copies = [pltpu.make_async_copy(kv_hbm.at[i], held_ref.at[i], kv_sems.at[i]) for i in range(local)]
    for copy in small + copies:
        copy.start()
    small[0].wait()
    kept = kept_pair(parents_ref[...], lax.axis_index("beam") * local, local)
    small[1].wait()
    small[2].wait()
    hidden = last_ref[...].astype(jnp.float32)
    square = jnp.mean(hidden * hidden, axis=-1, keepdims=True)
    normed = hidden * lax.rsqrt(square + 1e-05)
    reward = jax.nn.sigmoid(jnp.sum(normed * value_ref[...], axis=-1, keepdims=True))
    row = lax.broadcasted_iota(jnp.int32, reward.shape, 0)
    marks = [jnp.sum(jnp.where(row == k, reward, 0.0), axis=0, keepdims=True) for k in kept]
    tile = lax.broadcasted_iota(jnp.int32, (MARK, HEAD), 0)
    tile = jnp.where(tile < MARK // 2, marks[0], marks[1]).astype(jnp.bfloat16)
    for copy in copies:
        copy.wait()
    sends = []
    for f in range(heads):
        for r, k in enumerate(kept):
            for s in range(2):
                start = (r * 2 + s) * step
                piece_ref[f, start : start + step, :] = held_ref[k, s, :, f * HEAD : (f + 1) * HEAD]
        piece_ref[f, KEEP * 2 * step :, :] = tile
        for d in range(f, out_ref.shape[0], heads):
            sends.append(pltpu.make_async_copy(piece_ref.at[f], out_ref.at[d], out_sems.at[d]))
            sends[-1].start()
    for send in sends:
        send.wait()


def pick(chips, ms, item_ref, table_ref, _, *out_refs):
    rows = (table_ref.shape[1] - MARK) // KEEP
    local = out_refs[0].shape[0] // (2 * rows)
    chip = lax.axis_index("beam") % (2 * chips) // 2
    core = lax.axis_index("beam") % 2
    for n, m in enumerate(ms):
        for other in range(2):
            owner = (chip ^ m) * 2 + (core ^ other)
            for i in range(local):
                item = item_ref[owner * local + i]
                start = pl.multiple_of((item % KEEP) * rows, rows)
                to = (other * local + i) * rows
                out_refs[n][to : to + rows, :] = table_ref[item // KEEP, pl.ds(start, rows), :]


def share_rewards(item_ref, table_ref, out_ref):
    children, local = item_ref.shape[0], out_ref.shape[1]
    rows = table_ref.shape[1] - MARK
    mine = lax.axis_index("beam") * local
    upper = lax.broadcasted_iota(jnp.int32, (MARK, HEAD), 0) < MARK // 2
    lane = lax.broadcasted_iota(jnp.int32, (1, HEAD), 1)

    def reward(child):
        item = item_ref[child]
        tile = table_ref[item // KEEP, rows:, :].astype(jnp.float32)
        tile = jnp.where(upper == (item % KEEP == 0), tile, 0.0)
        return tile[:1, :] + tile[MARK // 2 : MARK // 2 + 1, :]

    total = jnp.zeros((1, HEAD), jnp.float32)
    for child in range(children):
        total = total + reward(child)
    picked = jnp.zeros((1, HEAD), jnp.float32)
    for i in range(local):
        picked = jnp.where(lane == i, reward(mine + i), picked)
    out_ref[...] = (children * picked / total)[:, :local]


def attend_new(q_ref, k_ref, v_ref, out_ref, stat_ref, sums_ref, tops_ref):
    new = q_ref.shape[1]
    half = new // 2
    heads = k_ref.shape[2] // HEAD
    group = q_ref.shape[2] // k_ref.shape[2]
    count = heads * group
    scale = HEAD**-0.5 * LOG2E
    ones = jnp.ones((new, HEAD), jnp.bfloat16)
    lane = lax.broadcasted_iota(jnp.int32, (half, HEAD), 1)
    row = lax.broadcasted_iota(jnp.int32, (half, half), 0)
    column = lax.broadcasted_iota(jnp.int32, (half, half), 1)
    hidden = jnp.concatenate([jnp.where(column <= row, 0.0, -jnp.inf)] * group, axis=0)
    sums_ref[...] = jnp.ones_like(sums_ref)
    tops_ref[...] = jnp.zeros_like(tops_ref)

    def block(f, shifted):
        lanes = lambda n: pl.ds(pl.multiple_of(n * HEAD, HEAD), HEAD)
        keys = k_ref[0, :, lanes(f)]
        values = jnp.concatenate([v_ref[0, :, lanes(f)], ones], axis=1)
        columns = [lanes(f * group + h) for h in range(group)]
        most = None
        for r in range(2):
            seen = (r + 1) * half
            rows = slice(r * half, (r + 1) * half)
            query = jnp.concatenate([q_ref[0, rows, c] for c in columns], axis=0)
            logits = mm(query, keys[:seen], NT) * scale
            blocks = [logits[:, n * half : (n + 1) * half] for n in range(r + 1)]
            if not shifted:
                for a in blocks:
                    size = jnp.max(jnp.abs(a).reshape(-1, 8, half), axis=0)
                    most = size if most is None else jnp.maximum(most, size)
            blocks[r] = blocks[r] + hidden
            if shifted:
                top = functools.reduce(jnp.maximum, [jnp.max(a, axis=1, keepdims=True) for a in blocks])
                top = top.astype(jnp.bfloat16).astype(jnp.float32)
                blocks = [a - top for a in blocks]
            weights = jnp.concatenate([jnp.exp2(a).astype(jnp.bfloat16) for a in blocks], axis=1)
            both = mm(weights, values[:seen])
            for h in range(group):
                s = slice(h * half, (h + 1) * half)
                out_ref[0, rows, columns[h]] = both[s, :HEAD].astype(jnp.bfloat16)
                here = lane == f * group + h
                sums_ref[rows, :] = jnp.where(here, both[s, HEAD:], sums_ref[rows, :])
                if shifted:
                    tops_ref[rows, :] = jnp.where(here, top[s], tops_ref[rows, :])
        return most

    most = functools.reduce(jnp.maximum, [block(f, False) for f in range(heads)])

    @pl.when(jnp.max(most) > LIMIT)
    def _():
        lax.fori_loop(0, heads, lambda f, c: (block(f, True), c)[1], 0)

    sums = sums_ref[...]
    high = sums.astype(jnp.bfloat16).astype(jnp.float32)
    rest = pltpu.roll(sums - high, count, 1)
    tops = pltpu.roll(tops_ref[...], 2 * count, 1)
    lane = lax.broadcasted_iota(jnp.int32, (new, HEAD), 1)
    stat = jnp.where(lane < count, high, jnp.where(lane < 2 * count, rest, jnp.where(lane < 3 * count, tops, 0.0)))
    stat_ref[0] = stat.astype(jnp.bfloat16)


def block_pair(a):
    zero = jnp.zeros_like(a)
    return jnp.concatenate([jnp.concatenate([a, zero], axis=1), jnp.concatenate([zero, a], axis=1)], axis=0)


def forward(*refs):
    *sent_refs, _, out_ref = refs
    rows = out_ref.shape[0] // len(sent_refs)
    for n, sent_ref in enumerate(sent_refs):
        out_ref[n * rows : (n + 1) * rows, :] = sent_ref[rows:, :]


class Block:
    def __init__(self, q_ref, part_ref, stat_ref, own_ref, other_ref, out_ref, count, place, i, f):
        new, width = q_ref.shape[1:]
        rows = own_ref.shape[0] // (2 * q_ref.shape[0])
        self.step = rows // 2
        pairs = width // (2 * HEAD)
        core = lax.axis_index("beam") % 2
        here = pl.ds(pl.multiple_of(i * rows, rows), rows)
        self.piece = jnp.where(f == core, own_ref[here, :], other_ref[here, :])
        group = [f * (pairs // 2) + p for p in range(pairs // 2)]
        self.columns = [pl.ds(pl.multiple_of(p * 2 * HEAD, 2 * HEAD), 2 * HEAD) for p in group]
        self.heads = [(place * pairs + p) * 2 for p in group]
        self.q_ref, self.part_ref, self.stat_ref, self.out_ref = q_ref, part_ref, stat_ref, out_ref
        self.i, self.count, self.new = i, count, new

    def logits(self):
        keys = block_pair(self.piece[: self.step])
        queries = jnp.concatenate([self.q_ref[self.i, :, c] for c in self.columns], axis=0)
        return mm(queries, keys, NT) * (HEAD**-0.5 * LOG2E)

    def tail(self):
        lane = lax.broadcasted_iota(jnp.int32, (self.new, HEAD), 1)
        pair_of_lane = jnp.where(lane < 2 * self.count, lane % self.count // 2 * 2, -1)
        stat = self.stat_ref[self.i]
        sums = jnp.concatenate([jnp.where(pair_of_lane == h, stat, jnp.zeros_like(stat)) for h in self.heads], axis=0)
        part = jnp.concatenate([self.part_ref[self.i, :, c] for c in self.columns], axis=0).astype(jnp.float32)
        values = block_pair(self.piece[self.step :])
        ones = block_pair(jnp.ones((self.step, HEAD), jnp.bfloat16))
        odd = lax.broadcasted_iota(jnp.int32, (HEAD, 2 * HEAD), 0) % 2
        spread = (odd == lax.broadcasted_iota(jnp.int32, (HEAD, 2 * HEAD), 1) // HEAD).astype(jnp.bfloat16)
        return values, ones, spread, sums, part

    def store(self, added, total):
        result = (added * pltpu.reciprocal(total, approx=True)).astype(jnp.bfloat16)
        for n, c in enumerate(self.columns):
            self.out_ref[self.i, :, c] = result[n * self.new : (n + 1) * self.new]

    def weigh(self):
        logits = self.logits()
        return jnp.exp2(logits).astype(jnp.bfloat16), jnp.max(logits.reshape(-1, 8, HEAD), axis=0)

    def finish(self, weights):
        part = jnp.concatenate([self.part_ref[self.i, :, c] for c in self.columns], axis=0).astype(jnp.float32)
        added = mm(weights, block_pair(self.piece[self.step :]))
        lane = lax.broadcasted_iota(jnp.int32, (self.new, HEAD), 1)
        low = lax.broadcasted_iota(jnp.int32, weights.shape, 1) < self.step
        stat = self.stat_ref[self.i].astype(jnp.float32)
        here = jnp.where(lane < 2 * self.count, lane % self.count, -1)
        wide = weights.astype(jnp.float32)
        totals = []
        for n, k in enumerate((low, ~low)):
            sums = jnp.concatenate([jnp.where(here == h + n, stat, 0.0) for h in self.heads], axis=0)
            total = jnp.sum(jnp.where(k, wide, 0.0) + sums, axis=1, keepdims=True)
            totals.append(jnp.broadcast_to(pltpu.reciprocal(total, approx=True), low.shape))
        result = ((part + added) * jnp.concatenate(totals, axis=1)).astype(jnp.bfloat16)
        for n, c in enumerate(self.columns):
            self.out_ref[self.i, :, c] = result[n * self.new : (n + 1) * self.new]

    def shifted(self):
        logits = self.logits()
        low = lax.broadcasted_iota(jnp.int32, logits.shape, 1) < self.step
        lane = lax.broadcasted_iota(jnp.int32, (self.new, HEAD), 1) - 2 * self.count
        stat = self.stat_ref[self.i].astype(jnp.float32)
        shift = lambda h: jnp.sum(jnp.where(lane == h, stat, 0.0), axis=1, keepdims=True)
        shifts = [jnp.concatenate([shift(h + n) for h in self.heads], axis=0) for n in range(2)]
        logits = logits - jnp.where(low, shifts[0], shifts[1])
        tops = [jnp.maximum(jnp.max(jnp.where(k, logits, 0.0), axis=1, keepdims=True), 0.0) for k in (low, ~low)]
        weights = jnp.exp2(logits - jnp.where(low, tops[0], tops[1])).astype(jnp.bfloat16)
        rest = jnp.concatenate([jnp.broadcast_to(jnp.exp2(-t), low.shape) for t in tops], axis=1)
        values, ones, spread, sums, part = self.tail()
        self.store(part * rest + mm(weights, values), mm(weights, ones) + mm(sums, spread) * rest)


def attend_blocks(works, stat_ref, held_ref, out_ref, sems, ready):
    local, _, width = works[0][0].shape
    count = out_ref.shape[2] // HEAD

    def block(n, i, f):
        q_ref, part_ref, own_ref, other_ref, place = works[n]
        return Block(q_ref, part_ref, stat_ref, own_ref, other_ref, held_ref.at[n], count, place, i, f)

    def send(n, i):
        lanes = pl.ds(pl.multiple_of(works[n][4] * width, width), width)
        return pltpu.make_async_copy(held_ref.at[n, i], out_ref.at[i, :, lanes], sems.at[n, i])

    lane = lax.broadcasted_iota(jnp.int32, stat_ref.shape[1:], 1)

    def work(n, i, carry):
        most, weights = carry
        later, top = block(n, i, 1).weigh()
        block(n, i, 0).finish(weights)
        most = jnp.maximum(most, top)
        following = jnp.minimum(i + 1, local - 1)
        ready(following, i + 1 < local)
        weights, top = block(n, following, 0).weigh()
        block(n, i, 1).finish(later)
        send(n, i).start()
        return jnp.maximum(most, top), weights

    def moved(i, most):
        tops = jnp.where(lane >= 2 * count, stat_ref[i].astype(jnp.float32), 0.0)
        tops = jnp.where(tops == 0.0, -jnp.inf, jnp.inf)
        return jnp.maximum(most, jnp.max(tops.reshape(-1, 8, HEAD), axis=0))

    most = jnp.full((8, HEAD), -jnp.inf, jnp.float32)
    ready(0, True)
    for n in range(len(works)):
        weights, top = block(n, 0, 0).weigh()
        most, _ = lax.fori_loop(0, local, functools.partial(work, n), (jnp.maximum(most, top), weights))
    most = lax.fori_loop(0, local, moved, most)
    every = [(n, i) for n in range(len(works)) for i in range(local)]
    for n, i in every:
        send(n, i).wait()

    @pl.when(jnp.max(most) > LIMIT)
    def _():
        for n in range(len(works)):
            lax.fori_loop(0, 2 * local, lambda t, c: (block(n, t // 2, t % 2).shifted(), c)[1], 0)
        for n, i in every:
            send(n, i).start()
        for n, i in every:
            send(n, i).wait()


def stage(q_ref, part_ref, m, i, to_q, to_part, sems, chips):
    width = to_q.shape[2]
    place = lax.axis_index("beam") % (2 * chips) // 2 ^ m
    lanes = pl.ds(pl.multiple_of(place * width, width), width)
    pairs = ((q_ref, to_q), (part_ref, to_part))
    return [pltpu.make_async_copy(a.at[i, :, lanes], to.at[i], sems.at[k, i]) for k, (a, to) in enumerate(pairs)]


def attend_first(chips, item_ref, table_ref, q_ref, part_ref, stat_ref, own_ref, other_ref, *refs):
    out_ref, share_ref, next_q, next_part, stat_out, token_ref = refs[:6]
    items, held_q, held_part, held, sems, next_sems, stat_sem, item_sem, out_sems = refs[6:]
    local = held_q.shape[0]
    chip = lax.axis_index("beam") % (2 * chips) // 2
    mine = lambda i: stage(q_ref, part_ref, 0, i, held_q, held_part, sems, chips)
    following = lambda i: stage(q_ref, part_ref, 1, i, next_q, next_part, next_sems, chips)
    stat_copy = pltpu.make_async_copy(stat_ref, stat_out, stat_sem)
    stat_copy.start()
    item_copy = pltpu.make_async_copy(item_ref, items, item_sem)
    item_copy.start()
    for i in range(local):
        for copy in mine(i):
            copy.start()
    token_ref[...] = jnp.zeros_like(token_ref)
    item_copy.wait()
    share_rewards(items, table_ref, share_ref)

    def ready(i, due):
        @pl.when(due)
        def _():
            for copy in mine(i):
                copy.wait()
            for copy in following(i):
                copy.start()

    stat_copy.wait()
    attend_blocks([(held_q, held_part, own_ref, other_ref, chip)], stat_out, held, out_ref, out_sems, ready)
    for i in range(local):
        for copy in following(i):
            copy.wait()


def attend_second(chips, q_ref, part_ref, next_q, next_part, stat_ref, own_ref, other_ref, _, *refs):
    out_ref, token_ref, *later = refs[: 2 + 2 * (chips - 2)]
    held, sems, next_sems = refs[2 + 2 * (chips - 2) :]
    local = held.shape[1]
    chip = lax.axis_index("beam") % (2 * chips) // 2

    def staged():
        for n, m in enumerate(range(2, chips)):
            for i in range(local):
                yield from stage(q_ref, part_ref, m, i, later[2 * n], later[2 * n + 1], next_sems.at[n], chips)

    for copy in staged():
        copy.start()
    token_ref[...] = jnp.zeros_like(token_ref)
    works = [(next_q, next_part, own_ref, other_ref, chip ^ 1)]
    attend_blocks(works, stat_ref, held, out_ref, sems, lambda i, due: None)
    for copy in staged():
        copy.wait()


def attend_last(chips, stat_ref, *refs):
    *operands, other_ref, _, out_ref, held, sems = refs
    count = other_ref.shape[0] // (chips - 2)
    chip = lax.axis_index("beam") % (2 * chips) // 2
    works = [
        (*operands[3 * n : 3 * n + 3], other_ref.at[pl.ds(n * count, count), :], chip ^ m)
        for n, m in enumerate(range(2, chips))
    ]
    attend_blocks(works, stat_ref, held, out_ref, sems, lambda i, due: None)


def params(mib):
    return pltpu.CompilerParams(vmem_limit_bytes=mib * MIB)


def swap(a, distance):
    count = lax.axis_size("beam")
    return lax.ppermute(a, "beam", [(i, i ^ distance) for i in range(count)])


def body(queries, new_keys, new_values, step_kv, prm_last, value_head, parents):
    beam_count = lax.axis_size("beam")
    group_index = lax.axis_index("beam")
    local, new, width = queries.shape
    children = parents.shape[0]
    step = step_kv.shape[2]
    kv_width = step_kv.shape[3]
    heads = kv_width // HEAD
    chips = heads // 2
    vmem = pl.BlockSpec(memory_space=pltpu.VMEM)
    smem = pl.BlockSpec(memory_space=pltpu.SMEM)
    hbm = pl.BlockSpec(memory_space=pltpu.HBM)
    bf16 = jnp.bfloat16

    rows = 2 * step
    in_hbm = lambda a: pltpu.with_memory_space_constraint(a, pltpu.HBM)
    in_vmem = lambda a: pltpu.with_memory_space_constraint(a, pltpu.VMEM)
    message = KEEP * rows + MARK
    packed = pl.pallas_call(
        pack,
        out_shape=jax.ShapeDtypeStruct((beam_count, message, HEAD), bf16),
        in_specs=[hbm] * 4,
        out_specs=hbm,
        scratch_shapes=[
            pltpu.VMEM((1, children), jnp.int32),
            pltpu.VMEM((local, 2, step, kv_width), bf16),
            pltpu.VMEM(prm_last.shape, bf16),
            pltpu.VMEM((1, value_head.shape[0]), jnp.float32),
            pltpu.VMEM((heads, message, HEAD), bf16),
            pltpu.SemaphoreType.DMA((local,)),
            pltpu.SemaphoreType.DMA((3,)),
            pltpu.SemaphoreType.DMA((beam_count,)),
        ],
        name="pack",
    )(in_hbm(parents.reshape(1, children)), in_hbm(step_kv), in_hbm(prm_last), in_hbm(value_head.reshape(1, -1)))
    table = lax.all_to_all(packed, "beam", 0, 0)

    cost = lambda f, t, b: pl.CostEstimate(flops=f, transcendentals=t, bytes_accessed=b)
    small = cost(1024, 0, 1024)
    whole = lambda w: pl.BlockSpec((1, new, w), lambda i: (i, 0, 0))
    part, stat = pl.pallas_call(
        attend_new,
        grid=(local,),
        out_shape=[
            jax.ShapeDtypeStruct((local, new, width), bf16),
            jax.ShapeDtypeStruct((local, new, HEAD), bf16),
        ],
        in_specs=[whole(width), whole(kv_width), whole(kv_width)],
        out_specs=[whole(width), whole(HEAD)],
        scratch_shapes=[pltpu.VMEM((new, HEAD), jnp.float32)] * 2,
        compiler_params=params(56),
        cost_estimate=cost(4 * local * new * new * width, local * new * new * width // HEAD, 6 * local * new * width),
        name="attend_new",
    )(queries, new_keys, new_values)

    owner = parents // local
    earlier = (owner[:, None] == owner[None, :]) & (parents[None, :] < parents[:, None])
    item = owner * KEEP + jnp.any(earlier, axis=1).astype(jnp.int32)
    near = lax.dynamic_slice_in_dim(item, group_index // heads * (heads * local), heads * local)
    anywhere = pl.BlockSpec(memory_space=pl.ANY)

    def picked(ms, after):
        return pl.pallas_call(
            functools.partial(pick, chips, ms),
            out_shape=[jax.ShapeDtypeStruct((2 * local * rows, HEAD), bf16)] * len(ms),
            in_specs=[smem, vmem, anywhere],
            out_specs=[vmem] * len(ms),
            compiler_params=params(4),
            cost_estimate=small,
            name="pick",
        )(near, table, after)

    def pass_on(sent, after):
        passed = pl.pallas_call(
            forward,
            out_shape=jax.ShapeDtypeStruct((len(sent) * local * rows, HEAD), bf16),
            in_specs=[vmem] * len(sent) + [anywhere],
            out_specs=vmem,
            compiler_params=params(2),
            cost_estimate=small,
            name="forward",
        )(*sent, after)
        return swap(passed, 1)

    far = tuple(range(2, chips))
    pieces = picked(range(chips), in_hbm(stat))
    own = [pieces[0]] + [swap(pieces[m], 2 * m) for m in range(1, chips)]
    wide = width // chips
    result = jax.ShapeDtypeStruct((local, new, width), bf16)
    token = jax.ShapeDtypeStruct((8, HEAD), jnp.float32)
    later = pltpu.VMEM((local, new, wide), bf16)
    held = lambda n: pltpu.VMEM((n, local, new, wide), bf16)
    many = pltpu.SemaphoreType.DMA
    attended, child_share, next_q, next_part, stat_held, done = pl.pallas_call(
        functools.partial(attend_first, chips),
        out_shape=[
            result,
            jax.ShapeDtypeStruct((1, local), jnp.float32),
            later,
            later,
            pltpu.VMEM(stat.shape, bf16),
            token,
        ],
        in_specs=[hbm, vmem, hbm, hbm, hbm, vmem, vmem],
        out_specs=[hbm] + [vmem] * 5,
        scratch_shapes=[pltpu.SMEM((children,), jnp.int32)]
        + [later] * 2
        + [held(1), many((2, local)), many((2, local)), many, many, many((1, local))],
        compiler_params=params(16),
        cost_estimate=small,
        name="attend_first",
    )(in_hbm(item), table, in_hbm(queries), in_hbm(part), in_hbm(stat), own[0], pass_on(own[:1], near))
    attended, done, *staged = pl.pallas_call(
        functools.partial(attend_second, chips),
        out_shape=[result, token] + [later] * (2 * len(far)),
        in_specs=[hbm, hbm] + [vmem] * 5 + [hbm],
        out_specs=[hbm, vmem] + [vmem] * (2 * len(far)),
        scratch_shapes=[held(1), many((1, local)), many((len(far), 2, local))],
        input_output_aliases={7: 0},
        compiler_params=params(12),
        cost_estimate=small,
        name="attend_second",
    )(
        in_hbm(queries),
        in_hbm(part),
        in_vmem(next_q),
        in_vmem(next_part),
        in_vmem(stat_held),
        own[1],
        pass_on(own[1:2], done),
        attended,
    )
    operands = []
    for n, m in enumerate(far):
        operands += [in_vmem(staged[2 * n]), in_vmem(staged[2 * n + 1]), own[m]]
    operands.append(pass_on(own[2:], done))
    attended = pl.pallas_call(
        functools.partial(attend_last, chips),
        out_shape=result,
        in_specs=[vmem] * (1 + len(operands)) + [hbm],
        out_specs=hbm,
        scratch_shapes=[held(len(far)), many((len(far), local))],
        input_output_aliases={1 + len(operands): 0},
        compiler_params=params(12),
        cost_estimate=small,
        name="attend_last",
    )(in_vmem(stat_held), *operands, attended)
    child_share = child_share.reshape(local)
    return (attended, child_share)


def solution(mesh):
    in_specs = (
        P(("prompts", "beam"), None, None),
        P(("prompts", "beam"), None, None),
        P(("prompts", "beam"), None, None),
        P(("prompts", "beam"), None, None, None),
        P(("prompts", "beam"), None),
        P(),
        P("prompts"),
    )
    out_specs = (P(("prompts", "beam"), None, None), P(("prompts", "beam")))
    return jax.shard_map(body, mesh=mesh, in_specs=in_specs, out_specs=out_specs, check_vma=False)
```

```python
import functools
import math

import jax
import jax.numpy as jnp
from jax import lax
from jax.experimental import pallas as pl
from jax.experimental.pallas import tpu as pltpu
from jax.sharding import PartitionSpec as P

HEAD = 128
KEEP = 2
MARK = 16
LIMIT = 100.0
SECOND = 1
LAST = (2, 3)
LOG2E = math.log2(math.e)
MIB = 1 << 20
NT = (((1,), (1,)), ((), ()))
NN = (((1,), (0,)), ((), ()))


def mm(a, b, dims=NN):
    return lax.dot_general(a, b, dims, preferred_element_type=jnp.float32)


def kept_pair(parents, base, local):
    own = (parents >= base) & (parents < base + local)
    first = jnp.min(jnp.where(own, parents - base, local))
    last = jnp.max(jnp.where(own, parents - base, -1))
    return first, last


def pack(parents_hbm, kv_hbm, last_hbm, value_hbm, out_ref, parents_ref, held_ref, last_ref, value_ref, piece_ref, *sems):
    local, _, step, width = kv_hbm.shape
    heads = width // HEAD
    kv_sems, sems, out_sems = sems
    small = [(parents_hbm, parents_ref), (last_hbm, last_ref), (value_hbm, value_ref)]
    small = [pltpu.make_async_copy(a, to, sems.at[n]) for n, (a, to) in enumerate(small)]
    copies = [pltpu.make_async_copy(kv_hbm.at[i], held_ref.at[i], kv_sems.at[i]) for i in range(local)]
    for copy in small + copies:
        copy.start()
    small[0].wait()
    kept = kept_pair(parents_ref[...], lax.axis_index("beam") * local, local)
    small[1].wait()
    small[2].wait()
    hidden = last_ref[...].astype(jnp.float32)
    square = jnp.mean(hidden * hidden, axis=-1, keepdims=True)
    normed = hidden * lax.rsqrt(square + 1e-05)
    reward = jax.nn.sigmoid(jnp.sum(normed * value_ref[...], axis=-1, keepdims=True))
    row = lax.broadcasted_iota(jnp.int32, reward.shape, 0)
    marks = [jnp.sum(jnp.where(row == k, reward, 0.0), axis=0, keepdims=True) for k in kept]
    tile = lax.broadcasted_iota(jnp.int32, (MARK, HEAD), 0)
    tile = jnp.where(tile < MARK // 2, marks[0], marks[1]).astype(jnp.bfloat16)
    for copy in copies:
        copy.wait()
    sends = []
    for f in range(heads):
        for r, k in enumerate(kept):
            for s in range(2):
                start = (r * 2 + s) * step
                piece_ref[f, start : start + step, :] = held_ref[k, s, :, f * HEAD : (f + 1) * HEAD]
        piece_ref[f, KEEP * 2 * step :, :] = tile
        for d in range(f, out_ref.shape[0], heads):
            sends.append(pltpu.make_async_copy(piece_ref.at[f], out_ref.at[d], out_sems.at[d]))
            sends[-1].start()
    for send in sends:
        send.wait()


def pick(chips, ms, item_ref, table_ref, _, *out_refs):
    rows = (table_ref.shape[1] - MARK) // KEEP
    local = out_refs[0].shape[0] // (2 * rows)
    chip = lax.axis_index("beam") % (2 * chips) // 2
    core = lax.axis_index("beam") % 2
    for n, m in enumerate(ms):
        for other in range(2):
            owner = (chip ^ m) * 2 + (core ^ other)
            for i in range(local):
                item = item_ref[owner * local + i]
                start = pl.multiple_of((item % KEEP) * rows, rows)
                to = (other * local + i) * rows
                out_refs[n][to : to + rows, :] = table_ref[item // KEEP, pl.ds(start, rows), :]


def share_rewards(item_ref, table_ref, out_ref):
    children, local = item_ref.shape[0], out_ref.shape[1]
    rows = table_ref.shape[1] - MARK
    mine = lax.axis_index("beam") * local
    upper = lax.broadcasted_iota(jnp.int32, (MARK, HEAD), 0) < MARK // 2
    lane = lax.broadcasted_iota(jnp.int32, (1, HEAD), 1)

    def reward(child):
        item = item_ref[child]
        tile = table_ref[item // KEEP, rows:, :].astype(jnp.float32)
        tile = jnp.where(upper == (item % KEEP == 0), tile, 0.0)
        return tile[:1, :] + tile[MARK // 2 : MARK // 2 + 1, :]

    total = jnp.zeros((1, HEAD), jnp.float32)
    for child in range(children):
        total = total + reward(child)
    picked = jnp.zeros((1, HEAD), jnp.float32)
    for i in range(local):
        picked = jnp.where(lane == i, reward(mine + i), picked)
    out_ref[...] = (children * picked / total)[:, :local]


def attend_new(q_ref, k_ref, v_ref, out_ref, stat_ref, sums_ref, tops_ref):
    new = q_ref.shape[1]
    half = new // 2
    heads = k_ref.shape[2] // HEAD
    group = q_ref.shape[2] // k_ref.shape[2]
    count = heads * group
    scale = HEAD**-0.5 * LOG2E
    ones = jnp.ones((new, HEAD), jnp.bfloat16)
    lane = lax.broadcasted_iota(jnp.int32, (half, HEAD), 1)
    row = lax.broadcasted_iota(jnp.int32, (half, half), 0)
    column = lax.broadcasted_iota(jnp.int32, (half, half), 1)
    hidden = jnp.concatenate([jnp.where(column <= row, 0.0, -jnp.inf)] * group, axis=0)
    sums_ref[...] = jnp.ones_like(sums_ref)
    tops_ref[...] = jnp.zeros_like(tops_ref)

    def block(f, shifted):
        lanes = lambda n: pl.ds(pl.multiple_of(n * HEAD, HEAD), HEAD)
        keys = k_ref[0, :, lanes(f)]
        values = jnp.concatenate([v_ref[0, :, lanes(f)], ones], axis=1)
        columns = [lanes(f * group + h) for h in range(group)]
        most = None
        for r in range(2):
            seen = (r + 1) * half
            rows = slice(r * half, (r + 1) * half)
            query = jnp.concatenate([q_ref[0, rows, c] for c in columns], axis=0)
            logits = mm(query, keys[:seen], NT) * scale
            blocks = [logits[:, n * half : (n + 1) * half] for n in range(r + 1)]
            if not shifted:
                for a in blocks:
                    size = jnp.max(jnp.abs(a).reshape(-1, 8, half), axis=0)
                    most = size if most is None else jnp.maximum(most, size)
            blocks[r] = blocks[r] + hidden
            if shifted:
                top = functools.reduce(jnp.maximum, [jnp.max(a, axis=1, keepdims=True) for a in blocks])
                top = top.astype(jnp.bfloat16).astype(jnp.float32)
                blocks = [a - top for a in blocks]
            weights = jnp.concatenate([jnp.exp2(a).astype(jnp.bfloat16) for a in blocks], axis=1)
            both = mm(weights, values[:seen])
            for h in range(group):
                s = slice(h * half, (h + 1) * half)
                out_ref[0, rows, columns[h]] = both[s, :HEAD].astype(jnp.bfloat16)
                here = lane == f * group + h
                sums_ref[rows, :] = jnp.where(here, both[s, HEAD:], sums_ref[rows, :])
                if shifted:
                    tops_ref[rows, :] = jnp.where(here, top[s], tops_ref[rows, :])
        return most

    most = functools.reduce(jnp.maximum, [block(f, False) for f in range(heads)])

    @pl.when(jnp.max(most) > LIMIT)
    def _():
        lax.fori_loop(0, heads, lambda f, c: (block(f, True), c)[1], 0)

    sums = sums_ref[...]
    high = sums.astype(jnp.bfloat16).astype(jnp.float32)
    rest = pltpu.roll(sums - high, count, 1)
    tops = pltpu.roll(tops_ref[...], 2 * count, 1)
    lane = lax.broadcasted_iota(jnp.int32, (new, HEAD), 1)
    stat = jnp.where(lane < count, high, jnp.where(lane < 2 * count, rest, jnp.where(lane < 3 * count, tops, 0.0)))
    stat_ref[0] = stat.astype(jnp.bfloat16)


def block_pair(a):
    zero = jnp.zeros_like(a)
    return jnp.concatenate([jnp.concatenate([a, zero], axis=1), jnp.concatenate([zero, a], axis=1)], axis=0)


def forward(*refs):
    *sent_refs, _, out_ref = refs
    rows = out_ref.shape[0] // len(sent_refs)
    for n, sent_ref in enumerate(sent_refs):
        out_ref[n * rows : (n + 1) * rows, :] = sent_ref[rows:, :]


class Block:
    def __init__(self, q_ref, part_ref, stat_ref, own_ref, other_ref, out_ref, count, place, i, f):
        new, width = q_ref.shape[1:]
        rows = own_ref.shape[0] // (2 * q_ref.shape[0])
        self.step = rows // 2
        pairs = width // (2 * HEAD)
        core = lax.axis_index("beam") % 2
        here = pl.ds(pl.multiple_of(i * rows, rows), rows)
        self.piece = jnp.where(f == core, own_ref[here, :], other_ref[here, :])
        group = [f * (pairs // 2) + p for p in range(pairs // 2)]
        self.columns = [pl.ds(pl.multiple_of(p * 2 * HEAD, 2 * HEAD), 2 * HEAD) for p in group]
        self.heads = [(place * pairs + p) * 2 for p in group]
        self.q_ref, self.part_ref, self.stat_ref, self.out_ref = q_ref, part_ref, stat_ref, out_ref
        self.i, self.count, self.new = i, count, new

    def logits(self):
        keys = block_pair(self.piece[: self.step])
        queries = jnp.concatenate([self.q_ref[self.i, :, c] for c in self.columns], axis=0)
        return mm(queries, keys, NT) * (HEAD**-0.5 * LOG2E)

    def tail(self):
        lane = lax.broadcasted_iota(jnp.int32, (self.new, HEAD), 1)
        pair_of_lane = jnp.where(lane < 2 * self.count, lane % self.count // 2 * 2, -1)
        stat = self.stat_ref[self.i]
        sums = jnp.concatenate([jnp.where(pair_of_lane == h, stat, jnp.zeros_like(stat)) for h in self.heads], axis=0)
        part = jnp.concatenate([self.part_ref[self.i, :, c] for c in self.columns], axis=0).astype(jnp.float32)
        values = block_pair(self.piece[self.step :])
        ones = block_pair(jnp.ones((self.step, HEAD), jnp.bfloat16))
        odd = lax.broadcasted_iota(jnp.int32, (HEAD, 2 * HEAD), 0) % 2
        spread = (odd == lax.broadcasted_iota(jnp.int32, (HEAD, 2 * HEAD), 1) // HEAD).astype(jnp.bfloat16)
        return values, ones, spread, sums, part

    def store(self, added, total):
        result = (added * pltpu.reciprocal(total, approx=True)).astype(jnp.bfloat16)
        for n, c in enumerate(self.columns):
            self.out_ref[self.i, :, c] = result[n * self.new : (n + 1) * self.new]

    def weigh(self):
        logits = self.logits()
        return jnp.exp2(logits).astype(jnp.bfloat16), jnp.max(logits.reshape(-1, 8, HEAD), axis=0)

    def finish(self, weights):
        part = jnp.concatenate([self.part_ref[self.i, :, c] for c in self.columns], axis=0).astype(jnp.float32)
        added = mm(weights, block_pair(self.piece[self.step :]))
        lane = lax.broadcasted_iota(jnp.int32, (self.new, HEAD), 1)
        low = lax.broadcasted_iota(jnp.int32, weights.shape, 1) < self.step
        stat = self.stat_ref[self.i].astype(jnp.float32)
        here = jnp.where(lane < 2 * self.count, lane % self.count, -1)
        wide = weights.astype(jnp.float32)
        totals = []
        for n, k in enumerate((low, ~low)):
            sums = jnp.concatenate([jnp.where(here == h + n, stat, 0.0) for h in self.heads], axis=0)
            total = jnp.sum(jnp.where(k, wide, 0.0) + sums, axis=1, keepdims=True)
            totals.append(jnp.broadcast_to(pltpu.reciprocal(total, approx=True), low.shape))
        result = ((part + added) * jnp.concatenate(totals, axis=1)).astype(jnp.bfloat16)
        for n, c in enumerate(self.columns):
            self.out_ref[self.i, :, c] = result[n * self.new : (n + 1) * self.new]

    def shifted(self):
        logits = self.logits()
        low = lax.broadcasted_iota(jnp.int32, logits.shape, 1) < self.step
        lane = lax.broadcasted_iota(jnp.int32, (self.new, HEAD), 1) - 2 * self.count
        stat = self.stat_ref[self.i].astype(jnp.float32)
        shift = lambda h: jnp.sum(jnp.where(lane == h, stat, 0.0), axis=1, keepdims=True)
        shifts = [jnp.concatenate([shift(h + n) for h in self.heads], axis=0) for n in range(2)]
        logits = logits - jnp.where(low, shifts[0], shifts[1])
        tops = [jnp.maximum(jnp.max(jnp.where(k, logits, 0.0), axis=1, keepdims=True), 0.0) for k in (low, ~low)]
        weights = jnp.exp2(logits - jnp.where(low, tops[0], tops[1])).astype(jnp.bfloat16)
        rest = jnp.concatenate([jnp.broadcast_to(jnp.exp2(-t), low.shape) for t in tops], axis=1)
        values, ones, spread, sums, part = self.tail()
        self.store(part * rest + mm(weights, values), mm(weights, ones) + mm(sums, spread) * rest)


def attend_blocks(works, stat_ref, held_ref, out_ref, sems, ready=None, rolled=False):
    local, _, width = works[0][0].shape
    count = out_ref.shape[2] // HEAD

    def block(n, i, f):
        q_ref, part_ref, own_ref, other_ref, place = works[n]
        return Block(q_ref, part_ref, stat_ref, own_ref, other_ref, held_ref.at[n], count, place, i, f)

    def send(n, i):
        lanes = pl.ds(pl.multiple_of(works[n][4] * width, width), width)
        return pltpu.make_async_copy(held_ref.at[n, i], out_ref.at[i, :, lanes], sems.at[n, i])

    lane = lax.broadcasted_iota(jnp.int32, stat_ref.shape[1:], 1)

    def moved(i, most):
        tops = jnp.where(lane >= 2 * count, stat_ref[i].astype(jnp.float32), 0.0)
        tops = jnp.where(tops == 0.0, -jnp.inf, jnp.inf)
        return jnp.maximum(most, jnp.max(tops.reshape(-1, 8, HEAD), axis=0))

    most = jnp.full((8, HEAD), -jnp.inf, jnp.float32)

    def run(order, most):
        held = None
        for t in range(len(order) + 1):
            last, held = held, None
            if t < len(order):
                n, i, f = order[t]
                if ready is not None and f == 0:
                    ready(i)
                held, top = block(n, i, f).weigh()
                most = jnp.maximum(most, top)
            if t > 0:
                n, i, f = order[t - 1]
                block(n, i, f).finish(last)
                if f == 1:
                    send(n, i).start()
        return most

    if rolled:
        most = lax.fori_loop(0, local, lambda i, most: run([(0, i, 0), (0, i, 1)], most), most)
    else:
        most = run([(n, i, f) for n in range(len(works)) for i in range(local) for f in range(2)], most)
    largest = jnp.max(lax.fori_loop(0, local, moved, most))
    every = [(n, i) for n in range(len(works)) for i in range(local)]
    for n, i in every:
        send(n, i).wait()

    @pl.when(largest > LIMIT)
    def _():
        for n in range(len(works)):
            lax.fori_loop(0, 2 * local, lambda t, c: (block(n, t // 2, t % 2).shifted(), c)[1], 0)
        for n, i in every:
            send(n, i).start()
        for n, i in every:
            send(n, i).wait()


def stage(q_ref, part_ref, m, i, to_q, to_part, sems, chips):
    width = to_q.shape[2]
    place = lax.axis_index("beam") % (2 * chips) // 2 ^ m
    lanes = pl.ds(pl.multiple_of(place * width, width), width)
    pairs = ((q_ref, to_q), (part_ref, to_part))
    return [pltpu.make_async_copy(a.at[i, :, lanes], to.at[i], sems.at[k, i]) for k, (a, to) in enumerate(pairs)]


def attend_first(chips, item_ref, table_ref, q_ref, part_ref, stat_ref, own_ref, other_ref, *refs):
    out_ref, share_ref, next_q, next_part, stat_out, token_ref = refs[:6]
    items, held_q, held_part, held, sems, next_sems, stat_sem, item_sem, out_sems = refs[6:]
    local = held_q.shape[0]
    chip = lax.axis_index("beam") % (2 * chips) // 2
    mine = lambda i: stage(q_ref, part_ref, 0, i, held_q, held_part, sems, chips)
    following = lambda i: stage(q_ref, part_ref, SECOND, i, next_q, next_part, next_sems, chips)
    stat_copy = pltpu.make_async_copy(stat_ref, stat_out, stat_sem)
    stat_copy.start()
    item_copy = pltpu.make_async_copy(item_ref, items, item_sem)
    item_copy.start()
    for i in range(local):
        for copy in mine(i):
            copy.start()
    token_ref[...] = jnp.zeros_like(token_ref)
    item_copy.wait()
    share_rewards(items, table_ref, share_ref)

    def ready(i):
        for copy in mine(i):
            copy.wait()
        for copy in following(i):
            copy.start()

    stat_copy.wait()
    attend_blocks([(held_q, held_part, own_ref, other_ref, chip)], stat_out, held, out_ref, out_sems, ready)
    for i in range(local):
        for copy in following(i):
            copy.wait()


def attend_second(chips, q_ref, part_ref, next_q, next_part, stat_ref, own_ref, other_ref, _, *refs):
    out_ref, token_ref, *later = refs[: 2 + 2 * len(LAST)]
    held, sems, next_sems = refs[2 + 2 * len(LAST) :]
    local = held.shape[1]
    chip = lax.axis_index("beam") % (2 * chips) // 2

    def staged():
        for n, m in enumerate(LAST):
            for i in range(local):
                yield from stage(q_ref, part_ref, m, i, later[2 * n], later[2 * n + 1], next_sems.at[n], chips)

    for copy in staged():
        copy.start()
    token_ref[...] = jnp.zeros_like(token_ref)
    works = [(next_q, next_part, own_ref, other_ref, chip ^ SECOND)]
    attend_blocks(works, stat_ref, held, out_ref, sems, rolled=True)
    for copy in staged():
        copy.wait()


def attend_last(chips, stat_ref, *refs):
    *operands, other_ref, _, out_ref, held, sems = refs
    count = other_ref.shape[0] // len(LAST)
    chip = lax.axis_index("beam") % (2 * chips) // 2
    works = [
        (*operands[3 * n : 3 * n + 3], other_ref.at[pl.ds(n * count, count), :], chip ^ m)
        for n, m in enumerate(LAST)
    ]
    attend_blocks(works, stat_ref, held, out_ref, sems)


def params(mib):
    return pltpu.CompilerParams(vmem_limit_bytes=mib * MIB)


def swap(a, distance):
    count = lax.axis_size("beam")
    return lax.ppermute(a, "beam", [(i, i ^ distance) for i in range(count)])


def body(queries, new_keys, new_values, step_kv, prm_last, value_head, parents):
    beam_count = lax.axis_size("beam")
    group_index = lax.axis_index("beam")
    local, new, width = queries.shape
    children = parents.shape[0]
    step = step_kv.shape[2]
    kv_width = step_kv.shape[3]
    heads = kv_width // HEAD
    chips = heads // 2
    vmem = pl.BlockSpec(memory_space=pltpu.VMEM)
    smem = pl.BlockSpec(memory_space=pltpu.SMEM)
    hbm = pl.BlockSpec(memory_space=pltpu.HBM)
    bf16 = jnp.bfloat16

    rows = 2 * step
    in_hbm = lambda a: pltpu.with_memory_space_constraint(a, pltpu.HBM)
    in_vmem = lambda a: pltpu.with_memory_space_constraint(a, pltpu.VMEM)
    message = KEEP * rows + MARK
    packed = pl.pallas_call(
        pack,
        out_shape=jax.ShapeDtypeStruct((beam_count, message, HEAD), bf16),
        in_specs=[hbm] * 4,
        out_specs=hbm,
        scratch_shapes=[
            pltpu.VMEM((1, children), jnp.int32),
            pltpu.VMEM((local, 2, step, kv_width), bf16),
            pltpu.VMEM(prm_last.shape, bf16),
            pltpu.VMEM((1, value_head.shape[0]), jnp.float32),
            pltpu.VMEM((heads, message, HEAD), bf16),
            pltpu.SemaphoreType.DMA((local,)),
            pltpu.SemaphoreType.DMA((3,)),
            pltpu.SemaphoreType.DMA((beam_count,)),
        ],
        name="pack",
    )(in_hbm(parents.reshape(1, children)), in_hbm(step_kv), in_hbm(prm_last), in_hbm(value_head.reshape(1, -1)))
    table = lax.all_to_all(packed, "beam", 0, 0)

    cost = lambda f, t, b: pl.CostEstimate(flops=f, transcendentals=t, bytes_accessed=b)
    small = cost(1024, 0, 1024)
    whole = lambda w: pl.BlockSpec((1, new, w), lambda i: (i, 0, 0))
    part, stat = pl.pallas_call(
        attend_new,
        grid=(local,),
        out_shape=[
            jax.ShapeDtypeStruct((local, new, width), bf16),
            jax.ShapeDtypeStruct((local, new, HEAD), bf16),
        ],
        in_specs=[whole(width), whole(kv_width), whole(kv_width)],
        out_specs=[whole(width), whole(HEAD)],
        scratch_shapes=[pltpu.VMEM((new, HEAD), jnp.float32)] * 2,
        compiler_params=params(56),
        cost_estimate=cost(4 * local * new * new * width, local * new * new * width // HEAD, 6 * local * new * width),
        name="attend_new",
    )(queries, new_keys, new_values)

    owner = parents // local
    earlier = (owner[:, None] == owner[None, :]) & (parents[None, :] < parents[:, None])
    item = owner * KEEP + jnp.any(earlier, axis=1).astype(jnp.int32)
    near = lax.dynamic_slice_in_dim(item, group_index // heads * (heads * local), heads * local)
    anywhere = pl.BlockSpec(memory_space=pl.ANY)

    def picked(ms, after):
        return pl.pallas_call(
            functools.partial(pick, chips, ms),
            out_shape=[jax.ShapeDtypeStruct((2 * local * rows, HEAD), bf16)] * len(ms),
            in_specs=[smem, vmem, anywhere],
            out_specs=[vmem] * len(ms),
            compiler_params=params(4),
            cost_estimate=small,
            name="pick",
        )(near, table, after)

    def pass_on(sent, after):
        passed = pl.pallas_call(
            forward,
            out_shape=jax.ShapeDtypeStruct((len(sent) * local * rows, HEAD), bf16),
            in_specs=[vmem] * len(sent) + [anywhere],
            out_specs=vmem,
            compiler_params=params(2),
            cost_estimate=small,
            name="forward",
        )(*sent, after)
        return swap(passed, 1)

    pieces = picked(range(chips), in_hbm(stat))
    own = [pieces[0]] + [swap(pieces[m], 2 * m) for m in range(1, chips)]
    wide = width // chips
    result = jax.ShapeDtypeStruct((local, new, width), bf16)
    token = jax.ShapeDtypeStruct((8, HEAD), jnp.float32)
    later = pltpu.VMEM((local, new, wide), bf16)
    held = lambda n: pltpu.VMEM((n, local, new, wide), bf16)
    many = pltpu.SemaphoreType.DMA
    attended, child_share, next_q, next_part, stat_held, done = pl.pallas_call(
        functools.partial(attend_first, chips),
        out_shape=[
            result,
            jax.ShapeDtypeStruct((1, local), jnp.float32),
            later,
            later,
            pltpu.VMEM(stat.shape, bf16),
            token,
        ],
        in_specs=[hbm, vmem, hbm, hbm, hbm, vmem, vmem],
        out_specs=[hbm] + [vmem] * 5,
        scratch_shapes=[pltpu.SMEM((children,), jnp.int32)]
        + [later] * 2
        + [held(1), many((2, local)), many((2, local)), many, many, many((1, local))],
        compiler_params=params(16),
        cost_estimate=small,
        name="attend_first",
    )(in_hbm(item), table, in_hbm(queries), in_hbm(part), in_hbm(stat), own[0], pass_on(own[:1], near))
    attended, done, *staged = pl.pallas_call(
        functools.partial(attend_second, chips),
        out_shape=[result, token] + [later] * (2 * len(LAST)),
        in_specs=[hbm, hbm] + [vmem] * 5 + [hbm],
        out_specs=[hbm, vmem] + [vmem] * (2 * len(LAST)),
        scratch_shapes=[held(1), many((1, local)), many((len(LAST), 2, local))],
        input_output_aliases={7: 0},
        compiler_params=params(12),
        cost_estimate=small,
        name="attend_second",
    )(
        in_hbm(queries),
        in_hbm(part),
        in_vmem(next_q),
        in_vmem(next_part),
        in_vmem(stat_held),
        own[SECOND],
        pass_on([own[SECOND]], done),
        attended,
    )
    operands = []
    for n, m in enumerate(LAST):
        operands += [in_vmem(staged[2 * n]), in_vmem(staged[2 * n + 1]), own[m]]
    operands.append(pass_on([own[m] for m in LAST], done))
    attended = pl.pallas_call(
        functools.partial(attend_last, chips),
        out_shape=result,
        in_specs=[vmem] * (1 + len(operands)) + [hbm],
        out_specs=hbm,
        scratch_shapes=[held(len(LAST)), many((len(LAST), local))],
        input_output_aliases={1 + len(operands): 0},
        compiler_params=params(12),
        cost_estimate=small,
        name="attend_last",
    )(in_vmem(stat_held), *operands, attended)
    child_share = child_share.reshape(local)
    return (attended, child_share)


def solution(mesh):
    in_specs = (
        P(("prompts", "beam"), None, None),
        P(("prompts", "beam"), None, None),
        P(("prompts", "beam"), None, None),
        P(("prompts", "beam"), None, None, None),
        P(("prompts", "beam"), None),
        P(),
        P("prompts"),
    )
    out_specs = (P(("prompts", "beam"), None, None), P(("prompts", "beam")))
    return jax.shard_map(body, mesh=mesh, in_specs=in_specs, out_specs=out_specs, check_vma=False)
```

```python
import functools
import math

import jax
import jax.numpy as jnp
from jax import lax
from jax.experimental import pallas as pl
from jax.experimental.pallas import tpu as pltpu
from jax.sharding import PartitionSpec as P

HEAD = 128
KEEP = 2
MARK = 16
LIMIT = 100.0
SECOND = 1
LAST = (2, 3)
LOG2E = math.log2(math.e)
MIB = 1 << 20
NT = (((1,), (1,)), ((), ()))
NN = (((1,), (0,)), ((), ()))


def mm(a, b, dims=NN):
    return lax.dot_general(a, b, dims, preferred_element_type=jnp.float32)


def kept_pair(parents, base, local):
    own = (parents >= base) & (parents < base + local)
    first = jnp.min(jnp.where(own, parents - base, local))
    last = jnp.max(jnp.where(own, parents - base, -1))
    return first, last


def pack(parents_hbm, kv_hbm, last_hbm, value_hbm, out_ref, parents_ref, held_ref, last_ref, value_ref, piece_ref, *sems):
    local, _, step, width = kv_hbm.shape
    heads = width // HEAD
    kv_sems, sems, out_sems = sems
    small = [(parents_hbm, parents_ref), (last_hbm, last_ref), (value_hbm, value_ref)]
    small = [pltpu.make_async_copy(a, to, sems.at[n]) for n, (a, to) in enumerate(small)]
    copies = [pltpu.make_async_copy(kv_hbm.at[i], held_ref.at[i], kv_sems.at[i]) for i in range(local)]
    for copy in small + copies:
        copy.start()
    small[0].wait()
    kept = kept_pair(parents_ref[...], lax.axis_index("beam") * local, local)
    small[1].wait()
    small[2].wait()
    hidden = last_ref[...].astype(jnp.float32)
    square = jnp.mean(hidden * hidden, axis=-1, keepdims=True)
    normed = hidden * lax.rsqrt(square + 1e-05)
    reward = jax.nn.sigmoid(jnp.sum(normed * value_ref[...], axis=-1, keepdims=True))
    row = lax.broadcasted_iota(jnp.int32, reward.shape, 0)
    marks = [jnp.sum(jnp.where(row == k, reward, 0.0), axis=0, keepdims=True) for k in kept]
    tile = lax.broadcasted_iota(jnp.int32, (MARK, HEAD), 0)
    tile = jnp.where(tile < MARK // 2, marks[0], marks[1]).astype(jnp.bfloat16)
    for copy in copies:
        copy.wait()
    sends = []
    for f in range(heads):
        for r, k in enumerate(kept):
            for s in range(2):
                start = (r * 2 + s) * step
                piece_ref[f, start : start + step, :] = held_ref[k, s, :, f * HEAD : (f + 1) * HEAD]
        piece_ref[f, KEEP * 2 * step :, :] = tile
        for d in range(f, out_ref.shape[0], heads):
            sends.append(pltpu.make_async_copy(piece_ref.at[f], out_ref.at[d], out_sems.at[d]))
            sends[-1].start()
    for send in sends:
        send.wait()


def pick(chips, ms, item_ref, table_ref, _, *out_refs):
    rows = (table_ref.shape[1] - MARK) // KEEP
    local = out_refs[0].shape[0] // (2 * rows)
    chip = lax.axis_index("beam") % (2 * chips) // 2
    core = lax.axis_index("beam") % 2
    for n, m in enumerate(ms):
        for other in range(2):
            owner = (chip ^ m) * 2 + (core ^ other)
            for i in range(local):
                item = item_ref[owner * local + i]
                start = pl.multiple_of((item % KEEP) * rows, rows)
                to = (other * local + i) * rows
                out_refs[n][to : to + rows, :] = table_ref[item // KEEP, pl.ds(start, rows), :]


def share_rewards(item_ref, table_ref, out_ref):
    children, local = item_ref.shape[0], out_ref.shape[1]
    rows = table_ref.shape[1] - MARK
    mine = lax.axis_index("beam") * local
    upper = lax.broadcasted_iota(jnp.int32, (MARK, HEAD), 0) < MARK // 2
    lane = lax.broadcasted_iota(jnp.int32, (1, HEAD), 1)

    def reward(child):
        item = item_ref[child]
        tile = table_ref[item // KEEP, rows:, :].astype(jnp.float32)
        tile = jnp.where(upper == (item % KEEP == 0), tile, 0.0)
        return tile[:1, :] + tile[MARK // 2 : MARK // 2 + 1, :]

    total = jnp.zeros((1, HEAD), jnp.float32)
    for child in range(children):
        total = total + reward(child)
    picked = jnp.zeros((1, HEAD), jnp.float32)
    for i in range(local):
        picked = jnp.where(lane == i, reward(mine + i), picked)
    out_ref[...] = (children * picked / total)[:, :local]


def attend_new(q_ref, k_ref, v_ref, out_ref, stat_ref, sums_ref, tops_ref):
    new = q_ref.shape[1]
    half = new // 2
    heads = k_ref.shape[2] // HEAD
    group = q_ref.shape[2] // k_ref.shape[2]
    count = heads * group
    scale = HEAD**-0.5 * LOG2E
    ones = jnp.ones((new, HEAD), jnp.bfloat16)
    lane = lax.broadcasted_iota(jnp.int32, (half, HEAD), 1)
    row = lax.broadcasted_iota(jnp.int32, (half, half), 0)
    column = lax.broadcasted_iota(jnp.int32, (half, half), 1)
    hidden = jnp.concatenate([jnp.where(column <= row, 0.0, -jnp.inf)] * group, axis=0)
    sums_ref[...] = jnp.ones_like(sums_ref)
    tops_ref[...] = jnp.zeros_like(tops_ref)

    def block(f, shifted):
        lanes = lambda n: pl.ds(pl.multiple_of(n * HEAD, HEAD), HEAD)
        keys = k_ref[0, :, lanes(f)]
        values = jnp.concatenate([v_ref[0, :, lanes(f)], ones], axis=1)
        columns = [lanes(f * group + h) for h in range(group)]
        most = None
        for r in range(2):
            seen = (r + 1) * half
            rows = slice(r * half, (r + 1) * half)
            query = jnp.concatenate([q_ref[0, rows, c] for c in columns], axis=0)
            logits = mm(query, keys[:seen], NT) * scale
            blocks = [logits[:, n * half : (n + 1) * half] for n in range(r + 1)]
            if not shifted:
                for a in blocks:
                    size = jnp.max(jnp.abs(a).reshape(-1, 8, half), axis=0)
                    most = size if most is None else jnp.maximum(most, size)
            blocks[r] = blocks[r] + hidden
            if shifted:
                top = functools.reduce(jnp.maximum, [jnp.max(a, axis=1, keepdims=True) for a in blocks])
                top = top.astype(jnp.bfloat16).astype(jnp.float32)
                blocks = [a - top for a in blocks]
            weights = jnp.concatenate([jnp.exp2(a).astype(jnp.bfloat16) for a in blocks], axis=1)
            both = mm(weights, values[:seen])
            for h in range(group):
                s = slice(h * half, (h + 1) * half)
                out_ref[0, rows, columns[h]] = both[s, :HEAD].astype(jnp.bfloat16)
                here = lane == f * group + h
                sums_ref[rows, :] = jnp.where(here, both[s, HEAD:], sums_ref[rows, :])
                if shifted:
                    tops_ref[rows, :] = jnp.where(here, top[s], tops_ref[rows, :])
        return most

    most = functools.reduce(jnp.maximum, [block(f, False) for f in range(heads)])

    @pl.when(jnp.max(most) > LIMIT)
    def _():
        lax.fori_loop(0, heads, lambda f, c: (block(f, True), c)[1], 0)

    sums = sums_ref[...]
    high = sums.astype(jnp.bfloat16).astype(jnp.float32)
    rest = pltpu.roll(sums - high, count, 1)
    tops = pltpu.roll(tops_ref[...], 2 * count, 1)
    lane = lax.broadcasted_iota(jnp.int32, (new, HEAD), 1)
    stat = jnp.where(lane < count, high, jnp.where(lane < 2 * count, rest, jnp.where(lane < 3 * count, tops, 0.0)))
    stat_ref[0] = stat.astype(jnp.bfloat16)


def block_pair(a):
    zero = jnp.zeros_like(a)
    return jnp.concatenate([jnp.concatenate([a, zero], axis=1), jnp.concatenate([zero, a], axis=1)], axis=0)


def forward(*refs):
    *sent_refs, _, out_ref = refs
    rows = out_ref.shape[0] // len(sent_refs)
    for n, sent_ref in enumerate(sent_refs):
        out_ref[n * rows : (n + 1) * rows, :] = sent_ref[rows:, :]


class Block:
    def __init__(self, q_ref, part_ref, stat_ref, own_ref, other_ref, out_ref, count, place, i, f):
        new, width = q_ref.shape[1:]
        rows = other_ref.shape[0] // q_ref.shape[0]
        self.step = rows // 2
        pairs = width // (2 * HEAD)
        core = lax.axis_index("beam") % 2
        here = pl.ds(pl.multiple_of(i * rows, rows), rows)
        self.piece = jnp.where(f == core, own_ref[here, :], other_ref[here, :])
        group = [f * (pairs // 2) + p for p in range(pairs // 2)]
        self.columns = [pl.ds(pl.multiple_of(p * 2 * HEAD, 2 * HEAD), 2 * HEAD) for p in group]
        self.heads = [(place * pairs + p) * 2 for p in group]
        self.q_ref, self.part_ref, self.stat_ref, self.out_ref = q_ref, part_ref, stat_ref, out_ref
        self.i, self.count, self.new = i, count, new

    def logits(self):
        keys = block_pair(self.piece[: self.step])
        queries = jnp.concatenate([self.q_ref[self.i, :, c] for c in self.columns], axis=0)
        return mm(queries, keys, NT) * (HEAD**-0.5 * LOG2E)

    def tail(self):
        lane = lax.broadcasted_iota(jnp.int32, (self.new, HEAD), 1)
        pair_of_lane = jnp.where(lane < 2 * self.count, lane % self.count // 2 * 2, -1)
        stat = self.stat_ref[self.i]
        sums = jnp.concatenate([jnp.where(pair_of_lane == h, stat, jnp.zeros_like(stat)) for h in self.heads], axis=0)
        part = jnp.concatenate([self.part_ref[self.i, :, c] for c in self.columns], axis=0).astype(jnp.float32)
        values = block_pair(self.piece[self.step :])
        ones = block_pair(jnp.ones((self.step, HEAD), jnp.bfloat16))
        odd = lax.broadcasted_iota(jnp.int32, (HEAD, 2 * HEAD), 0) % 2
        spread = (odd == lax.broadcasted_iota(jnp.int32, (HEAD, 2 * HEAD), 1) // HEAD).astype(jnp.bfloat16)
        return values, ones, spread, sums, part

    def store(self, added, total):
        result = (added * pltpu.reciprocal(total, approx=True)).astype(jnp.bfloat16)
        for n, c in enumerate(self.columns):
            self.out_ref[self.i, :, c] = result[n * self.new : (n + 1) * self.new]

    def weigh(self):
        logits = self.logits()
        return jnp.exp2(logits).astype(jnp.bfloat16), jnp.max(logits.reshape(-1, 8, HEAD), axis=0)

    def finish(self, weights):
        part = jnp.concatenate([self.part_ref[self.i, :, c] for c in self.columns], axis=0).astype(jnp.float32)
        added = mm(weights, block_pair(self.piece[self.step :]))
        lane = lax.broadcasted_iota(jnp.int32, (self.new, HEAD), 1)
        low = lax.broadcasted_iota(jnp.int32, weights.shape, 1) < self.step
        stat = self.stat_ref[self.i].astype(jnp.float32)
        here = jnp.where(lane < 2 * self.count, lane % self.count, -1)
        wide = weights.astype(jnp.float32)
        totals = []
        for n, k in enumerate((low, ~low)):
            sums = jnp.concatenate([jnp.where(here == h + n, stat, 0.0) for h in self.heads], axis=0)
            total = jnp.sum(jnp.where(k, wide, 0.0) + sums, axis=1, keepdims=True)
            totals.append(jnp.broadcast_to(pltpu.reciprocal(total, approx=True), low.shape))
        result = ((part + added) * jnp.concatenate(totals, axis=1)).astype(jnp.bfloat16)
        for n, c in enumerate(self.columns):
            self.out_ref[self.i, :, c] = result[n * self.new : (n + 1) * self.new]

    def shifted(self):
        logits = self.logits()
        low = lax.broadcasted_iota(jnp.int32, logits.shape, 1) < self.step
        lane = lax.broadcasted_iota(jnp.int32, (self.new, HEAD), 1) - 2 * self.count
        stat = self.stat_ref[self.i].astype(jnp.float32)
        shift = lambda h: jnp.sum(jnp.where(lane == h, stat, 0.0), axis=1, keepdims=True)
        shifts = [jnp.concatenate([shift(h + n) for h in self.heads], axis=0) for n in range(2)]
        logits = logits - jnp.where(low, shifts[0], shifts[1])
        tops = [jnp.maximum(jnp.max(jnp.where(k, logits, 0.0), axis=1, keepdims=True), 0.0) for k in (low, ~low)]
        weights = jnp.exp2(logits - jnp.where(low, tops[0], tops[1])).astype(jnp.bfloat16)
        rest = jnp.concatenate([jnp.broadcast_to(jnp.exp2(-t), low.shape) for t in tops], axis=1)
        values, ones, spread, sums, part = self.tail()
        self.store(part * rest + mm(weights, values), mm(weights, ones) + mm(sums, spread) * rest)


def run_blocks(block, order, most, ready=None, after=None):
    held = None
    for t in range(len(order) + 1):
        last, held = held, None
        if t < len(order):
            if ready is not None:
                ready(*order[t])
            held, top = block(*order[t]).weigh()
            most = jnp.maximum(most, top)
        if t > 0:
            block(*order[t - 1]).finish(last)
            if after is not None:
                after(*order[t - 1])
    return most


def shifted_rows(stat_ref, count):
    lane = lax.broadcasted_iota(jnp.int32, stat_ref.shape[1:], 1)

    def moved(i, most):
        tops = jnp.where(lane >= 2 * count, stat_ref[i].astype(jnp.float32), 0.0)
        tops = jnp.where(tops == 0.0, -jnp.inf, jnp.inf)
        return jnp.maximum(most, jnp.max(tops.reshape(-1, 8, HEAD), axis=0))

    return lax.fori_loop(0, stat_ref.shape[0], moved, jnp.full((8, HEAD), -jnp.inf, jnp.float32))


def attend_blocks(work, stat_ref, held_ref, out_ref, sems, ready=None, rolled=False):
    q_ref, part_ref, own_ref, other_ref, place = work
    local, _, width = q_ref.shape
    count = out_ref.shape[2] // HEAD

    def block(i, f):
        return Block(q_ref, part_ref, stat_ref, own_ref, other_ref, held_ref, count, place, i, f)

    def send(i):
        lanes = pl.ds(pl.multiple_of(place * width, width), width)
        return pltpu.make_async_copy(held_ref.at[i], out_ref.at[i, :, lanes], sems.at[i])

    def after(i, f):
        if f == 1:
            send(i).start()

    most = shifted_rows(stat_ref, count)
    if rolled:
        run = lambda i, most: run_blocks(block, [(i, 0), (i, 1)], most, after=after)
        most = lax.fori_loop(0, local, run, most)
    else:
        most = run_blocks(block, [(i, f) for i in range(local) for f in range(2)], most, ready, after)
    largest = jnp.max(most)
    for i in range(local):
        send(i).wait()

    @pl.when(largest > LIMIT)
    def _():
        lax.fori_loop(0, 2 * local, lambda t, c: (block(t // 2, t % 2).shifted(), c)[1], 0)
        for i in range(local):
            send(i).start()
        for i in range(local):
            send(i).wait()


def stage(q_ref, part_ref, m, i, to_q, to_part, sems, chips):
    width = to_q.shape[2]
    place = lax.axis_index("beam") % (2 * chips) // 2 ^ m
    lanes = pl.ds(pl.multiple_of(place * width, width), width)
    pairs = ((q_ref, to_q), (part_ref, to_part))
    return [pltpu.make_async_copy(a.at[i, :, lanes], to.at[i], sems.at[k, i]) for k, (a, to) in enumerate(pairs)]


def attend_first(chips, item_ref, table_ref, q_ref, part_ref, stat_ref, own_ref, other_ref, *refs):
    out_ref, share_ref, next_q, next_part, stat_out, token_ref = refs[:6]
    items, held_q, held_part, held, sems, next_sems, stat_sem, item_sem, out_sems = refs[6:]
    local = held_q.shape[0]
    chip = lax.axis_index("beam") % (2 * chips) // 2
    mine = lambda i: stage(q_ref, part_ref, 0, i, held_q, held_part, sems, chips)
    following = lambda i: stage(q_ref, part_ref, SECOND, i, next_q, next_part, next_sems, chips)
    stat_copy = pltpu.make_async_copy(stat_ref, stat_out, stat_sem)
    stat_copy.start()
    item_copy = pltpu.make_async_copy(item_ref, items, item_sem)
    item_copy.start()
    for i in range(local):
        for copy in mine(i):
            copy.start()
    token_ref[...] = jnp.zeros_like(token_ref)
    item_copy.wait()
    share_rewards(items, table_ref, share_ref)

    def ready(i, f):
        if f == 0:
            for copy in mine(i):
                copy.wait()
            for copy in following(i):
                copy.start()

    stat_copy.wait()
    attend_blocks((held_q, held_part, own_ref, other_ref, chip), stat_out, held, out_ref, out_sems, ready)
    for i in range(local):
        for copy in following(i):
            copy.wait()


def attend_second(chips, q_ref, part_ref, next_q, next_part, stat_ref, own_ref, other_ref, _, *refs):
    out_ref, token_ref, *later = refs[: 2 + 2 * len(LAST)]
    held, sems, next_sems = refs[2 + 2 * len(LAST) :]
    local = held.shape[0]
    chip = lax.axis_index("beam") % (2 * chips) // 2

    def staged():
        for n, m in enumerate(LAST):
            for i in range(local):
                yield from stage(q_ref, part_ref, m, i, later[2 * n], later[2 * n + 1], next_sems.at[n], chips)

    for copy in staged():
        copy.start()
    token_ref[...] = jnp.zeros_like(token_ref)
    work = (next_q, next_part, own_ref, other_ref, chip ^ SECOND)
    attend_blocks(work, stat_ref, held, out_ref, sems, rolled=True)
    for copy in staged():
        copy.wait()


def attend_half(chips, same, stat_ref, operands, held_ref, count, after=None):
    chip = lax.axis_index("beam") % (2 * chips) // 2
    f = lax.axis_index("beam") % 2 if same else 1 - lax.axis_index("beam") % 2
    local = stat_ref.shape[0]

    def block(n, i):
        q_ref, part_ref, piece_ref = operands[n]
        return Block(q_ref, part_ref, stat_ref, piece_ref, piece_ref, held_ref.at[n], count, chip ^ LAST[n], i, f)

    order = [(n, i) for n in range(len(LAST)) for i in range(local)]
    most = jnp.max(run_blocks(block, order, shifted_rows(stat_ref, count), after=after))

    def redo():
        for n in range(len(LAST)):
            lax.fori_loop(0, local, lambda i, c: (block(n, i).shifted(), c)[1], 0)

    return most > LIMIT, redo


def attend_own(chips, count, stat_ref, *refs):
    *operands, held_ref = refs
    rows = operands[2].shape[0] // 2
    works = [(*operands[3 * n : 3 * n + 2], operands[3 * n + 2].at[pl.ds(0, rows), :]) for n in range(len(LAST))]
    large, redo = attend_half(chips, True, stat_ref, works, held_ref, count)

    @pl.when(large)
    def _():
        redo()


def attend_last(chips, stat_ref, *refs):
    *operands, other_ref, made_ref, _, out_ref, held_ref, sems = refs
    local, _, width = operands[0].shape
    half = width // 2
    rows = other_ref.shape[0] // len(LAST)
    works = [(*operands[2 * n : 2 * n + 2], other_ref.at[pl.ds(n * rows, rows), :]) for n in range(len(LAST))]
    chip = lax.axis_index("beam") % (2 * chips) // 2
    core = lax.axis_index("beam") % 2

    def send(k, n, i):
        f = core if k == 0 else 1 - core
        there = pl.ds(pl.multiple_of((chip ^ LAST[n]) * width + f * half, half), half)
        here = pl.ds(pl.multiple_of(f * half, half), half)
        source = (made_ref, held_ref)[k].at[n, i, :, here]
        return pltpu.make_async_copy(source, out_ref.at[i, :, there], sems.at[k, n, i])

    every = [(n, i) for n in range(len(LAST)) for i in range(local)]
    for n, i in every:
        send(0, n, i).start()
    after = lambda n, i: send(1, n, i).start()
    large, redo = attend_half(chips, False, stat_ref, works, held_ref, out_ref.shape[2] // HEAD, after)
    for k in range(2):
        for n, i in every:
            send(k, n, i).wait()

    @pl.when(large)
    def _():
        redo()
        for n, i in every:
            send(1, n, i).start()
        for n, i in every:
            send(1, n, i).wait()


def params(mib):
    return pltpu.CompilerParams(vmem_limit_bytes=mib * MIB)


def swap(a, distance):
    count = lax.axis_size("beam")
    return lax.ppermute(a, "beam", [(i, i ^ distance) for i in range(count)])


def body(queries, new_keys, new_values, step_kv, prm_last, value_head, parents):
    beam_count = lax.axis_size("beam")
    group_index = lax.axis_index("beam")
    local, new, width = queries.shape
    children = parents.shape[0]
    step = step_kv.shape[2]
    kv_width = step_kv.shape[3]
    heads = kv_width // HEAD
    chips = heads // 2
    vmem = pl.BlockSpec(memory_space=pltpu.VMEM)
    smem = pl.BlockSpec(memory_space=pltpu.SMEM)
    hbm = pl.BlockSpec(memory_space=pltpu.HBM)
    bf16 = jnp.bfloat16

    rows = 2 * step
    in_hbm = lambda a: pltpu.with_memory_space_constraint(a, pltpu.HBM)
    in_vmem = lambda a: pltpu.with_memory_space_constraint(a, pltpu.VMEM)
    message = KEEP * rows + MARK
    packed = pl.pallas_call(
        pack,
        out_shape=jax.ShapeDtypeStruct((beam_count, message, HEAD), bf16),
        in_specs=[hbm] * 4,
        out_specs=hbm,
        scratch_shapes=[
            pltpu.VMEM((1, children), jnp.int32),
            pltpu.VMEM((local, 2, step, kv_width), bf16),
            pltpu.VMEM(prm_last.shape, bf16),
            pltpu.VMEM((1, value_head.shape[0]), jnp.float32),
            pltpu.VMEM((heads, message, HEAD), bf16),
            pltpu.SemaphoreType.DMA((local,)),
            pltpu.SemaphoreType.DMA((3,)),
            pltpu.SemaphoreType.DMA((beam_count,)),
        ],
        name="pack",
    )(in_hbm(parents.reshape(1, children)), in_hbm(step_kv), in_hbm(prm_last), in_hbm(value_head.reshape(1, -1)))
    table = lax.all_to_all(packed, "beam", 0, 0)

    cost = lambda f, t, b: pl.CostEstimate(flops=f, transcendentals=t, bytes_accessed=b)
    small = cost(1024, 0, 1024)
    whole = lambda w: pl.BlockSpec((1, new, w), lambda i: (i, 0, 0))
    part, stat = pl.pallas_call(
        attend_new,
        grid=(local,),
        out_shape=[
            jax.ShapeDtypeStruct((local, new, width), bf16),
            jax.ShapeDtypeStruct((local, new, HEAD), bf16),
        ],
        in_specs=[whole(width), whole(kv_width), whole(kv_width)],
        out_specs=[whole(width), whole(HEAD)],
        scratch_shapes=[pltpu.VMEM((new, HEAD), jnp.float32)] * 2,
        compiler_params=params(56),
        cost_estimate=cost(4 * local * new * new * width, local * new * new * width // HEAD, 6 * local * new * width),
        name="attend_new",
    )(queries, new_keys, new_values)

    owner = parents // local
    earlier = (owner[:, None] == owner[None, :]) & (parents[None, :] < parents[:, None])
    item = owner * KEEP + jnp.any(earlier, axis=1).astype(jnp.int32)
    near = lax.dynamic_slice_in_dim(item, group_index // heads * (heads * local), heads * local)
    anywhere = pl.BlockSpec(memory_space=pl.ANY)

    def picked(ms, after):
        return pl.pallas_call(
            functools.partial(pick, chips, ms),
            out_shape=[jax.ShapeDtypeStruct((2 * local * rows, HEAD), bf16)] * len(ms),
            in_specs=[smem, vmem, anywhere],
            out_specs=[vmem] * len(ms),
            compiler_params=params(4),
            cost_estimate=small,
            name="pick",
        )(near, table, after)

    def pass_on(sent, after):
        passed = pl.pallas_call(
            forward,
            out_shape=jax.ShapeDtypeStruct((len(sent) * local * rows, HEAD), bf16),
            in_specs=[vmem] * len(sent) + [anywhere],
            out_specs=vmem,
            compiler_params=params(2),
            cost_estimate=small,
            name="forward",
        )(*sent, after)
        return swap(passed, 1)

    pieces = picked(range(chips), in_hbm(stat))
    own = [pieces[0]] + [swap(pieces[m], 2 * m) for m in range(1, chips)]
    wide = width // chips
    result = jax.ShapeDtypeStruct((local, new, width), bf16)
    token = jax.ShapeDtypeStruct((8, HEAD), jnp.float32)
    later = pltpu.VMEM((local, new, wide), bf16)
    halves = pltpu.VMEM((len(LAST), local, new, wide), bf16)
    many = pltpu.SemaphoreType.DMA
    attended, child_share, next_q, next_part, stat_held, done = pl.pallas_call(
        functools.partial(attend_first, chips),
        out_shape=[
            result,
            jax.ShapeDtypeStruct((1, local), jnp.float32),
            later,
            later,
            pltpu.VMEM(stat.shape, bf16),
            token,
        ],
        in_specs=[hbm, vmem, hbm, hbm, hbm, vmem, vmem],
        out_specs=[hbm] + [vmem] * 5,
        scratch_shapes=[pltpu.SMEM((children,), jnp.int32)]
        + [later] * 2
        + [later, many((2, local)), many((2, local)), many, many, many((local,))],
        compiler_params=params(16),
        cost_estimate=small,
        name="attend_first",
    )(in_hbm(item), table, in_hbm(queries), in_hbm(part), in_hbm(stat), own[0], pass_on(own[:1], near))
    attended, done, *staged = pl.pallas_call(
        functools.partial(attend_second, chips),
        out_shape=[result, token] + [later] * (2 * len(LAST)),
        in_specs=[hbm, hbm] + [vmem] * 5 + [hbm],
        out_specs=[hbm, vmem] + [vmem] * (2 * len(LAST)),
        scratch_shapes=[later, many((local,)), many((len(LAST), 2, local))],
        input_output_aliases={7: 0},
        compiler_params=params(12),
        cost_estimate=small,
        name="attend_second",
    )(
        in_hbm(queries),
        in_hbm(part),
        in_vmem(next_q),
        in_vmem(next_part),
        in_vmem(stat_held),
        own[SECOND],
        pass_on([own[SECOND]], done),
        attended,
    )
    others = pass_on([own[m] for m in LAST], done)
    staged = [in_vmem(a) for a in staged]
    operands = []
    for n, m in enumerate(LAST):
        operands += [staged[2 * n], staged[2 * n + 1], own[m]]
    made = pl.pallas_call(
        functools.partial(attend_own, chips, width // HEAD),
        out_shape=halves,
        in_specs=[vmem] * (1 + len(operands)),
        out_specs=vmem,
        compiler_params=params(8),
        cost_estimate=small,
        name="attend_own",
    )(in_vmem(stat_held), *operands)
    attended = pl.pallas_call(
        functools.partial(attend_last, chips),
        out_shape=result,
        in_specs=[vmem] * (3 + len(staged)) + [hbm],
        out_specs=hbm,
        scratch_shapes=[halves, many((2, len(LAST), local))],
        input_output_aliases={3 + len(staged): 0},
        compiler_params=params(12),
        cost_estimate=small,
        name="attend_last",
    )(in_vmem(stat_held), *staged, others, in_vmem(made), attended)
    child_share = child_share.reshape(local)
    return (attended, child_share)


def solution(mesh):
    in_specs = (
        P(("prompts", "beam"), None, None),
        P(("prompts", "beam"), None, None),
        P(("prompts", "beam"), None, None),
        P(("prompts", "beam"), None, None, None),
        P(("prompts", "beam"), None),
        P(),
        P("prompts"),
    )
    out_specs = (P(("prompts", "beam"), None, None), P(("prompts", "beam")))
    return jax.shard_map(body, mesh=mesh, in_specs=in_specs, out_specs=out_specs, check_vma=False)
```

```python
import functools
import math

import jax
import jax.numpy as jnp
from jax import lax
from jax.experimental import pallas as pl
from jax.experimental.pallas import tpu as pltpu
from jax.sharding import PartitionSpec as P

HEAD = 128
KEEP = 2
MARK = 16
LIMIT = 100.0
SECOND = 1
LAST = (2, 3)
LOG2E = math.log2(math.e)
MIB = 1 << 20
NT = (((1,), (1,)), ((), ()))
NN = (((1,), (0,)), ((), ()))


def mm(a, b, dims=NN):
    return lax.dot_general(a, b, dims, preferred_element_type=jnp.float32)


def kept_pair(parents, base, local):
    own = (parents >= base) & (parents < base + local)
    first = jnp.min(jnp.where(own, parents - base, local))
    last = jnp.max(jnp.where(own, parents - base, -1))
    return first, last


def pack(parents_hbm, kv_hbm, last_hbm, value_hbm, out_ref, parents_ref, held_ref, last_ref, value_ref, piece_ref, *sems):
    local, _, step, width = kv_hbm.shape
    heads = width // HEAD
    kv_sems, sems, out_sems = sems
    small = [(parents_hbm, parents_ref), (last_hbm, last_ref), (value_hbm, value_ref)]
    small = [pltpu.make_async_copy(a, to, sems.at[n]) for n, (a, to) in enumerate(small)]
    copies = [pltpu.make_async_copy(kv_hbm.at[i], held_ref.at[i], kv_sems.at[i]) for i in range(local)]
    for copy in small + copies:
        copy.start()
    small[0].wait()
    kept = kept_pair(parents_ref[...], lax.axis_index("beam") * local, local)
    small[1].wait()
    small[2].wait()
    hidden = last_ref[...].astype(jnp.float32)
    square = jnp.mean(hidden * hidden, axis=-1, keepdims=True)
    normed = hidden * lax.rsqrt(square + 1e-05)
    reward = jax.nn.sigmoid(jnp.sum(normed * value_ref[...], axis=-1, keepdims=True))
    row = lax.broadcasted_iota(jnp.int32, reward.shape, 0)
    marks = [jnp.sum(jnp.where(row == k, reward, 0.0), axis=0, keepdims=True) for k in kept]
    tile = lax.broadcasted_iota(jnp.int32, (MARK, HEAD), 0)
    tile = jnp.where(tile < MARK // 2, marks[0], marks[1]).astype(jnp.bfloat16)
    for copy in copies:
        copy.wait()
    sends = []
    for f in range(heads):
        for r, k in enumerate(kept):
            for s in range(2):
                start = (r * 2 + s) * step
                piece_ref[f, start : start + step, :] = held_ref[k, s, :, f * HEAD : (f + 1) * HEAD]
        piece_ref[f, KEEP * 2 * step :, :] = tile
        for d in range(f, out_ref.shape[0], heads):
            sends.append(pltpu.make_async_copy(piece_ref.at[f], out_ref.at[d], out_sems.at[d]))
            sends[-1].start()
    for send in sends:
        send.wait()


def pick(chips, ms, item_ref, table_ref, _, *out_refs):
    rows = (table_ref.shape[1] - MARK) // KEEP
    local = out_refs[0].shape[0] // (2 * rows)
    chip = lax.axis_index("beam") % (2 * chips) // 2
    core = lax.axis_index("beam") % 2
    for n, m in enumerate(ms):
        for other in range(2):
            owner = (chip ^ m) * 2 + (core ^ other)
            for i in range(local):
                item = item_ref[owner * local + i]
                start = pl.multiple_of((item % KEEP) * rows, rows)
                to = (other * local + i) * rows
                out_refs[n][to : to + rows, :] = table_ref[item // KEEP, pl.ds(start, rows), :]


def share_rewards(item_ref, table_ref, out_ref):
    children, local = item_ref.shape[0], out_ref.shape[1]
    rows = table_ref.shape[1] - MARK
    mine = lax.axis_index("beam") * local
    upper = lax.broadcasted_iota(jnp.int32, (MARK, HEAD), 0) < MARK // 2
    lane = lax.broadcasted_iota(jnp.int32, (1, HEAD), 1)

    def reward(child):
        item = item_ref[child]
        tile = table_ref[item // KEEP, rows:, :].astype(jnp.float32)
        tile = jnp.where(upper == (item % KEEP == 0), tile, 0.0)
        return tile[:1, :] + tile[MARK // 2 : MARK // 2 + 1, :]

    total = jnp.zeros((1, HEAD), jnp.float32)
    for child in range(children):
        total = total + reward(child)
    picked = jnp.zeros((1, HEAD), jnp.float32)
    for i in range(local):
        picked = jnp.where(lane == i, reward(mine + i), picked)
    out_ref[...] = (children * picked / total)[:, :local]


def attend_new(q_ref, k_ref, v_ref, out_ref, stat_ref, sums_ref, tops_ref):
    new = q_ref.shape[1]
    half = new // 2
    heads = k_ref.shape[2] // HEAD
    group = q_ref.shape[2] // k_ref.shape[2]
    count = heads * group
    scale = HEAD**-0.5 * LOG2E
    ones = jnp.ones((new, HEAD), jnp.bfloat16)
    lane = lax.broadcasted_iota(jnp.int32, (half, HEAD), 1)
    row = lax.broadcasted_iota(jnp.int32, (half, half), 0)
    column = lax.broadcasted_iota(jnp.int32, (half, half), 1)
    hidden = jnp.concatenate([jnp.where(column <= row, 0.0, -jnp.inf)] * group, axis=0)
    sums_ref[...] = jnp.ones_like(sums_ref)
    tops_ref[...] = jnp.zeros_like(tops_ref)

    def block(f, shifted):
        lanes = lambda n: pl.ds(pl.multiple_of(n * HEAD, HEAD), HEAD)
        keys = k_ref[0, :, lanes(f)]
        values = jnp.concatenate([v_ref[0, :, lanes(f)], ones], axis=1)
        columns = [lanes(f * group + h) for h in range(group)]
        most = None
        for r in range(2):
            seen = (r + 1) * half
            rows = slice(r * half, (r + 1) * half)
            query = jnp.concatenate([q_ref[0, rows, c] for c in columns], axis=0)
            logits = mm(query, keys[:seen], NT) * scale
            blocks = [logits[:, n * half : (n + 1) * half] for n in range(r + 1)]
            if not shifted:
                for a in blocks:
                    size = jnp.max(jnp.abs(a).reshape(-1, 8, half), axis=0)
                    most = size if most is None else jnp.maximum(most, size)
            blocks[r] = blocks[r] + hidden
            if shifted:
                top = functools.reduce(jnp.maximum, [jnp.max(a, axis=1, keepdims=True) for a in blocks])
                top = top.astype(jnp.bfloat16).astype(jnp.float32)
                blocks = [a - top for a in blocks]
            weights = jnp.concatenate([jnp.exp2(a).astype(jnp.bfloat16) for a in blocks], axis=1)
            both = mm(weights, values[:seen])
            for h in range(group):
                s = slice(h * half, (h + 1) * half)
                out_ref[0, rows, columns[h]] = both[s, :HEAD].astype(jnp.bfloat16)
                here = lane == f * group + h
                sums_ref[rows, :] = jnp.where(here, both[s, HEAD:], sums_ref[rows, :])
                if shifted:
                    tops_ref[rows, :] = jnp.where(here, top[s], tops_ref[rows, :])
        return most

    most = functools.reduce(jnp.maximum, [block(f, False) for f in range(heads)])

    @pl.when(jnp.max(most) > LIMIT)
    def _():
        lax.fori_loop(0, heads, lambda f, c: (block(f, True), c)[1], 0)

    sums = sums_ref[...]
    high = sums.astype(jnp.bfloat16).astype(jnp.float32)
    rest = pltpu.roll(sums - high, count, 1)
    tops = pltpu.roll(tops_ref[...], 2 * count, 1)
    lane = lax.broadcasted_iota(jnp.int32, (new, HEAD), 1)
    stat = jnp.where(lane < count, high, jnp.where(lane < 2 * count, rest, jnp.where(lane < 3 * count, tops, 0.0)))
    stat_ref[0] = stat.astype(jnp.bfloat16)


def block_pair(a):
    zero = jnp.zeros_like(a)
    return jnp.concatenate([jnp.concatenate([a, zero], axis=1), jnp.concatenate([zero, a], axis=1)], axis=0)


def forward(*refs):
    *sent_refs, _, out_ref = refs
    rows = out_ref.shape[0] // len(sent_refs)
    for n, sent_ref in enumerate(sent_refs):
        out_ref[n * rows : (n + 1) * rows, :] = sent_ref[rows:, :]


class Block:
    def __init__(self, q_ref, part_ref, stat_ref, own_ref, other_ref, out_ref, count, place, i, f):
        new, width = q_ref.shape[1:]
        rows = other_ref.shape[0] // q_ref.shape[0]
        self.step = rows // 2
        pairs = width // (2 * HEAD)
        core = lax.axis_index("beam") % 2
        here = pl.ds(pl.multiple_of(i * rows, rows), rows)
        self.piece = jnp.where(f == core, own_ref[here, :], other_ref[here, :])
        group = [f * (pairs // 2) + p for p in range(pairs // 2)]
        self.columns = [pl.ds(pl.multiple_of(p * 2 * HEAD, 2 * HEAD), 2 * HEAD) for p in group]
        self.heads = [(place * pairs + p) * 2 for p in group]
        self.q_ref, self.part_ref, self.stat_ref, self.out_ref = q_ref, part_ref, stat_ref, out_ref
        self.i, self.count, self.new = i, count, new

    def logits(self):
        keys = block_pair(self.piece[: self.step])
        queries = jnp.concatenate([self.q_ref[self.i, :, c] for c in self.columns], axis=0)
        return mm(queries, keys, NT) * (HEAD**-0.5 * LOG2E)

    def tail(self):
        lane = lax.broadcasted_iota(jnp.int32, (self.new, HEAD), 1)
        pair_of_lane = jnp.where(lane < 2 * self.count, lane % self.count // 2 * 2, -1)
        stat = self.stat_ref[self.i]
        sums = jnp.concatenate([jnp.where(pair_of_lane == h, stat, jnp.zeros_like(stat)) for h in self.heads], axis=0)
        part = jnp.concatenate([self.part_ref[self.i, :, c] for c in self.columns], axis=0).astype(jnp.float32)
        values = block_pair(self.piece[self.step :])
        ones = block_pair(jnp.ones((self.step, HEAD), jnp.bfloat16))
        odd = lax.broadcasted_iota(jnp.int32, (HEAD, 2 * HEAD), 0) % 2
        spread = (odd == lax.broadcasted_iota(jnp.int32, (HEAD, 2 * HEAD), 1) // HEAD).astype(jnp.bfloat16)
        return values, ones, spread, sums, part

    def store(self, added, total):
        result = (added * pltpu.reciprocal(total, approx=True)).astype(jnp.bfloat16)
        for n, c in enumerate(self.columns):
            self.out_ref[self.i, :, c] = result[n * self.new : (n + 1) * self.new]

    def weigh(self):
        logits = self.logits()
        return jnp.exp2(logits).astype(jnp.bfloat16), jnp.max(logits.reshape(-1, 8, HEAD), axis=0)

    def finish(self, weights):
        part = jnp.concatenate([self.part_ref[self.i, :, c] for c in self.columns], axis=0).astype(jnp.float32)
        added = mm(weights, block_pair(self.piece[self.step :]))
        lane = lax.broadcasted_iota(jnp.int32, (self.new, HEAD), 1)
        low = lax.broadcasted_iota(jnp.int32, weights.shape, 1) < self.step
        stat = self.stat_ref[self.i].astype(jnp.float32)
        here = jnp.where(lane < 2 * self.count, lane % self.count, -1)
        wide = weights.astype(jnp.float32)
        totals = []
        for n, k in enumerate((low, ~low)):
            sums = jnp.concatenate([jnp.where(here == h + n, stat, 0.0) for h in self.heads], axis=0)
            total = jnp.sum(jnp.where(k, wide, 0.0) + sums, axis=1, keepdims=True)
            totals.append(jnp.broadcast_to(pltpu.reciprocal(total, approx=True), low.shape))
        result = ((part + added) * jnp.concatenate(totals, axis=1)).astype(jnp.bfloat16)
        for n, c in enumerate(self.columns):
            self.out_ref[self.i, :, c] = result[n * self.new : (n + 1) * self.new]

    def shifted(self):
        logits = self.logits()
        low = lax.broadcasted_iota(jnp.int32, logits.shape, 1) < self.step
        lane = lax.broadcasted_iota(jnp.int32, (self.new, HEAD), 1) - 2 * self.count
        stat = self.stat_ref[self.i].astype(jnp.float32)
        shift = lambda h: jnp.sum(jnp.where(lane == h, stat, 0.0), axis=1, keepdims=True)
        shifts = [jnp.concatenate([shift(h + n) for h in self.heads], axis=0) for n in range(2)]
        logits = logits - jnp.where(low, shifts[0], shifts[1])
        tops = [jnp.maximum(jnp.max(jnp.where(k, logits, 0.0), axis=1, keepdims=True), 0.0) for k in (low, ~low)]
        weights = jnp.exp2(logits - jnp.where(low, tops[0], tops[1])).astype(jnp.bfloat16)
        rest = jnp.concatenate([jnp.broadcast_to(jnp.exp2(-t), low.shape) for t in tops], axis=1)
        values, ones, spread, sums, part = self.tail()
        self.store(part * rest + mm(weights, values), mm(weights, ones) + mm(sums, spread) * rest)


def run_blocks(block, order, most, ready=None, after=None):
    held = None
    for t in range(len(order) + 1):
        last, held = held, None
        if t < len(order):
            if ready is not None:
                ready(*order[t])
            held, top = block(*order[t]).weigh()
            most = jnp.maximum(most, top)
        if t > 0:
            block(*order[t - 1]).finish(last)
            if after is not None:
                after(*order[t - 1])
    return most


def shifted_rows(stat_ref, count):
    lane = lax.broadcasted_iota(jnp.int32, stat_ref.shape[1:], 1)

    def moved(i, most):
        tops = jnp.where(lane >= 2 * count, stat_ref[i].astype(jnp.float32), 0.0)
        tops = jnp.where(tops == 0.0, -jnp.inf, jnp.inf)
        return jnp.maximum(most, jnp.max(tops.reshape(-1, 8, HEAD), axis=0))

    return lax.fori_loop(0, stat_ref.shape[0], moved, jnp.full((8, HEAD), -jnp.inf, jnp.float32))


def attend_blocks(work, stat_ref, most, held_ref, out_ref, sems, ready=None, rolled=False):
    q_ref, part_ref, own_ref, other_ref, place = work
    local, _, width = q_ref.shape
    count = out_ref.shape[2] // HEAD

    def block(i, f):
        return Block(q_ref, part_ref, stat_ref, own_ref, other_ref, held_ref, count, place, i, f)

    def send(i):
        lanes = pl.ds(pl.multiple_of(place * width, width), width)
        return pltpu.make_async_copy(held_ref.at[i], out_ref.at[i, :, lanes], sems.at[i])

    def after(i, f):
        if f == 1:
            send(i).start()

    if rolled:
        run = lambda i, most: run_blocks(block, [(i, 0), (i, 1)], most, after=after)
        most = lax.fori_loop(0, local, run, most)
    else:
        most = run_blocks(block, [(i, f) for i in range(local) for f in range(2)], most, ready, after)
    largest = jnp.max(most)
    for i in range(local):
        send(i).wait()

    @pl.when(largest > LIMIT)
    def _():
        lax.fori_loop(0, 2 * local, lambda t, c: (block(t // 2, t % 2).shifted(), c)[1], 0)
        for i in range(local):
            send(i).start()
        for i in range(local):
            send(i).wait()


def stage(q_ref, part_ref, m, i, to_q, to_part, sems, chips):
    width = to_q.shape[2]
    place = lax.axis_index("beam") % (2 * chips) // 2 ^ m
    lanes = pl.ds(pl.multiple_of(place * width, width), width)
    pairs = ((q_ref, to_q), (part_ref, to_part))
    return [pltpu.make_async_copy(a.at[i, :, lanes], to.at[i], sems.at[k, i]) for k, (a, to) in enumerate(pairs)]


def attend_first(chips, item_ref, table_ref, q_ref, part_ref, stat_ref, own_ref, other_ref, *refs):
    out_ref, share_ref, next_q, next_part, stat_out, token_ref = refs[:6]
    items, held_q, held_part, held, sems, next_sems, stat_sem, item_sem, out_sems = refs[6:]
    local = held_q.shape[0]
    chip = lax.axis_index("beam") % (2 * chips) // 2
    mine = lambda i: stage(q_ref, part_ref, 0, i, held_q, held_part, sems, chips)
    following = lambda i: stage(q_ref, part_ref, SECOND, i, next_q, next_part, next_sems, chips)
    stat_copy = pltpu.make_async_copy(stat_ref, stat_out, stat_sem)
    stat_copy.start()
    item_copy = pltpu.make_async_copy(item_ref, items, item_sem)
    item_copy.start()
    for i in range(local):
        for copy in mine(i):
            copy.start()
    item_copy.wait()
    share_rewards(items, table_ref, share_ref)

    def ready(i, f):
        if f == 0:
            for copy in mine(i):
                copy.wait()
            for copy in following(i):
                copy.start()

    stat_copy.wait()
    most = shifted_rows(stat_out, out_ref.shape[2] // HEAD)
    token_ref[...] = most
    attend_blocks((held_q, held_part, own_ref, other_ref, chip), stat_out, most, held, out_ref, out_sems, ready)
    for i in range(local):
        for copy in following(i):
            copy.wait()


def attend_second(chips, q_ref, part_ref, next_q, next_part, stat_ref, own_ref, other_ref, moved_ref, _, *refs):
    out_ref, token_ref, *later = refs[: 2 + 2 * len(LAST)]
    held, sems, next_sems = refs[2 + 2 * len(LAST) :]
    local = held.shape[0]
    chip = lax.axis_index("beam") % (2 * chips) // 2

    def staged():
        for n, m in enumerate(LAST):
            for i in range(local):
                yield from stage(q_ref, part_ref, m, i, later[2 * n], later[2 * n + 1], next_sems.at[n], chips)

    for copy in staged():
        copy.start()
    token_ref[...] = jnp.zeros_like(token_ref)
    work = (next_q, next_part, own_ref, other_ref, chip ^ SECOND)
    attend_blocks(work, stat_ref, moved_ref[...], held, out_ref, sems, rolled=True)
    for copy in staged():
        copy.wait()


def attend_half(chips, same, stat_ref, moved_ref, operands, held_ref, count, after=None):
    chip = lax.axis_index("beam") % (2 * chips) // 2
    f = lax.axis_index("beam") % 2 if same else 1 - lax.axis_index("beam") % 2
    local = stat_ref.shape[0]

    def block(n, i):
        q_ref, part_ref, piece_ref = operands[n]
        return Block(q_ref, part_ref, stat_ref, piece_ref, piece_ref, held_ref.at[n], count, chip ^ LAST[n], i, f)

    order = [(n, i) for n in range(len(LAST)) for i in range(local)]
    most = jnp.max(run_blocks(block, order, moved_ref[...], after=after))

    def redo():
        for n in range(len(LAST)):
            lax.fori_loop(0, local, lambda i, c: (block(n, i).shifted(), c)[1], 0)

    return most > LIMIT, redo


def attend_own(chips, count, stat_ref, moved_ref, *refs):
    *operands, held_ref = refs
    rows = operands[2].shape[0] // 2
    works = [(*operands[3 * n : 3 * n + 2], operands[3 * n + 2].at[pl.ds(0, rows), :]) for n in range(len(LAST))]
    large, redo = attend_half(chips, True, stat_ref, moved_ref, works, held_ref, count)

    @pl.when(large)
    def _():
        redo()


def attend_last(chips, stat_ref, moved_ref, *refs):
    *operands, other_ref, made_ref, _, out_ref, held_ref, sems = refs
    local, _, width = operands[0].shape
    half = width // 2
    rows = other_ref.shape[0] // len(LAST)
    works = [(*operands[2 * n : 2 * n + 2], other_ref.at[pl.ds(n * rows, rows), :]) for n in range(len(LAST))]
    chip = lax.axis_index("beam") % (2 * chips) // 2
    core = lax.axis_index("beam") % 2

    def send(k, n, i):
        f = core if k == 0 else 1 - core
        there = pl.ds(pl.multiple_of((chip ^ LAST[n]) * width + f * half, half), half)
        here = pl.ds(pl.multiple_of(f * half, half), half)
        source = (made_ref, held_ref)[k].at[n, i, :, here]
        return pltpu.make_async_copy(source, out_ref.at[i, :, there], sems.at[k, n, i])

    every = [(n, i) for n in range(len(LAST)) for i in range(local)]
    for n, i in every:
        send(0, n, i).start()
    after = lambda n, i: send(1, n, i).start()
    large, redo = attend_half(chips, False, stat_ref, moved_ref, works, held_ref, out_ref.shape[2] // HEAD, after)
    for k in range(2):
        for n, i in every:
            send(k, n, i).wait()

    @pl.when(large)
    def _():
        redo()
        for n, i in every:
            send(1, n, i).start()
        for n, i in every:
            send(1, n, i).wait()


def params(mib):
    return pltpu.CompilerParams(vmem_limit_bytes=mib * MIB)


def swap(a, distance):
    count = lax.axis_size("beam")
    return lax.ppermute(a, "beam", [(i, i ^ distance) for i in range(count)])


def body(queries, new_keys, new_values, step_kv, prm_last, value_head, parents):
    beam_count = lax.axis_size("beam")
    group_index = lax.axis_index("beam")
    local, new, width = queries.shape
    children = parents.shape[0]
    step = step_kv.shape[2]
    kv_width = step_kv.shape[3]
    heads = kv_width // HEAD
    chips = heads // 2
    vmem = pl.BlockSpec(memory_space=pltpu.VMEM)
    smem = pl.BlockSpec(memory_space=pltpu.SMEM)
    hbm = pl.BlockSpec(memory_space=pltpu.HBM)
    bf16 = jnp.bfloat16

    rows = 2 * step
    in_hbm = lambda a: pltpu.with_memory_space_constraint(a, pltpu.HBM)
    in_vmem = lambda a: pltpu.with_memory_space_constraint(a, pltpu.VMEM)
    message = KEEP * rows + MARK
    packed = pl.pallas_call(
        pack,
        out_shape=jax.ShapeDtypeStruct((beam_count, message, HEAD), bf16),
        in_specs=[hbm] * 4,
        out_specs=hbm,
        scratch_shapes=[
            pltpu.VMEM((1, children), jnp.int32),
            pltpu.VMEM((local, 2, step, kv_width), bf16),
            pltpu.VMEM(prm_last.shape, bf16),
            pltpu.VMEM((1, value_head.shape[0]), jnp.float32),
            pltpu.VMEM((heads, message, HEAD), bf16),
            pltpu.SemaphoreType.DMA((local,)),
            pltpu.SemaphoreType.DMA((3,)),
            pltpu.SemaphoreType.DMA((beam_count,)),
        ],
        name="pack",
    )(in_hbm(parents.reshape(1, children)), in_hbm(step_kv), in_hbm(prm_last), in_hbm(value_head.reshape(1, -1)))
    table = lax.all_to_all(packed, "beam", 0, 0)

    cost = lambda f, t, b: pl.CostEstimate(flops=f, transcendentals=t, bytes_accessed=b)
    small = cost(1024, 0, 1024)
    whole = lambda w: pl.BlockSpec((1, new, w), lambda i: (i, 0, 0))
    part, stat = pl.pallas_call(
        attend_new,
        grid=(local,),
        out_shape=[
            jax.ShapeDtypeStruct((local, new, width), bf16),
            jax.ShapeDtypeStruct((local, new, HEAD), bf16),
        ],
        in_specs=[whole(width), whole(kv_width), whole(kv_width)],
        out_specs=[whole(width), whole(HEAD)],
        scratch_shapes=[pltpu.VMEM((new, HEAD), jnp.float32)] * 2,
        compiler_params=params(56),
        cost_estimate=cost(4 * local * new * new * width, local * new * new * width // HEAD, 6 * local * new * width),
        name="attend_new",
    )(queries, new_keys, new_values)

    owner = parents // local
    earlier = (owner[:, None] == owner[None, :]) & (parents[None, :] < parents[:, None])
    item = owner * KEEP + jnp.any(earlier, axis=1).astype(jnp.int32)
    near = lax.dynamic_slice_in_dim(item, group_index // heads * (heads * local), heads * local)
    anywhere = pl.BlockSpec(memory_space=pl.ANY)

    def picked(ms, after):
        return pl.pallas_call(
            functools.partial(pick, chips, ms),
            out_shape=[jax.ShapeDtypeStruct((2 * local * rows, HEAD), bf16)] * len(ms),
            in_specs=[smem, vmem, anywhere],
            out_specs=[vmem] * len(ms),
            compiler_params=params(4),
            cost_estimate=small,
            name="pick",
        )(near, table, after)

    def pass_on(sent, after):
        passed = pl.pallas_call(
            forward,
            out_shape=jax.ShapeDtypeStruct((len(sent) * local * rows, HEAD), bf16),
            in_specs=[vmem] * len(sent) + [anywhere],
            out_specs=vmem,
            compiler_params=params(2),
            cost_estimate=small,
            name="forward",
        )(*sent, after)
        return swap(passed, 1)

    pieces = picked(range(chips), in_hbm(stat))
    own = [pieces[0]] + [swap(pieces[m], 2 * m) for m in range(1, chips)]
    wide = width // chips
    result = jax.ShapeDtypeStruct((local, new, width), bf16)
    token = jax.ShapeDtypeStruct((8, HEAD), jnp.float32)
    later = pltpu.VMEM((local, new, wide), bf16)
    halves = pltpu.VMEM((len(LAST), local, new, wide), bf16)
    many = pltpu.SemaphoreType.DMA
    attended, child_share, next_q, next_part, stat_held, done = pl.pallas_call(
        functools.partial(attend_first, chips),
        out_shape=[
            result,
            jax.ShapeDtypeStruct((1, local), jnp.float32),
            later,
            later,
            pltpu.VMEM(stat.shape, bf16),
            token,
        ],
        in_specs=[hbm, vmem, hbm, hbm, hbm, vmem, vmem],
        out_specs=[hbm] + [vmem] * 5,
        scratch_shapes=[pltpu.SMEM((children,), jnp.int32)]
        + [later] * 2
        + [later, many((2, local)), many((2, local)), many, many, many((local,))],
        compiler_params=params(16),
        cost_estimate=small,
        name="attend_first",
    )(in_hbm(item), table, in_hbm(queries), in_hbm(part), in_hbm(stat), own[0], pass_on(own[:1], near))
    moved = done
    attended, done, *staged = pl.pallas_call(
        functools.partial(attend_second, chips),
        out_shape=[result, token] + [later] * (2 * len(LAST)),
        in_specs=[hbm, hbm] + [vmem] * 6 + [hbm],
        out_specs=[hbm, vmem] + [vmem] * (2 * len(LAST)),
        scratch_shapes=[later, many((local,)), many((len(LAST), 2, local))],
        input_output_aliases={8: 0},
        compiler_params=params(12),
        cost_estimate=small,
        name="attend_second",
    )(
        in_hbm(queries),
        in_hbm(part),
        in_vmem(next_q),
        in_vmem(next_part),
        in_vmem(stat_held),
        own[SECOND],
        pass_on([own[SECOND]], done),
        moved,
        attended,
    )
    others = pass_on([own[m] for m in LAST], done)
    staged = [in_vmem(a) for a in staged]
    operands = []
    for n, m in enumerate(LAST):
        operands += [staged[2 * n], staged[2 * n + 1], own[m]]
    made = pl.pallas_call(
        functools.partial(attend_own, chips, width // HEAD),
        out_shape=halves,
        in_specs=[vmem] * (2 + len(operands)),
        out_specs=vmem,
        compiler_params=params(8),
        cost_estimate=small,
        name="attend_own",
    )(in_vmem(stat_held), moved, *operands)
    attended = pl.pallas_call(
        functools.partial(attend_last, chips),
        out_shape=result,
        in_specs=[vmem] * (4 + len(staged)) + [hbm],
        out_specs=hbm,
        scratch_shapes=[halves, many((2, len(LAST), local))],
        input_output_aliases={4 + len(staged): 0},
        compiler_params=params(12),
        cost_estimate=small,
        name="attend_last",
    )(in_vmem(stat_held), moved, *staged, others, in_vmem(made), attended)
    child_share = child_share.reshape(local)
    return (attended, child_share)


def solution(mesh):
    in_specs = (
        P(("prompts", "beam"), None, None),
        P(("prompts", "beam"), None, None),
        P(("prompts", "beam"), None, None),
        P(("prompts", "beam"), None, None, None),
        P(("prompts", "beam"), None),
        P(),
        P("prompts"),
    )
    out_specs = (P(("prompts", "beam"), None, None), P(("prompts", "beam")))
    return jax.shard_map(body, mesh=mesh, in_specs=in_specs, out_specs=out_specs, check_vma=False)
```

```python
import functools
import math

import jax
import jax.numpy as jnp
from jax import lax
from jax.experimental import pallas as pl
from jax.experimental.pallas import tpu as pltpu
from jax.sharding import PartitionSpec as P

HEAD = 128
KEEP = 2
MARK = 16
LIMIT = 100.0
SECOND = 1
LAST = (2, 3)
LOG2E = math.log2(math.e)
MIB = 1 << 20
NT = (((1,), (1,)), ((), ()))
NN = (((1,), (0,)), ((), ()))


def mm(a, b, dims=NN):
    return lax.dot_general(a, b, dims, preferred_element_type=jnp.float32)


def kept_pair(parents, base, local):
    own = (parents >= base) & (parents < base + local)
    first = jnp.min(jnp.where(own, parents - base, local))
    last = jnp.max(jnp.where(own, parents - base, -1))
    return first, last


def pack(parents_hbm, kv_hbm, last_hbm, value_hbm, out_ref, parents_ref, held_ref, last_ref, value_ref, piece_ref, *sems):
    local, _, step, width = kv_hbm.shape
    heads = width // HEAD
    kv_sems, sems, out_sems = sems
    small = [(parents_hbm, parents_ref), (last_hbm, last_ref), (value_hbm, value_ref)]
    small = [pltpu.make_async_copy(a, to, sems.at[n]) for n, (a, to) in enumerate(small)]
    copies = [pltpu.make_async_copy(kv_hbm.at[i], held_ref.at[i], kv_sems.at[i]) for i in range(local)]
    for copy in small + copies:
        copy.start()
    small[0].wait()
    kept = kept_pair(parents_ref[...], lax.axis_index("beam") * local, local)
    small[1].wait()
    small[2].wait()
    hidden = last_ref[...].astype(jnp.float32)
    square = jnp.mean(hidden * hidden, axis=-1, keepdims=True)
    normed = hidden * lax.rsqrt(square + 1e-05)
    reward = jax.nn.sigmoid(jnp.sum(normed * value_ref[...], axis=-1, keepdims=True))
    row = lax.broadcasted_iota(jnp.int32, reward.shape, 0)
    marks = [jnp.sum(jnp.where(row == k, reward, 0.0), axis=0, keepdims=True) for k in kept]
    tile = lax.broadcasted_iota(jnp.int32, (MARK, HEAD), 0)
    tile = jnp.where(tile < MARK // 2, marks[0], marks[1]).astype(jnp.bfloat16)
    for copy in copies:
        copy.wait()
    sends = []
    for f in range(heads):
        for r, k in enumerate(kept):
            for s in range(2):
                start = (r * 2 + s) * step
                piece_ref[f, start : start + step, :] = held_ref[k, s, :, f * HEAD : (f + 1) * HEAD]
        piece_ref[f, KEEP * 2 * step :, :] = tile
        for d in range(f, out_ref.shape[0], heads):
            sends.append(pltpu.make_async_copy(piece_ref.at[f], out_ref.at[d], out_sems.at[d]))
            sends[-1].start()
    for send in sends:
        send.wait()


def pick(chips, ms, item_ref, table_ref, _, *out_refs):
    rows = (table_ref.shape[1] - MARK) // KEEP
    local = out_refs[0].shape[0] // (2 * rows)
    chip = lax.axis_index("beam") % (2 * chips) // 2
    core = lax.axis_index("beam") % 2
    for n, m in enumerate(ms):
        for other in range(2):
            owner = (chip ^ m) * 2 + (core ^ other)
            for i in range(local):
                item = item_ref[owner * local + i]
                start = pl.multiple_of((item % KEEP) * rows, rows)
                to = (other * local + i) * rows
                out_refs[n][to : to + rows, :] = table_ref[item // KEEP, pl.ds(start, rows), :]


def share_rewards(item_ref, table_ref, out_ref):
    children, local = item_ref.shape[0], out_ref.shape[1]
    rows = table_ref.shape[1] - MARK
    mine = lax.axis_index("beam") * local
    upper = lax.broadcasted_iota(jnp.int32, (MARK, HEAD), 0) < MARK // 2
    lane = lax.broadcasted_iota(jnp.int32, (1, HEAD), 1)

    def reward(child):
        item = item_ref[child]
        tile = table_ref[item // KEEP, rows:, :].astype(jnp.float32)
        tile = jnp.where(upper == (item % KEEP == 0), tile, 0.0)
        return tile[:1, :] + tile[MARK // 2 : MARK // 2 + 1, :]

    total = jnp.zeros((1, HEAD), jnp.float32)
    for child in range(children):
        total = total + reward(child)
    picked = jnp.zeros((1, HEAD), jnp.float32)
    for i in range(local):
        picked = jnp.where(lane == i, reward(mine + i), picked)
    out_ref[...] = (children * picked / total)[:, :local]


def attend_new(q_ref, k_ref, v_ref, out_ref, stat_ref, sums_ref, tops_ref):
    new = q_ref.shape[1]
    half = new // 2
    heads = k_ref.shape[2] // HEAD
    group = q_ref.shape[2] // k_ref.shape[2]
    count = heads * group
    scale = HEAD**-0.5 * LOG2E
    ones = jnp.ones((new, HEAD), jnp.bfloat16)
    lane = lax.broadcasted_iota(jnp.int32, (half, HEAD), 1)
    row = lax.broadcasted_iota(jnp.int32, (half, half), 0)
    column = lax.broadcasted_iota(jnp.int32, (half, half), 1)
    hidden = jnp.concatenate([jnp.where(column <= row, 0.0, -jnp.inf)] * group, axis=0)
    sums_ref[...] = jnp.ones_like(sums_ref)
    tops_ref[...] = jnp.zeros_like(tops_ref)

    def block(f, shifted):
        lanes = lambda n: pl.ds(pl.multiple_of(n * HEAD, HEAD), HEAD)
        keys = k_ref[0, :, lanes(f)]
        values = jnp.concatenate([v_ref[0, :, lanes(f)], ones], axis=1)
        columns = [lanes(f * group + h) for h in range(group)]
        most = None
        for r in range(2):
            seen = (r + 1) * half
            rows = slice(r * half, (r + 1) * half)
            query = jnp.concatenate([q_ref[0, rows, c] for c in columns], axis=0)
            logits = mm(query, keys[:seen], NT) * scale
            blocks = [logits[:, n * half : (n + 1) * half] for n in range(r + 1)]
            if not shifted:
                for a in blocks:
                    size = jnp.max(jnp.abs(a).reshape(-1, 8, half), axis=0)
                    most = size if most is None else jnp.maximum(most, size)
            blocks[r] = blocks[r] + hidden
            if shifted:
                top = functools.reduce(jnp.maximum, [jnp.max(a, axis=1, keepdims=True) for a in blocks])
                top = top.astype(jnp.bfloat16).astype(jnp.float32)
                blocks = [a - top for a in blocks]
            weights = jnp.concatenate([jnp.exp2(a).astype(jnp.bfloat16) for a in blocks], axis=1)
            both = mm(weights, values[:seen])
            for h in range(group):
                s = slice(h * half, (h + 1) * half)
                out_ref[0, rows, columns[h]] = both[s, :HEAD].astype(jnp.bfloat16)
                here = lane == f * group + h
                sums_ref[rows, :] = jnp.where(here, both[s, HEAD:], sums_ref[rows, :])
                if shifted:
                    tops_ref[rows, :] = jnp.where(here, top[s], tops_ref[rows, :])
        return most

    most = functools.reduce(jnp.maximum, [block(f, False) for f in range(heads)])

    @pl.when(jnp.max(most) > LIMIT)
    def _():
        lax.fori_loop(0, heads, lambda f, c: (block(f, True), c)[1], 0)

    sums = sums_ref[...]
    high = sums.astype(jnp.bfloat16).astype(jnp.float32)
    rest = pltpu.roll(sums - high, count, 1)
    tops = pltpu.roll(tops_ref[...], 2 * count, 1)
    lane = lax.broadcasted_iota(jnp.int32, (new, HEAD), 1)
    stat = jnp.where(lane < count, high, jnp.where(lane < 2 * count, rest, jnp.where(lane < 3 * count, tops, 0.0)))
    stat_ref[0] = stat.astype(jnp.bfloat16)


def block_pair(a):
    zero = jnp.zeros_like(a)
    return jnp.concatenate([jnp.concatenate([a, zero], axis=1), jnp.concatenate([zero, a], axis=1)], axis=0)


def forward(*refs):
    *sent_refs, _, out_ref = refs
    rows = out_ref.shape[0] // len(sent_refs)
    for n, sent_ref in enumerate(sent_refs):
        out_ref[n * rows : (n + 1) * rows, :] = sent_ref[rows:, :]


class Block:
    def __init__(self, q_ref, part_ref, stat_ref, own_ref, other_ref, out_ref, count, place, i, f):
        new, width = q_ref.shape[1:]
        rows = other_ref.shape[0] // q_ref.shape[0]
        self.step = rows // 2
        pairs = width // (2 * HEAD)
        core = lax.axis_index("beam") % 2
        here = pl.ds(pl.multiple_of(i * rows, rows), rows)
        self.piece = jnp.where(f == core, own_ref[here, :], other_ref[here, :])
        group = [f * (pairs // 2) + p for p in range(pairs // 2)]
        self.columns = [pl.ds(pl.multiple_of(p * 2 * HEAD, 2 * HEAD), 2 * HEAD) for p in group]
        self.heads = [(place * pairs + p) * 2 for p in group]
        self.q_ref, self.part_ref, self.stat_ref, self.out_ref = q_ref, part_ref, stat_ref, out_ref
        self.i, self.count, self.new = i, count, new

    def logits(self):
        keys = block_pair(self.piece[: self.step])
        queries = jnp.concatenate([self.q_ref[self.i, :, c] for c in self.columns], axis=0)
        return mm(queries, keys, NT) * (HEAD**-0.5 * LOG2E)

    def tail(self):
        lane = lax.broadcasted_iota(jnp.int32, (self.new, HEAD), 1)
        pair_of_lane = jnp.where(lane < 2 * self.count, lane % self.count // 2 * 2, -1)
        stat = self.stat_ref[self.i]
        sums = jnp.concatenate([jnp.where(pair_of_lane == h, stat, jnp.zeros_like(stat)) for h in self.heads], axis=0)
        part = jnp.concatenate([self.part_ref[self.i, :, c] for c in self.columns], axis=0).astype(jnp.float32)
        values = block_pair(self.piece[self.step :])
        ones = block_pair(jnp.ones((self.step, HEAD), jnp.bfloat16))
        odd = lax.broadcasted_iota(jnp.int32, (HEAD, 2 * HEAD), 0) % 2
        spread = (odd == lax.broadcasted_iota(jnp.int32, (HEAD, 2 * HEAD), 1) // HEAD).astype(jnp.bfloat16)
        return values, ones, spread, sums, part

    def store(self, added, total):
        result = (added * pltpu.reciprocal(total, approx=True)).astype(jnp.bfloat16)
        for n, c in enumerate(self.columns):
            self.out_ref[self.i, :, c] = result[n * self.new : (n + 1) * self.new]

    def weigh(self):
        logits = self.logits()
        return jnp.exp2(logits).astype(jnp.bfloat16), jnp.max(logits.reshape(-1, 8, HEAD), axis=0)

    def finish(self, weights):
        part = jnp.concatenate([self.part_ref[self.i, :, c] for c in self.columns], axis=0).astype(jnp.float32)
        added = mm(weights, block_pair(self.piece[self.step :]))
        lane = lax.broadcasted_iota(jnp.int32, (self.new, HEAD), 1)
        low = lax.broadcasted_iota(jnp.int32, weights.shape, 1) < self.step
        stat = self.stat_ref[self.i].astype(jnp.float32)
        here = jnp.where(lane < 2 * self.count, lane % self.count, -1)
        wide = weights.astype(jnp.float32)
        totals = []
        for n, k in enumerate((low, ~low)):
            sums = jnp.concatenate([jnp.where(here == h + n, stat, 0.0) for h in self.heads], axis=0)
            total = jnp.sum(jnp.where(k, wide, 0.0) + sums, axis=1, keepdims=True)
            totals.append(jnp.broadcast_to(pltpu.reciprocal(total, approx=True), low.shape))
        result = ((part + added) * jnp.concatenate(totals, axis=1)).astype(jnp.bfloat16)
        for n, c in enumerate(self.columns):
            self.out_ref[self.i, :, c] = result[n * self.new : (n + 1) * self.new]

    def shifted(self):
        logits = self.logits()
        low = lax.broadcasted_iota(jnp.int32, logits.shape, 1) < self.step
        lane = lax.broadcasted_iota(jnp.int32, (self.new, HEAD), 1) - 2 * self.count
        stat = self.stat_ref[self.i].astype(jnp.float32)
        shift = lambda h: jnp.sum(jnp.where(lane == h, stat, 0.0), axis=1, keepdims=True)
        shifts = [jnp.concatenate([shift(h + n) for h in self.heads], axis=0) for n in range(2)]
        logits = logits - jnp.where(low, shifts[0], shifts[1])
        tops = [jnp.maximum(jnp.max(jnp.where(k, logits, 0.0), axis=1, keepdims=True), 0.0) for k in (low, ~low)]
        weights = jnp.exp2(logits - jnp.where(low, tops[0], tops[1])).astype(jnp.bfloat16)
        rest = jnp.concatenate([jnp.broadcast_to(jnp.exp2(-t), low.shape) for t in tops], axis=1)
        values, ones, spread, sums, part = self.tail()
        self.store(part * rest + mm(weights, values), mm(weights, ones) + mm(sums, spread) * rest)


def run_blocks(block, order, most, ready=None, after=None):
    held = None
    for t in range(len(order) + 1):
        last, held = held, None
        if t < len(order):
            if ready is not None:
                ready(*order[t])
            held, top = block(*order[t]).weigh()
            most = jnp.maximum(most, top)
        if t > 0:
            block(*order[t - 1]).finish(last)
            if after is not None:
                after(*order[t - 1])
    return most


def shifted_rows(stat_ref, count):
    lane = lax.broadcasted_iota(jnp.int32, stat_ref.shape[1:], 1)

    def moved(i, most):
        tops = jnp.where(lane >= 2 * count, stat_ref[i].astype(jnp.float32), 0.0)
        tops = jnp.where(tops == 0.0, -jnp.inf, jnp.inf)
        return jnp.maximum(most, jnp.max(tops.reshape(-1, 8, HEAD), axis=0))

    return lax.fori_loop(0, stat_ref.shape[0], moved, jnp.full((8, HEAD), -jnp.inf, jnp.float32))


def attend_blocks(work, stat_ref, most, held_ref, out_ref, sems, ready=None, rolled=False):
    q_ref, part_ref, own_ref, other_ref, place = work
    local, _, width = q_ref.shape
    count = out_ref.shape[2] // HEAD

    def block(i, f):
        return Block(q_ref, part_ref, stat_ref, own_ref, other_ref, held_ref, count, place, i, f)

    def send(i):
        lanes = pl.ds(pl.multiple_of(place * width, width), width)
        return pltpu.make_async_copy(held_ref.at[i], out_ref.at[i, :, lanes], sems.at[i])

    def after(i, f):
        if f == 1:
            send(i).start()

    if rolled:
        run = lambda i, most: run_blocks(block, [(i, 0), (i, 1)], most, after=after)
        most = lax.fori_loop(0, local, run, most)
    else:
        most = run_blocks(block, [(i, f) for i in range(local) for f in range(2)], most, ready, after)
    largest = jnp.max(most)
    for i in range(local):
        send(i).wait()

    @pl.when(largest > LIMIT)
    def _():
        lax.fori_loop(0, 2 * local, lambda t, c: (block(t // 2, t % 2).shifted(), c)[1], 0)
        for i in range(local):
            send(i).start()
        for i in range(local):
            send(i).wait()


def stage(q_ref, part_ref, m, i, to_q, to_part, sems, chips):
    width = to_q.shape[2]
    place = lax.axis_index("beam") % (2 * chips) // 2 ^ m
    lanes = pl.ds(pl.multiple_of(place * width, width), width)
    pairs = ((q_ref, to_q), (part_ref, to_part))
    return [pltpu.make_async_copy(a.at[i, :, lanes], to.at[i], sems.at[k, i]) for k, (a, to) in enumerate(pairs)]


def attend_first(chips, item_ref, table_ref, q_ref, part_ref, stat_ref, own_ref, other_ref, *refs):
    out_ref, share_ref, next_q, next_part, stat_out, token_ref = refs[:6]
    items, held_q, held_part, held, sems, next_sems, stat_sem, item_sem, out_sems = refs[6:]
    local = held_q.shape[0]
    chip = lax.axis_index("beam") % (2 * chips) // 2
    mine = lambda i: stage(q_ref, part_ref, 0, i, held_q, held_part, sems, chips)
    following = lambda i: stage(q_ref, part_ref, SECOND, i, next_q, next_part, next_sems, chips)
    stat_copy = pltpu.make_async_copy(stat_ref, stat_out, stat_sem)
    stat_copy.start()
    item_copy = pltpu.make_async_copy(item_ref, items, item_sem)
    item_copy.start()
    for i in range(local):
        for copy in mine(i):
            copy.start()
    item_copy.wait()
    share_rewards(items, table_ref, share_ref)

    def ready(i, f):
        if f == 0:
            for copy in mine(i):
                copy.wait()
            for copy in following(i):
                copy.start()

    stat_copy.wait()
    most = shifted_rows(stat_out, out_ref.shape[2] // HEAD)
    token_ref[...] = most
    attend_blocks((held_q, held_part, own_ref, other_ref, chip), stat_out, most, held, out_ref, out_sems, ready)
    for i in range(local):
        for copy in following(i):
            copy.wait()


def attend_second(chips, q_ref, part_ref, next_q, next_part, stat_ref, own_ref, other_ref, moved_ref, _, *refs):
    out_ref, token_ref, *later = refs[: 2 + 2 * len(LAST)]
    held, sems, next_sems = refs[2 + 2 * len(LAST) :]
    local = held.shape[0]
    chip = lax.axis_index("beam") % (2 * chips) // 2

    def staged():
        for n, m in enumerate(LAST):
            for i in range(local):
                yield from stage(q_ref, part_ref, m, i, later[2 * n], later[2 * n + 1], next_sems.at[n], chips)

    for copy in staged():
        copy.start()
    token_ref[...] = jnp.zeros_like(token_ref)
    work = (next_q, next_part, own_ref, other_ref, chip ^ SECOND)
    attend_blocks(work, stat_ref, moved_ref[...], held, out_ref, sems, rolled=True)
    for copy in staged():
        copy.wait()


def attend_half(chips, same, stat_ref, moved_ref, operands, held_ref, count, after=None):
    chip = lax.axis_index("beam") % (2 * chips) // 2
    f = lax.axis_index("beam") % 2 if same else 1 - lax.axis_index("beam") % 2
    local = stat_ref.shape[0]

    def block(n, i):
        q_ref, part_ref, piece_ref = operands[n]
        return Block(q_ref, part_ref, stat_ref, piece_ref, piece_ref, held_ref.at[n], count, chip ^ LAST[n], i, f)

    order = [(n, i) for n in range(len(LAST)) for i in range(local)]
    most = jnp.max(run_blocks(block, order, moved_ref[...], after=after))

    def redo():
        for n in range(len(LAST)):
            lax.fori_loop(0, local, lambda i, c: (block(n, i).shifted(), c)[1], 0)

    return most > LIMIT, redo


def attend_own(chips, count, stat_ref, moved_ref, *refs):
    *operands, held_ref = refs
    rows = operands[2].shape[0] // 2
    works = [(*operands[3 * n : 3 * n + 2], operands[3 * n + 2].at[pl.ds(0, rows), :]) for n in range(len(LAST))]
    large, redo = attend_half(chips, True, stat_ref, moved_ref, works, held_ref, count)

    @pl.when(large)
    def _():
        redo()


def attend_last(chips, stat_ref, moved_ref, *refs):
    *operands, other_ref, made_ref, _, out_ref, held_ref, sems = refs
    local, _, width = operands[0].shape
    half = width // 2
    rows = other_ref.shape[0] // len(LAST)
    works = [(*operands[2 * n : 2 * n + 2], other_ref.at[pl.ds(n * rows, rows), :]) for n in range(len(LAST))]
    chip = lax.axis_index("beam") % (2 * chips) // 2
    core = lax.axis_index("beam") % 2

    def send(k, n, i):
        f = core if k == 0 else 1 - core
        there = pl.ds(pl.multiple_of((chip ^ LAST[n]) * width + f * half, half), half)
        here = pl.ds(pl.multiple_of(f * half, half), half)
        source = (made_ref, held_ref)[k].at[n, i, :, here]
        return pltpu.make_async_copy(source, out_ref.at[i, :, there], sems.at[k, n, i])

    every = [(n, i) for n in range(len(LAST)) for i in range(local)]
    def after(n, i):
        t = every.index((n, i))
        for e in every[2 * t : 2 * t + 2]:
            send(0, *e).start()
        send(1, n, i).start()

    large, redo = attend_half(chips, False, stat_ref, moved_ref, works, held_ref, out_ref.shape[2] // HEAD, after)
    for k in range(2):
        for n, i in every:
            send(k, n, i).wait()

    @pl.when(large)
    def _():
        redo()
        for n, i in every:
            send(1, n, i).start()
        for n, i in every:
            send(1, n, i).wait()


def params(mib):
    return pltpu.CompilerParams(vmem_limit_bytes=mib * MIB)


def swap(a, distance):
    count = lax.axis_size("beam")
    return lax.ppermute(a, "beam", [(i, i ^ distance) for i in range(count)])


def body(queries, new_keys, new_values, step_kv, prm_last, value_head, parents):
    beam_count = lax.axis_size("beam")
    group_index = lax.axis_index("beam")
    local, new, width = queries.shape
    children = parents.shape[0]
    step = step_kv.shape[2]
    kv_width = step_kv.shape[3]
    heads = kv_width // HEAD
    chips = heads // 2
    vmem = pl.BlockSpec(memory_space=pltpu.VMEM)
    smem = pl.BlockSpec(memory_space=pltpu.SMEM)
    hbm = pl.BlockSpec(memory_space=pltpu.HBM)
    bf16 = jnp.bfloat16

    rows = 2 * step
    in_hbm = lambda a: pltpu.with_memory_space_constraint(a, pltpu.HBM)
    in_vmem = lambda a: pltpu.with_memory_space_constraint(a, pltpu.VMEM)
    message = KEEP * rows + MARK
    packed = pl.pallas_call(
        pack,
        out_shape=jax.ShapeDtypeStruct((beam_count, message, HEAD), bf16),
        in_specs=[hbm] * 4,
        out_specs=hbm,
        scratch_shapes=[
            pltpu.VMEM((1, children), jnp.int32),
            pltpu.VMEM((local, 2, step, kv_width), bf16),
            pltpu.VMEM(prm_last.shape, bf16),
            pltpu.VMEM((1, value_head.shape[0]), jnp.float32),
            pltpu.VMEM((heads, message, HEAD), bf16),
            pltpu.SemaphoreType.DMA((local,)),
            pltpu.SemaphoreType.DMA((3,)),
            pltpu.SemaphoreType.DMA((beam_count,)),
        ],
        name="pack",
    )(in_hbm(parents.reshape(1, children)), in_hbm(step_kv), in_hbm(prm_last), in_hbm(value_head.reshape(1, -1)))
    table = lax.all_to_all(packed, "beam", 0, 0)

    cost = lambda f, t, b: pl.CostEstimate(flops=f, transcendentals=t, bytes_accessed=b)
    small = cost(1024, 0, 1024)
    whole = lambda w: pl.BlockSpec((1, new, w), lambda i: (i, 0, 0))
    part, stat = pl.pallas_call(
        attend_new,
        grid=(local,),
        out_shape=[
            jax.ShapeDtypeStruct((local, new, width), bf16),
            jax.ShapeDtypeStruct((local, new, HEAD), bf16),
        ],
        in_specs=[whole(width), whole(kv_width), whole(kv_width)],
        out_specs=[whole(width), whole(HEAD)],
        scratch_shapes=[pltpu.VMEM((new, HEAD), jnp.float32)] * 2,
        compiler_params=params(56),
        cost_estimate=cost(4 * local * new * new * width, local * new * new * width // HEAD, 6 * local * new * width),
        name="attend_new",
    )(queries, new_keys, new_values)

    owner = parents // local
    earlier = (owner[:, None] == owner[None, :]) & (parents[None, :] < parents[:, None])
    item = owner * KEEP + jnp.any(earlier, axis=1).astype(jnp.int32)
    near = lax.dynamic_slice_in_dim(item, group_index // heads * (heads * local), heads * local)
    anywhere = pl.BlockSpec(memory_space=pl.ANY)

    def picked(ms, after):
        return pl.pallas_call(
            functools.partial(pick, chips, ms),
            out_shape=[jax.ShapeDtypeStruct((2 * local * rows, HEAD), bf16)] * len(ms),
            in_specs=[smem, vmem, anywhere],
            out_specs=[vmem] * len(ms),
            compiler_params=params(4),
            cost_estimate=small,
            name="pick",
        )(near, table, after)

    def pass_on(sent, after):
        passed = pl.pallas_call(
            forward,
            out_shape=jax.ShapeDtypeStruct((len(sent) * local * rows, HEAD), bf16),
            in_specs=[vmem] * len(sent) + [anywhere],
            out_specs=vmem,
            compiler_params=params(2),
            cost_estimate=small,
            name="forward",
        )(*sent, after)
        return swap(passed, 1)

    pieces = picked(range(chips), in_hbm(stat))
    own = [pieces[0]] + [swap(pieces[m], 2 * m) for m in range(1, chips)]
    wide = width // chips
    result = jax.ShapeDtypeStruct((local, new, width), bf16)
    token = jax.ShapeDtypeStruct((8, HEAD), jnp.float32)
    later = pltpu.VMEM((local, new, wide), bf16)
    halves = pltpu.VMEM((len(LAST), local, new, wide), bf16)
    many = pltpu.SemaphoreType.DMA
    attended, child_share, next_q, next_part, stat_held, done = pl.pallas_call(
        functools.partial(attend_first, chips),
        out_shape=[
            result,
            jax.ShapeDtypeStruct((1, local), jnp.float32),
            later,
            later,
            pltpu.VMEM(stat.shape, bf16),
            token,
        ],
        in_specs=[hbm, vmem, hbm, hbm, hbm, vmem, vmem],
        out_specs=[hbm] + [vmem] * 5,
        scratch_shapes=[pltpu.SMEM((children,), jnp.int32)]
        + [later] * 2
        + [later, many((2, local)), many((2, local)), many, many, many((local,))],
        compiler_params=params(16),
        cost_estimate=small,
        name="attend_first",
    )(in_hbm(item), table, in_hbm(queries), in_hbm(part), in_hbm(stat), own[0], pass_on(own[:1], near))
    moved = done
    attended, done, *staged = pl.pallas_call(
        functools.partial(attend_second, chips),
        out_shape=[result, token] + [later] * (2 * len(LAST)),
        in_specs=[hbm, hbm] + [vmem] * 6 + [hbm],
        out_specs=[hbm, vmem] + [vmem] * (2 * len(LAST)),
        scratch_shapes=[later, many((local,)), many((len(LAST), 2, local))],
        input_output_aliases={8: 0},
        compiler_params=params(12),
        cost_estimate=small,
        name="attend_second",
    )(
        in_hbm(queries),
        in_hbm(part),
        in_vmem(next_q),
        in_vmem(next_part),
        in_vmem(stat_held),
        own[SECOND],
        pass_on([own[SECOND]], done),
        moved,
        attended,
    )
    others = pass_on([own[m] for m in LAST], done)
    staged = [in_vmem(a) for a in staged]
    operands = []
    for n, m in enumerate(LAST):
        operands += [staged[2 * n], staged[2 * n + 1], own[m]]
    made = pl.pallas_call(
        functools.partial(attend_own, chips, width // HEAD),
        out_shape=halves,
        in_specs=[vmem] * (2 + len(operands)),
        out_specs=vmem,
        compiler_params=params(8),
        cost_estimate=small,
        name="attend_own",
    )(in_vmem(stat_held), moved, *operands)
    attended = pl.pallas_call(
        functools.partial(attend_last, chips),
        out_shape=result,
        in_specs=[vmem] * (4 + len(staged)) + [hbm],
        out_specs=hbm,
        scratch_shapes=[halves, many((2, len(LAST), local))],
        input_output_aliases={4 + len(staged): 0},
        compiler_params=params(12),
        cost_estimate=small,
        name="attend_last",
    )(in_vmem(stat_held), moved, *staged, others, in_vmem(made), attended)
    child_share = child_share.reshape(local)
    return (attended, child_share)


def solution(mesh):
    in_specs = (
        P(("prompts", "beam"), None, None),
        P(("prompts", "beam"), None, None),
        P(("prompts", "beam"), None, None),
        P(("prompts", "beam"), None, None, None),
        P(("prompts", "beam"), None),
        P(),
        P("prompts"),
    )
    out_specs = (P(("prompts", "beam"), None, None), P(("prompts", "beam")))
    return jax.shard_map(body, mesh=mesh, in_specs=in_specs, out_specs=out_specs, check_vma=False)
```
